32 devices in a mesh: ctx: 16 (over z, x, core), pipe: 2 (over y).
Axes of the slice: x: 2, y: 2, z: 4, core: 2. Of those that a mesh axis runs over, the one named last changes fastest.
Arguments:
- query_fwd: bfloat16 [2, 2048, 2048], P('pipe', 'ctx'), may hold values from -6 to 6
- key_fwd: bfloat16 [2, 2048, 512], P('pipe', 'ctx'), may hold values from -6 to 6
- value_fwd: bfloat16 [2, 2048, 512], P('pipe', 'ctx'), may hold values from -6 to 6
- gate_fwd: bfloat16 [2, 2048, 2048], P('pipe', 'ctx'), may hold values from -6 to 6
- types_fwd: int32 [2, 2048], P('pipe', 'ctx'), may hold values from 0 to 63
- query_bwd: bfloat16 [2, 2048, 2048], P('pipe', 'ctx'), may hold values from -6 to 6
- key_bwd: bfloat16 [2, 2048, 512], P('pipe', 'ctx'), may hold values from -6 to 6
- value_bwd: bfloat16 [2, 2048, 512], P('pipe', 'ctx'), may hold values from -6 to 6
- grad_out: bfloat16 [2, 2048, 2048], P('pipe', 'ctx'), may hold values from -6 to 6
- types_bwd: int32 [2, 2048], P('pipe', 'ctx'), may hold values from 0 to 63
- type_key: bfloat16 [2, 64, 512], P('pipe'), may hold values from -4.1875 to 4.1875
- norm_gain: float32 [2, 2048], P('pipe'), may hold values from 0.5 to 1.5
- stretch_order: int32 [2, 32], P('pipe'), may hold values from 0 to 31, as said below
Outputs:
- handed: bfloat16 [2, 2048, 2048], P('pipe', 'ctx')
- query_grad: bfloat16 [2, 2048, 2048], P('pipe', 'ctx')
- key_grad: bfloat16 [2, 2048, 512], P('pipe', 'ctx')
- value_grad: bfloat16 [2, 2048, 512], P('pipe', 'ctx')
The draws below stay inside these ranges and needn't reach their ends.
Inputs may be any that keep to these rules, and one draw needn't show every extreme that they name: `stretch_order`: in each section's row the stored stretch slots 2 c and 2 c + 1 (those of index c of ctx) hold two stretches whose numbers add to 31, in either order; each row names every stretch once.
All inputs are finite; a program needn't handle non-finite values.
Results may differ from the reference program's by a relative error of at most 0.02.
Values may be sent and summed in bfloat16 or wider, within the bound.
No kernel may reach another device: no remote copies, remote signals or barrier semaphores. Data moves between devices by JAX's collectives and lax.ppermute only.
A program may use at most 128 MiB of HBM per device.

```python
import math
import jax
import jax.numpy as jnp
from jax import lax

HEAD = 128
TYPES = 64
TOK_DEV = 128
STRETCHES = 32
TOKENS = 2048
SECTIONS = 2
QW = 2048
KVW = 512
N_CTX = 16


def draw_stretch_order(key, part):
    key = jax.random.fold_in(key, 11)
    section_keys = jax.random.split(key, SECTIONS)

    def one_section(section_key):
        perm_key, flip_key = jax.random.split(section_key)
        early_ids = jax.random.permutation(perm_key, STRETCHES // 2).astype(jnp.int32)
        late_ids = STRETCHES - 1 - early_ids
        flip_bits = jax.random.randint(flip_key, (STRETCHES // 2,), 0, 2, dtype=jnp.int32)
        leading = jnp.where(flip_bits == 1, late_ids, early_ids)
        trailing = jnp.where(flip_bits == 1, early_ids, late_ids)
        return jnp.stack([leading, trailing], axis=1).reshape(STRETCHES).astype(jnp.int32)
    return jax.vmap(one_section)(section_keys)


def with_ends(result, rng, smallest, largest):
    longest = result.shape.index(max(result.shape))
    spots = []
    for shift in (0, 1):
        where = [jax.random.randint(jax.random.fold_in(rng, axis), (), 0, length) for axis, length in enumerate(result.shape)]
        where[longest] = (where[longest] + shift) % result.shape[longest]
        spots.append(tuple(where))
    return result.at[spots[0]].set(smallest).at[spots[1]].set(largest)


def level_of(rng, extent, cuts, least, largest):
    gain = 1.0
    for dim, blocks in cuts:
        heights = jax.random.uniform(jax.random.fold_in(jax.random.fold_in(rng, 6), dim), (blocks,), jnp.float32, least / len(cuts), largest / len(cuts))
        gain = gain * jnp.repeat(jnp.exp(heights), extent[dim] // blocks).reshape((-1,) + (1,) * (len(extent) - 1 - dim))
    return gain


def normal_values(rng, shape, spread, most, cuts=(), kind=jnp.bfloat16):
    array = spread * jax.random.normal(rng, shape, jnp.float32)
    if cuts:
        array = array * level_of(rng, shape, cuts, -0.22, 0.18)
    return jnp.clip(array, -most, most).astype(kind)


def setup_inputs(seed: int = 0) -> dict:
    key_list = jax.random.split(jax.random.key(seed), 14)
    return {
        "query_fwd": normal_values(key_list[0], (SECTIONS, TOKENS, QW), 1.0, 6.0, ((0, 2), (1, 16))),
        "key_fwd": normal_values(key_list[1], (SECTIONS, TOKENS, KVW), 1.0, 6.0, ((0, 2), (1, 16))),
        "value_fwd": normal_values(key_list[2], (SECTIONS, TOKENS, KVW), 1.0, 6.0, ((0, 2), (1, 16))),
        "gate_fwd": normal_values(key_list[3], (SECTIONS, TOKENS, QW), 1.0, 6.0, ((0, 2), (1, 16))),
        "types_fwd": with_ends(jax.random.randint(key_list[4], (SECTIONS, TOKENS), 0, TYPES), jax.random.fold_in(key_list[4], 1), 0, TYPES - 1).astype(jnp.int32),
        "query_bwd": normal_values(key_list[5], (SECTIONS, TOKENS, QW), 1.0, 6.0, ((0, 2), (1, 16))),
        "key_bwd": normal_values(key_list[6], (SECTIONS, TOKENS, KVW), 1.0, 6.0, ((0, 2), (1, 16))),
        "value_bwd": normal_values(key_list[7], (SECTIONS, TOKENS, KVW), 1.0, 6.0, ((0, 2), (1, 16))),
        "grad_out": normal_values(key_list[8], (SECTIONS, TOKENS, QW), 1.0, 6.0, ((0, 2), (1, 16))),
        "types_bwd": with_ends(jax.random.randint(key_list[9], (SECTIONS, TOKENS), 0, TYPES), jax.random.fold_in(key_list[9], 1), 0, TYPES - 1).astype(jnp.int32),
        "type_key": normal_values(key_list[10], (SECTIONS, TYPES, KVW), 0.7, 4.1875, ((0, 2),)),
        "norm_gain": jnp.clip(1.0 + 0.1 * jax.random.normal(key_list[11], (SECTIONS, QW), jnp.float32), 0.5, 1.5),
        "stretch_order": draw_stretch_order(jax.random.fold_in(key_list[13], 71), 0),
    }


norm_eps = 1e-06

def silu_slope(scores):
    sigmoid_part = jax.nn.sigmoid(scores)
    return sigmoid_part * (1.0 + scores * (1.0 - sigmoid_part))

def typed_keys(key_rows, event_types, type_table):
    onehot = (event_types[:, None] == jnp.arange(type_table.shape[0], dtype=jnp.int32)[None, :]).astype(jnp.bfloat16)
    type_rows = jnp.dot(onehot, type_table, preferred_element_type=jnp.float32)
    return (key_rows.astype(jnp.float32) + type_rows).astype(jnp.bfloat16)

def invert(stretch_perm):
    total_stretches = stretch_perm.shape[0]
    matches = stretch_perm[None, :] == jnp.arange(total_stretches, dtype=jnp.int32)[:, None]
    return lax.optimization_barrier(jnp.sum(jnp.where(matches, jnp.arange(total_stretches, dtype=jnp.int32)[None, :], 0), axis=1)).astype(jnp.int32)

def to_sequence(stored, inverse, stretch_rows):
    return jnp.take(stored.reshape(-1, stretch_rows, stored.shape[1]), inverse, axis=0).reshape(-1, stored.shape[1])

def position(stretch_perm, slot_index, stretch_rows):
    leading = lax.dynamic_index_in_dim(stretch_perm, slot_index, keepdims=False)
    return leading * stretch_rows + jnp.arange(stretch_rows, dtype=jnp.int32)

def score_block(queries, query_pos, key_rows, value_rows, key_pos):
    row_count = queries.shape[0]
    kv_heads = key_rows.shape[1] // HEAD
    groups = queries.shape[1] // key_rows.shape[1]
    query_heads = queries.astype(jnp.float32).reshape(row_count, kv_heads, groups, HEAD)
    key_heads = key_rows.astype(jnp.float32).reshape(-1, kv_heads, HEAD)
    value_heads = value_rows.astype(jnp.float32).reshape(-1, kv_heads, HEAD)
    scores = jnp.einsum('qhgd,thd->hgqt', query_heads, key_heads) * HEAD ** (-0.5)
    visible = key_pos[None, :] <= query_pos[:, None]
    shrink = lax.rsqrt((query_pos + 1).astype(jnp.float32))[:, None]
    weights = (jnp.where(visible, jax.nn.silu(scores), 0.0) * shrink).astype(jnp.bfloat16)
    return (query_heads, key_heads, value_heads, scores, visible, shrink, weights)

def forward_block(queries, query_pos, key_rows, value_rows, key_pos):
    query_heads, key_heads, value_heads, scores, visible, shrink, weights = score_block(queries, query_pos, key_rows, value_rows, key_pos)
    return jnp.einsum('hgqt,thd->qhgd', weights.astype(jnp.float32), value_heads).reshape(queries.shape[0], -1)

def backward_block(queries, grad_rows, query_pos, key_rows, value_rows, key_pos):
    query_heads, key_heads, value_heads, scores, visible, shrink, weights = score_block(queries, query_pos, key_rows, value_rows, key_pos)
    grad_heads = grad_rows.astype(jnp.float32).reshape(query_heads.shape)
    weight_grad = jnp.einsum('qhgd,thd->hgqt', grad_heads, value_heads)
    score_grad = (jnp.where(visible, weight_grad * silu_slope(scores), 0.0) * shrink).astype(jnp.bfloat16)
    query_part = jnp.einsum('hgqt,thd->qhgd', score_grad.astype(jnp.float32), key_heads).reshape(queries.shape[0], -1)
    key_part = jnp.einsum('hgqt,qhgd->thd', score_grad.astype(jnp.float32), query_heads) * HEAD ** (-0.5)
    value_part = jnp.einsum('hgqt,qhgd->thd', weights.astype(jnp.float32), grad_heads)
    kv_width = key_rows.shape[1]
    return (query_part, jnp.concatenate([key_part.reshape(-1, kv_width), value_part.reshape(-1, kv_width)], axis=1))

def rows_forward(queries, query_pos, seq_keys, seq_values, block_rows):
    block_count = query_pos[-1] // block_rows + 1

    def advance(step_index, running):
        offset = step_index * block_rows
        key_rows = lax.dynamic_slice_in_dim(seq_keys, offset, block_rows, 0)
        value_rows = lax.dynamic_slice_in_dim(seq_values, offset, block_rows, 0)
        key_pos = offset + jnp.arange(block_rows, dtype=jnp.int32)
        return running + forward_block(queries, query_pos, key_rows, value_rows, key_pos)
    return lax.fori_loop(0, block_count, advance, jnp.zeros(queries.shape, jnp.float32))

def rows_backward(queries, grad_rows, query_pos, seq_keys, seq_values, block_rows, buffer):
    block_count = query_pos[-1] // block_rows + 1

    def advance(step_index, carried):
        running, buffer_in = carried
        offset = step_index * block_rows
        key_rows = lax.dynamic_slice_in_dim(seq_keys, offset, block_rows, 0)
        value_rows = lax.dynamic_slice_in_dim(seq_values, offset, block_rows, 0)
        key_pos = offset + jnp.arange(block_rows, dtype=jnp.int32)
        query_part, kv_part = backward_block(queries, grad_rows, query_pos, key_rows, value_rows, key_pos)
        former = lax.dynamic_slice_in_dim(buffer_in, offset, block_rows, 0)
        return (running + query_part, lax.dynamic_update_slice_in_dim(buffer_in, former + kv_part, offset, 0))
    return lax.fori_loop(0, block_count, advance, (jnp.zeros(queries.shape, jnp.float32), buffer))

def one_section(inputs):
    query_fwd, key_fwd, value_fwd, gate_fwd, types_fwd, query_bwd, key_bwd, value_bwd, grad_out, types_bwd, type_table, norm_gain, stretch_perm = inputs
    stretch_rows = TOK_DEV // 2
    block_rows = math.gcd(TOKENS, 512)
    kv_width = key_fwd.shape[1]
    inverse = invert(stretch_perm)
    keys_f = typed_keys(key_fwd, types_fwd, type_table)
    keys_b = typed_keys(key_bwd, types_bwd, type_table)
    seq_keys_f = to_sequence(keys_f, inverse, stretch_rows)
    seq_values_f = to_sequence(value_fwd, inverse, stretch_rows)
    seq_keys_b = to_sequence(keys_b, inverse, stretch_rows)
    seq_values_b = to_sequence(value_bwd, inverse, stretch_rows)

    def forward_device(device):
        outputs = []
        for stretch_slot in range(2):
            slot_index = 2 * device + stretch_slot
            queries = lax.dynamic_slice_in_dim(query_fwd, slot_index * stretch_rows, stretch_rows, 0)
            outputs.append(rows_forward(queries, position(stretch_perm, slot_index, stretch_rows), seq_keys_f, seq_values_f, block_rows))
        return jnp.concatenate(outputs, axis=0)
    attended = lax.map(forward_device, jnp.arange(N_CTX, dtype=jnp.int32)).reshape(TOKENS, -1)
    mean_square = lax.optimization_barrier(jnp.mean(attended * attended, axis=1, keepdims=True))
    gated = (attended * lax.rsqrt(mean_square + norm_eps) * norm_gain[None, :] * gate_fwd.astype(jnp.float32)).astype(jnp.bfloat16)

    def backward_device(grand_total, device):
        buffer = jnp.zeros((TOKENS, 2 * kv_width), jnp.float32)
        query_parts = []
        for stretch_slot in range(2):
            slot_index = 2 * device + stretch_slot
            queries = lax.dynamic_slice_in_dim(query_bwd, slot_index * stretch_rows, stretch_rows, 0)
            grad_rows = lax.dynamic_slice_in_dim(grad_out, slot_index * stretch_rows, stretch_rows, 0)
            query_part, buffer = rows_backward(queries, grad_rows, position(stretch_perm, slot_index, stretch_rows), seq_keys_b, seq_values_b, block_rows, buffer)
            query_parts.append(query_part)
        rounded = lax.optimization_barrier(buffer.astype(jnp.bfloat16))
        return (grand_total + rounded.astype(jnp.float32), jnp.concatenate(query_parts, axis=0))
    grand_total, query_sums = lax.scan(backward_device, jnp.zeros((TOKENS, 2 * kv_width), jnp.float32), jnp.arange(N_CTX, dtype=jnp.int32))
    query_grad = (query_sums.reshape(TOKENS, -1) * HEAD ** (-0.5)).astype(jnp.bfloat16)
    stored = jnp.take(grand_total.reshape(-1, stretch_rows, 2 * kv_width), stretch_perm, axis=0).reshape(TOKENS, 2 * kv_width)
    return (gated, query_grad, stored[:, :kv_width].astype(jnp.bfloat16), stored[:, kv_width:].astype(jnp.bfloat16))

def reference(query_fwd, key_fwd, value_fwd, gate_fwd, types_fwd, query_bwd, key_bwd, value_bwd, grad_out, types_bwd, type_key, norm_gain, stretch_order):
    gated, query_grad, key_grad, value_grad = lax.map(one_section, (query_fwd, key_fwd, value_fwd, gate_fwd, types_fwd, query_bwd, key_bwd, value_bwd, grad_out, types_bwd, type_key, norm_gain, stretch_order))
    handed = jnp.roll(gated, 1, axis=0)
    return (handed, query_grad, key_grad, value_grad)
```

```python
import functools
import math

import jax
import jax.numpy as jnp
from jax import lax
from jax.experimental import pallas as pl
from jax.experimental.pallas import tpu as pltpu
from jax.sharding import PartitionSpec as P

HEAD = 128
QUAD = 4
SCALE = HEAD ** (-0.5)
EXP2_SCALE = -SCALE / math.log(2.0)
norm_eps = 1e-06

VMEM = pl.BlockSpec(memory_space=pltpu.VMEM)
SMEM = pl.BlockSpec(memory_space=pltpu.SMEM)
PARAMS = pltpu.CompilerParams(vmem_limit_bytes=40 * 1024 * 1024)

NN = (((1,), (0,)), ((), ()))
NT = (((1,), (1,)), ((), ()))
TN = (((0,), (0,)), ((), ()))


def dot(a, b, dims):
    return lax.dot_general(a, b, dims, preferred_element_type=jnp.float32)


def bf16(*shape):
    return jax.ShapeDtypeStruct(shape, jnp.bfloat16)


def place():
    index = lax.axis_index("ctx")
    return index // QUAD, index % QUAD


def columns(index, width):
    return pl.ds(pl.multiple_of(index * width, width), width)


def pack_keys(key_ref, value_ref, types_ref, table_ref, *refs):
    pieces, typed = refs[:QUAD], refs[QUAD]
    _, member = place()
    type_count = table_ref.shape[1]
    onehot = (
        lax.broadcasted_iota(jnp.int32, (type_count, types_ref.shape[1]), 0) == types_ref[...]
    ).astype(jnp.float32).astype(jnp.bfloat16)
    type_rows = dot(onehot, table_ref[0], TN)
    typed[...] = (key_ref[0].astype(jnp.float32) + type_rows).astype(jnp.bfloat16)
    for d in range(QUAD):
        head = columns(member ^ d, HEAD)
        pieces[d][:, :HEAD] = typed[:, head]
        pieces[d][:, HEAD:] = value_ref[0, :, head]


def pack_queries(query_b_ref, grad_ref, query_f_ref, *pieces):
    _, member = place()
    width = query_b_ref.shape[2] // QUAD
    for d in range(QUAD):
        head = columns(member ^ d, width)
        pieces[d][:, :width] = query_b_ref[0, :, head]
        pieces[d][:, width : 2 * width] = grad_ref[0, :, head]
        pieces[d][:, 2 * width :] = query_f_ref[0, :, head]


def stretch_of(order_ref, quad_index, member, d, e):
    return order_ref[0, 2 * (quad_index * QUAD + (member ^ d)) + e]


def rows_at(index, count):
    return pl.ds(pl.multiple_of(index * count, count), count)


def in_sequence(order_ref, stacks, stretch_rows, keys, values):
    z, member = place()
    nz = len(stacks)
    for s, stack in enumerate(stacks):
        source = lax.rem(z - s + nz, nz)
        for d in range(QUAD):
            for e in range(2):
                rows = rows_at(stretch_of(order_ref, source, member, d, e), stretch_rows)
                lower = (2 * d + e) * stretch_rows
                keys[rows, :] = stack[lower : lower + stretch_rows, :HEAD]
                values[rows, :] = stack[lower : lower + stretch_rows, HEAD:]


def shrink_of(stretch, stretch_rows):
    pos = stretch * stretch_rows + lax.broadcasted_iota(jnp.int32, (stretch_rows, HEAD), 0)
    return lax.rsqrt((pos + 1).astype(jnp.float32))


def step_place(first, second, step, d, groups):
    blocks = first // groups + 1
    late = step >= blocks
    row = jnp.where(late, 2 * d + 1, 2 * d)
    stretch = jnp.where(late, second, first)
    block = jnp.where(late, step - blocks, step)
    return row, stretch, block


def sigmoid_of(raw, visible):
    part = pl.reciprocal(1.0 + jnp.exp2(raw * EXP2_SCALE), approx=True)
    return jnp.where(visible, part, 0.0)


def forward_kernel(nz, order_ref, *refs):
    queries, refs = refs[:QUAD], refs[QUAD:]
    stacks, refs = refs[:nz], refs[nz:]
    outs, refs = refs[:QUAD], refs[QUAD:]
    keys, values, stacked, total, gap = refs
    z, member = place()
    stretch_rows = queries[0].shape[0] // 2
    groups = queries[0].shape[1] // (3 * HEAD)
    block_rows = groups * stretch_rows
    steps = keys.shape[0] // block_rows + 1
    in_sequence(order_ref, stacks, stretch_rows, keys, values)
    offset = 2 * groups * HEAD
    for d in range(QUAD):
        for e in range(2):
            for g in range(groups):
                stacked[2 * d + e, g * stretch_rows : (g + 1) * stretch_rows, :] = queries[d][
                    e * stretch_rows : (e + 1) * stretch_rows,
                    offset + g * HEAD : offset + (g + 1) * HEAD,
                ]
    total[...] = jnp.zeros_like(total)
    gap[...] = lax.broadcasted_iota(jnp.int32, gap.shape, 1) - lax.rem(
        lax.broadcasted_iota(jnp.int32, gap.shape, 0), stretch_rows
    )

    def advance(step, _):
        for d in range(QUAD):
            row, stretch, block = step_place(
                stretch_of(order_ref, z, member, d, 0),
                stretch_of(order_ref, z, member, d, 1),
                step,
                d,
                groups,
            )
            rows = rows_at(block, block_rows)
            raw = dot(stacked[row], keys[rows, :], NT)
            visible = gap[...] <= stretch * stretch_rows - block * block_rows
            weights = (raw * SCALE * sigmoid_of(raw, visible)).astype(jnp.bfloat16)
            total[row] += dot(weights, values[rows, :], NN)
        return 0

    lax.fori_loop(0, steps, advance, 0)
    for d in range(QUAD):
        for e in range(2):
            shrink = shrink_of(stretch_of(order_ref, z, member, d, e), stretch_rows)
            for g in range(groups):
                outs[d][e * stretch_rows : (e + 1) * stretch_rows, g * HEAD : (g + 1) * HEAD] = (
                    total[2 * d + e, g * stretch_rows : (g + 1) * stretch_rows, :] * shrink
                ).astype(jnp.bfloat16)


def backward_kernel(nz, order_ref, *refs):
    queries, refs = refs[:QUAD], refs[QUAD:]
    stacks, refs = refs[:nz], refs[nz:]
    query_outs, refs = refs[:QUAD], refs[QUAD:]
    key_outs, refs = refs[:nz], refs[nz:]
    keys, values, keys_t, stacked, grads, total_t, key_total, value_total, gap = refs
    z, member = place()
    stretch_rows = queries[0].shape[0] // 2
    groups = queries[0].shape[1] // (3 * HEAD)
    block_rows = groups * stretch_rows
    blocks = keys.shape[0] // block_rows
    steps = blocks + 1
    in_sequence(order_ref, stacks, stretch_rows, keys, values)
    for block in range(blocks):
        lower = block * block_rows
        keys_t[block] = keys[lower : lower + block_rows, :].T
    offset = groups * HEAD
    for d in range(QUAD):
        for e in range(2):
            shrink = shrink_of(stretch_of(order_ref, z, member, d, e), stretch_rows)
            rows = slice(e * stretch_rows, (e + 1) * stretch_rows)
            for g in range(groups):
                into = slice(g * stretch_rows, (g + 1) * stretch_rows)
                stacked[2 * d + e, into, :] = queries[d][rows, g * HEAD : (g + 1) * HEAD]
                grads[2 * d + e, into, :] = (
                    queries[d][rows, offset + g * HEAD : offset + (g + 1) * HEAD].astype(
                        jnp.float32
                    )
                    * shrink
                ).astype(jnp.bfloat16)
    total_t[...] = jnp.zeros_like(total_t)
    key_total[...] = jnp.zeros_like(key_total)
    value_total[...] = jnp.zeros_like(value_total)
    gap[...] = lax.broadcasted_iota(jnp.int32, gap.shape, 0) - lax.rem(
        lax.broadcasted_iota(jnp.int32, gap.shape, 1), stretch_rows
    )

    def advance(step, _):
        for d in range(QUAD):
            row, stretch, block = step_place(
                stretch_of(order_ref, z, member, d, 0),
                stretch_of(order_ref, z, member, d, 1),
                step,
                d,
                groups,
            )
            rows = rows_at(block, block_rows)
            raw = dot(keys[rows, :], stacked[row], NT)
            weight_grad = dot(values[rows, :], grads[row], NT)
            visible = gap[...] <= stretch * stretch_rows - block * block_rows
            part = sigmoid_of(raw, visible)
            weights = raw * SCALE * part
            score_grad = (weight_grad * (part + weights * (1.0 - part))).astype(jnp.bfloat16)
            weights = weights.astype(jnp.bfloat16)
            total_t[row] += dot(keys_t[block], score_grad, NN)
            key_total[rows, :] += dot(score_grad, stacked[row], NN)
            value_total[rows, :] += dot(weights, grads[row], NN)
        return 0

    lax.fori_loop(0, steps, advance, 0)
    for d in range(QUAD):
        for e in range(2):
            query_grad = (total_t[2 * d + e].T * SCALE).astype(jnp.bfloat16)
            for g in range(groups):
                query_outs[d][
                    e * stretch_rows : (e + 1) * stretch_rows, g * HEAD : (g + 1) * HEAD
                ] = query_grad[g * stretch_rows : (g + 1) * stretch_rows, :]
    for s in range(nz):
        target = lax.rem(z + s, nz)
        for d in range(QUAD):
            for e in range(2):
                rows = rows_at(stretch_of(order_ref, target, member, d, e), stretch_rows)
                lower = (2 * d + e) * stretch_rows
                key_outs[s][lower : lower + stretch_rows, :HEAD] = (
                    key_total[rows, :] * SCALE
                ).astype(jnp.bfloat16)
                key_outs[s][lower : lower + stretch_rows, HEAD:] = value_total[rows, :].astype(
                    jnp.bfloat16
                )


def sum_kernel(nz, *refs):
    parts, pieces = refs[:nz], refs[nz:]
    rows = pieces[0].shape[0]
    for d in range(QUAD):
        lower = d * rows
        pieces[d][...] = sum(
            part[lower : lower + rows, :].astype(jnp.float32) for part in parts
        ).astype(jnp.bfloat16)


def key_grad_kernel(*refs):
    pieces, (key_out, value_out) = refs[:QUAD], refs[QUAD:]
    _, member = place()
    for d in range(QUAD):
        head = columns(member ^ d, HEAD)
        key_out[0, :, head] = pieces[d][:, :HEAD]
        value_out[0, :, head] = pieces[d][:, HEAD:]


def query_grad_kernel(*refs):
    pieces, out = refs[:QUAD], refs[QUAD]
    _, member = place()
    for d in range(QUAD):
        out[0, :, columns(member ^ d, pieces[d].shape[1])] = pieces[d][...]


def gate_kernel(*refs):
    pieces, (gate_ref, gain_ref, out) = refs[:QUAD], refs[QUAD:]
    _, member = place()
    attended = [piece[...].astype(jnp.float32) for piece in pieces]
    square = sum(jnp.sum(part * part, axis=1, keepdims=True) for part in attended)
    factor = lax.rsqrt(square / gate_ref.shape[2] + norm_eps)
    for d in range(QUAD):
        head = columns(member ^ d, pieces[d].shape[1])
        out[0, :, head] = (
            attended[d] * factor * gain_ref[:, head] * gate_ref[0, :, head].astype(jnp.float32)
        ).astype(jnp.bfloat16)


def call(kernel, name, out_shape, specs, *args, scratch=(), flops=0, transcendentals=0):
    size = sum(a.size * a.dtype.itemsize for a in args)
    size += sum(math.prod(o.shape) * o.dtype.itemsize for o in out_shape)
    return pl.pallas_call(
        kernel,
        name=name,
        out_shape=out_shape,
        in_specs=specs,
        out_specs=[VMEM] * len(out_shape),
        scratch_shapes=list(scratch),
        compiler_params=PARAMS,
        cost_estimate=pl.CostEstimate(
            flops=flops, bytes_accessed=size, transcendentals=transcendentals
        ),
    )(*args)


def body(
    query_fwd,
    key_fwd,
    value_fwd,
    gate_fwd,
    types_fwd,
    query_bwd,
    key_bwd,
    value_bwd,
    grad_out,
    types_bwd,
    type_key,
    norm_gain,
    stretch_order,
):
    devices = lax.axis_size("ctx")
    nz = devices // QUAD
    rows = query_fwd.shape[1]
    total_rows = rows * devices
    width = query_fwd.shape[2] // QUAD
    groups = width // HEAD
    stretch_rows = rows // 2
    block_rows = groups * stretch_rows
    steps = total_rows // block_rows + 1
    pairs = steps * QUAD * block_rows * block_rows

    def swap(pieces):
        return [pieces[0]] + [
            lax.ppermute(pieces[d], "ctx", [(i, i ^ d) for i in range(devices)])
            for d in range(1, QUAD)
        ]

    def turn(block, s):
        return lax.ppermute(
            block, "ctx", [(i, (i + s * QUAD) % devices) for i in range(devices)]
        )

    def pack(key, value, types, name):
        return call(
            pack_keys,
            name,
            [bf16(rows, 2 * HEAD)] * QUAD,
            [VMEM] * 4,
            key,
            value,
            types,
            type_key,
            scratch=[pltpu.VMEM(key.shape[1:], jnp.bfloat16)],
        )

    def gather(pieces):
        stack = jnp.concatenate(swap(pieces), axis=0)
        return [stack] + [turn(stack, s) for s in range(1, nz)]

    back_stacks = gather(pack(key_bwd, value_bwd, types_bwd, "pack_keys_bwd"))
    queries = swap(
        call(
            pack_queries,
            "pack_queries",
            [bf16(rows, 3 * width)] * QUAD,
            [VMEM] * 3,
            query_bwd,
            grad_out,
            query_fwd,
        )
    )
    stacks = gather(pack(key_fwd, value_fwd, types_fwd, "pack_keys_fwd"))

    sequence = [pltpu.VMEM((total_rows, HEAD), jnp.bfloat16)] * 2
    stacked = pltpu.VMEM((2 * QUAD, block_rows, HEAD), jnp.bfloat16)
    gap = pltpu.VMEM((block_rows, block_rows), jnp.int32)
    outs = call(
        functools.partial(backward_kernel, nz),
        "backward",
        [bf16(rows, width)] * QUAD + [bf16(QUAD * rows, 2 * HEAD)] * nz,
        [SMEM] + [VMEM] * (QUAD + nz),
        stretch_order,
        *queries,
        *back_stacks,
        scratch=sequence
        + [
            pltpu.VMEM((total_rows // block_rows, HEAD, block_rows), jnp.bfloat16),
            stacked,
            stacked,
            pltpu.VMEM((2 * QUAD, HEAD, block_rows), jnp.float32),
            pltpu.VMEM((total_rows, HEAD), jnp.float32),
            pltpu.VMEM((total_rows, HEAD), jnp.float32),
            gap,
        ],
        flops=10 * pairs * HEAD,
        transcendentals=2 * pairs,
    )
    query_pieces, key_parts = outs[:QUAD], outs[QUAD:]
    key_pieces = swap(
        call(
            functools.partial(sum_kernel, nz),
            "sum_key_parts",
            [bf16(rows, 2 * HEAD)] * QUAD,
            [VMEM] * nz,
            key_parts[0],
            *[turn(key_parts[s], s) for s in range(1, nz)],
        )
    )
    query_pieces = swap(query_pieces)

    attended = swap(
        call(
            functools.partial(forward_kernel, nz),
            "forward",
            [bf16(rows, width)] * QUAD,
            [SMEM] + [VMEM] * (QUAD + nz),
            stretch_order,
            *queries,
            *stacks,
            scratch=sequence
            + [stacked, pltpu.VMEM((2 * QUAD, block_rows, HEAD), jnp.float32), gap],
            flops=4 * pairs * HEAD,
            transcendentals=2 * pairs,
        )
    )
    (gated,) = call(
        gate_kernel,
        "gate",
        [bf16(*gate_fwd.shape)],
        [VMEM] * (QUAD + 2),
        *attended,
        gate_fwd,
        norm_gain,
    )
    sections = lax.axis_size("pipe")
    handed = lax.ppermute(gated, "pipe", [(i, (i + 1) % sections) for i in range(sections)])
    (query_grad,) = call(
        query_grad_kernel,
        "query_grad",
        [bf16(*query_bwd.shape)],
        [VMEM] * QUAD,
        *query_pieces,
    )
    key_grad, value_grad = call(
        key_grad_kernel,
        "key_grad",
        [bf16(*key_bwd.shape), bf16(*value_bwd.shape)],
        [VMEM] * QUAD,
        *key_pieces,
    )
    return handed, query_grad, key_grad, value_grad


def solution(mesh):
    rows = P("pipe", "ctx", None)
    types = P("pipe", "ctx")
    return jax.shard_map(
        body,
        mesh=mesh,
        in_specs=(
            rows,
            rows,
            rows,
            rows,
            types,
            rows,
            rows,
            rows,
            rows,
            types,
            P("pipe", None, None),
            P("pipe", None),
            P("pipe", None),
        ),
        out_specs=(rows, rows, rows, rows),
        check_vma=False,
    )
```

```python
import functools
import math

import jax
import jax.numpy as jnp
from jax import lax
from jax.experimental import pallas as pl
from jax.experimental.pallas import tpu as pltpu
from jax.sharding import PartitionSpec as P

HEAD = 128
QUAD = 4
SCALE = HEAD ** (-0.5)
EXP2_SCALE = -SCALE / math.log(2.0)
norm_eps = 1e-06

VMEM = pl.BlockSpec(memory_space=pltpu.VMEM)
HBM = pl.BlockSpec(memory_space=pltpu.HBM)
SMEM = pl.BlockSpec(memory_space=pltpu.SMEM)
PARAMS = pltpu.CompilerParams(vmem_limit_bytes=40 * 1024 * 1024)

NN = (((1,), (0,)), ((), ()))
NT = (((1,), (1,)), ((), ()))
TN = (((0,), (0,)), ((), ()))


def dot(a, b, dims):
    return lax.dot_general(a, b, dims, preferred_element_type=jnp.float32)


def bf16(*shape):
    return jax.ShapeDtypeStruct(shape, jnp.bfloat16)


def place():
    index = lax.axis_index("ctx")
    return index // QUAD, index % QUAD


def columns(index, width):
    return pl.ds(pl.multiple_of(index * width, width), width)


def pack_keys(key_ref, value_ref, types_ref, table_ref, *refs):
    pieces, (keys, types, table, typed, arrived, placed) = refs[:QUAD], refs[QUAD:]
    _, member = place()
    copies = [
        pltpu.make_async_copy(source, target, arrived.at[i])
        for i, (source, target) in enumerate(
            [(types_ref, types), (table_ref.at[0], table), (key_ref.at[0], keys)]
        )
    ]
    copies += [
        pltpu.make_async_copy(
            value_ref.at[0, :, columns(member ^ d, HEAD)], pieces[d].at[:, HEAD:], placed.at[d]
        )
        for d in range(QUAD)
    ]
    for copy in copies:
        copy.start()
    for copy in copies[:3]:
        copy.wait()
    onehot = (
        lax.broadcasted_iota(jnp.int32, (table.shape[0], types.shape[1]), 0) == types[...]
    ).astype(jnp.float32).astype(jnp.bfloat16)
    type_rows = dot(onehot, table[...], TN)
    typed[...] = (keys[...].astype(jnp.float32) + type_rows).astype(jnp.bfloat16)
    for d in range(QUAD):
        pieces[d][:, :HEAD] = typed[:, columns(member ^ d, HEAD)]
    for copy in copies[3:]:
        copy.wait()


def pack_queries(query_b_ref, grad_ref, query_f_ref, *refs):
    pieces, placed = refs[:QUAD], refs[QUAD]
    _, member = place()
    width = query_b_ref.shape[2] // QUAD
    copies = [
        pltpu.make_async_copy(
            source.at[0, :, columns(member ^ d, width)],
            pieces[d].at[:, i * width : (i + 1) * width],
            placed.at[3 * d + i],
        )
        for d in reversed(range(QUAD))
        for i, source in enumerate([query_b_ref, grad_ref, query_f_ref])
    ]
    for copy in copies:
        copy.start()
    for copy in copies:
        copy.wait()


def stretch_of(order_ref, quad_index, member, d, e):
    return order_ref[0, 2 * (quad_index * QUAD + (member ^ d)) + e]


def rows_at(index, count):
    return pl.ds(pl.multiple_of(index * count, count), count)


def in_sequence(order_ref, stacks, stretch_rows, keys, values):
    _, member = place()
    for source in range(stacks.shape[0]):
        stack = stacks.at[source]
        for d in range(QUAD):
            for e in range(2):
                rows = rows_at(stretch_of(order_ref, source, member, d, e), stretch_rows)
                lower = (2 * d + e) * stretch_rows
                keys[rows, :] = stack[lower : lower + stretch_rows, :HEAD]
                values[rows, :] = stack[lower : lower + stretch_rows, HEAD:]


def shrink_of(stretch, stretch_rows):
    pos = stretch * stretch_rows + lax.broadcasted_iota(jnp.int32, (stretch_rows, HEAD), 0)
    return lax.rsqrt((pos + 1).astype(jnp.float32))


def step_place(first, second, step, d, groups):
    blocks = first // groups + 1
    late = step >= blocks
    row = jnp.where(late, 2 * d + 1, 2 * d)
    stretch = jnp.where(late, second, first)
    block = jnp.where(late, step - blocks, step)
    return row, stretch, block


def sigmoid_of(raw, visible):
    part = pl.reciprocal(1.0 + jnp.exp2(raw * EXP2_SCALE), approx=True)
    return jnp.where(visible, part, 0.0)


def forward_kernel(order_ref, *refs):
    queries, refs = refs[:QUAD], refs[QUAD:]
    stacks, refs = refs[0], refs[1:]
    outs, refs = refs[:QUAD], refs[QUAD:]
    keys, values, stacked, total, gap = refs
    z, member = place()
    stretch_rows = queries[0].shape[0] // 2
    groups = queries[0].shape[1] // (3 * HEAD)
    block_rows = groups * stretch_rows
    steps = keys.shape[0] // block_rows + 1
    in_sequence(order_ref, stacks, stretch_rows, keys, values)
    offset = 2 * groups * HEAD
    for d in range(QUAD):
        for e in range(2):
            for g in range(groups):
                stacked[2 * d + e, g * stretch_rows : (g + 1) * stretch_rows, :] = queries[d][
                    e * stretch_rows : (e + 1) * stretch_rows,
                    offset + g * HEAD : offset + (g + 1) * HEAD,
                ]
    total[...] = jnp.zeros_like(total)
    gap[...] = lax.broadcasted_iota(jnp.int32, gap.shape, 1) - lax.rem(
        lax.broadcasted_iota(jnp.int32, gap.shape, 0), stretch_rows
    )

    def advance(step, _):
        for d in range(QUAD):
            row, stretch, block = step_place(
                stretch_of(order_ref, z, member, d, 0),
                stretch_of(order_ref, z, member, d, 1),
                step,
                d,
                groups,
            )
            rows = rows_at(block, block_rows)
            raw = dot(stacked[row], keys[rows, :], NT)
            visible = gap[...] <= stretch * stretch_rows - block * block_rows
            weights = (raw * SCALE * sigmoid_of(raw, visible)).astype(jnp.bfloat16)
            total[row] += dot(weights, values[rows, :], NN)
        return 0

    lax.fori_loop(0, steps, advance, 0)
    for d in range(QUAD):
        for e in range(2):
            shrink = shrink_of(stretch_of(order_ref, z, member, d, e), stretch_rows)
            for g in range(groups):
                outs[d][e * stretch_rows : (e + 1) * stretch_rows, g * HEAD : (g + 1) * HEAD] = (
                    total[2 * d + e, g * stretch_rows : (g + 1) * stretch_rows, :] * shrink
                ).astype(jnp.bfloat16)


def backward_kernel(order_ref, *refs):
    queries, refs = refs[:QUAD], refs[QUAD:]
    stacks, refs = refs[0], refs[1:]
    query_outs, refs = refs[:QUAD], refs[QUAD:]
    key_out, refs = refs[0], refs[1:]
    keys, values, keys_t, stacked, grads, total_t, key_total, value_total, gap = refs
    z, member = place()
    stretch_rows = queries[0].shape[0] // 2
    groups = queries[0].shape[1] // (3 * HEAD)
    block_rows = groups * stretch_rows
    blocks = keys.shape[0] // block_rows
    steps = blocks + 1
    in_sequence(order_ref, stacks, stretch_rows, keys, values)
    for block in range(blocks):
        lower = block * block_rows
        keys_t[block] = keys[lower : lower + block_rows, :].T
    offset = groups * HEAD
    for d in range(QUAD):
        for e in range(2):
            shrink = shrink_of(stretch_of(order_ref, z, member, d, e), stretch_rows)
            rows = slice(e * stretch_rows, (e + 1) * stretch_rows)
            for g in range(groups):
                into = slice(g * stretch_rows, (g + 1) * stretch_rows)
                stacked[2 * d + e, into, :] = queries[d][rows, g * HEAD : (g + 1) * HEAD]
                grads[2 * d + e, into, :] = (
                    queries[d][rows, offset + g * HEAD : offset + (g + 1) * HEAD].astype(
                        jnp.float32
                    )
                    * shrink
                ).astype(jnp.bfloat16)
    total_t[...] = jnp.zeros_like(total_t)
    key_total[...] = jnp.zeros_like(key_total)
    value_total[...] = jnp.zeros_like(value_total)
    gap[...] = lax.broadcasted_iota(jnp.int32, gap.shape, 0) - lax.rem(
        lax.broadcasted_iota(jnp.int32, gap.shape, 1), stretch_rows
    )

    def advance(step, _):
        for d in range(QUAD):
            row, stretch, block = step_place(
                stretch_of(order_ref, z, member, d, 0),
                stretch_of(order_ref, z, member, d, 1),
                step,
                d,
                groups,
            )
            rows = rows_at(block, block_rows)
            raw = dot(keys[rows, :], stacked[row], NT)
            weight_grad = dot(values[rows, :], grads[row], NT)
            visible = gap[...] <= stretch * stretch_rows - block * block_rows
            part = sigmoid_of(raw, visible)
            weights = raw * SCALE * part
            score_grad = (weight_grad * (part + weights * (1.0 - part))).astype(jnp.bfloat16)
            weights = weights.astype(jnp.bfloat16)
            total_t[row] += dot(keys_t[block], score_grad, NN)
            key_total[rows, :] += dot(score_grad, stacked[row], NN)
            value_total[rows, :] += dot(weights, grads[row], NN)
        return 0

    lax.fori_loop(0, steps, advance, 0)
    for d in range(QUAD):
        for e in range(2):
            query_grad = (total_t[2 * d + e].T * SCALE).astype(jnp.bfloat16)
            for g in range(groups):
                query_outs[d][
                    e * stretch_rows : (e + 1) * stretch_rows, g * HEAD : (g + 1) * HEAD
                ] = query_grad[g * stretch_rows : (g + 1) * stretch_rows, :]
    for target in range(key_out.shape[0]):
        for d in range(QUAD):
            for e in range(2):
                rows = rows_at(stretch_of(order_ref, target, member, d, e), stretch_rows)
                lower = (2 * d + e) * stretch_rows
                key_out[target, lower : lower + stretch_rows, :HEAD] = (
                    key_total[rows, :] * SCALE
                ).astype(jnp.bfloat16)
                key_out[target, lower : lower + stretch_rows, HEAD:] = value_total[rows, :].astype(
                    jnp.bfloat16
                )


def key_grad_kernel(*refs):
    pieces, (key_out, value_out) = refs[:QUAD], refs[QUAD:]
    _, member = place()
    for d in range(QUAD):
        head = columns(member ^ d, HEAD)
        key_out[0, :, head] = pieces[d][:, :HEAD]
        value_out[0, :, head] = pieces[d][:, HEAD:]


def query_grad_kernel(*refs):
    pieces, out = refs[:QUAD], refs[QUAD]
    _, member = place()
    for d in range(QUAD):
        out[0, :, columns(member ^ d, pieces[d].shape[1])] = pieces[d][...]


def gate_kernel(*refs):
    pieces, (gate_ref, gain_ref, out) = refs[:QUAD], refs[QUAD:]
    _, member = place()
    attended = [piece[...].astype(jnp.float32) for piece in pieces]
    square = sum(jnp.sum(part * part, axis=1, keepdims=True) for part in attended)
    factor = lax.rsqrt(square / gate_ref.shape[2] + norm_eps)
    for d in range(QUAD):
        head = columns(member ^ d, pieces[d].shape[1])
        out[0, :, head] = (
            attended[d] * factor * gain_ref[:, head] * gate_ref[0, :, head].astype(jnp.float32)
        ).astype(jnp.bfloat16)


def call(kernel, name, out_shape, specs, *args, scratch=(), flops=0, transcendentals=0):
    size = sum(a.size * a.dtype.itemsize for a in args)
    size += sum(math.prod(o.shape) * o.dtype.itemsize for o in out_shape)
    return pl.pallas_call(
        kernel,
        name=name,
        out_shape=out_shape,
        in_specs=specs,
        out_specs=[VMEM] * len(out_shape),
        scratch_shapes=list(scratch),
        compiler_params=PARAMS,
        cost_estimate=pl.CostEstimate(
            flops=flops, bytes_accessed=size, transcendentals=transcendentals
        ),
    )(*args)


def body(
    query_fwd,
    key_fwd,
    value_fwd,
    gate_fwd,
    types_fwd,
    query_bwd,
    key_bwd,
    value_bwd,
    grad_out,
    types_bwd,
    type_key,
    norm_gain,
    stretch_order,
):
    devices = lax.axis_size("ctx")
    nz = devices // QUAD
    rows = query_fwd.shape[1]
    total_rows = rows * devices
    width = query_fwd.shape[2] // QUAD
    groups = width // HEAD
    stretch_rows = rows // 2
    block_rows = groups * stretch_rows
    steps = total_rows // block_rows + 1
    pairs = steps * QUAD * block_rows * block_rows

    def swap(pieces):
        return [pieces[0]] + [
            lax.ppermute(pieces[d], "ctx", [(i, i ^ d) for i in range(devices)])
            for d in range(1, QUAD)
        ]

    def turn(block, s):
        return lax.ppermute(
            block, "ctx", [(i, (i + s * QUAD) % devices) for i in range(devices)]
        )

    def hand(block, d):
        sections = lax.axis_size("pipe")
        route = [
            (i * sections + p, (i ^ d) * sections + (p + 1) % sections)
            for i in range(devices)
            for p in range(sections)
        ]
        return lax.ppermute(block, ("ctx", "pipe"), route)

    def pack(key, value, types, name):
        return call(
            pack_keys,
            name,
            [bf16(rows, 2 * HEAD)] * QUAD,
            [HBM] * 4,
            key,
            value,
            types,
            type_key,
            scratch=[
                pltpu.VMEM(key.shape[1:], jnp.bfloat16),
                pltpu.VMEM(types.shape, jnp.int32),
                pltpu.VMEM(type_key.shape[1:], jnp.bfloat16),
                pltpu.VMEM(key.shape[1:], jnp.bfloat16),
                pltpu.SemaphoreType.DMA((3,)),
                pltpu.SemaphoreType.DMA((QUAD,)),
            ],
        )

    lines = [[z * QUAD + m for z in range(nz)] for m in range(QUAD)]

    def gather(pieces):
        stack = jnp.concatenate(swap(pieces), axis=0)
        return lax.all_gather(stack, "ctx", axis_index_groups=lines)

    back_stacks = gather(pack(key_bwd, value_bwd, types_bwd, "pack_keys_bwd"))
    queries = swap(
        call(
            pack_queries,
            "pack_queries",
            [bf16(rows, 3 * width)] * QUAD,
            [HBM] * 3,
            query_bwd,
            grad_out,
            query_fwd,
            scratch=[pltpu.SemaphoreType.DMA((3 * QUAD,))],
        )
    )
    gate_before, gain_before = hand(gate_fwd, 0), hand(norm_gain, 0)
    stacks = gather(pack(key_fwd, value_fwd, types_fwd, "pack_keys_fwd"))

    sequence = [pltpu.VMEM((total_rows, HEAD), jnp.bfloat16)] * 2
    stacked = pltpu.VMEM((2 * QUAD, block_rows, HEAD), jnp.bfloat16)
    gap = pltpu.VMEM((block_rows, block_rows), jnp.int32)
    outs = call(
        backward_kernel,
        "backward",
        [bf16(rows, width)] * QUAD + [bf16(nz, QUAD * rows, 2 * HEAD)],
        [SMEM] + [VMEM] * (QUAD + 1),
        stretch_order,
        *queries,
        back_stacks,
        scratch=sequence
        + [
            pltpu.VMEM((total_rows // block_rows, HEAD, block_rows), jnp.bfloat16),
            stacked,
            stacked,
            pltpu.VMEM((2 * QUAD, HEAD, block_rows), jnp.float32),
            pltpu.VMEM((total_rows, HEAD), jnp.float32),
            pltpu.VMEM((total_rows, HEAD), jnp.float32),
            gap,
        ],
        flops=10 * pairs * HEAD,
        transcendentals=2 * pairs,
    )
    query_pieces, key_parts = outs[:QUAD], outs[QUAD]
    key_sum = lax.psum_scatter(key_parts, "ctx", axis_index_groups=lines)
    key_pieces = swap([key_sum[d * rows : (d + 1) * rows] for d in range(QUAD)])
    query_pieces = swap(query_pieces)

    attended = call(
        forward_kernel,
        "forward",
        [bf16(rows, width)] * QUAD,
        [SMEM] + [VMEM] * (QUAD + 1),
        stretch_order,
        *queries,
        stacks,
        scratch=sequence
        + [stacked, pltpu.VMEM((2 * QUAD, block_rows, HEAD), jnp.float32), gap],
    )
    (handed,) = call(
        gate_kernel,
        "gate",
        [bf16(*gate_fwd.shape)],
        [VMEM] * (QUAD + 2),
        *[hand(attended[d], d) for d in range(QUAD)],
        gate_before,
        gain_before,
    )
    (query_grad,) = call(
        query_grad_kernel,
        "query_grad",
        [bf16(*query_bwd.shape)],
        [VMEM] * QUAD,
        *query_pieces,
    )
    key_grad, value_grad = call(
        key_grad_kernel,
        "key_grad",
        [bf16(*key_bwd.shape), bf16(*value_bwd.shape)],
        [VMEM] * QUAD,
        *key_pieces,
    )
    return handed, query_grad, key_grad, value_grad


def solution(mesh):
    rows = P("pipe", "ctx", None)
    types = P("pipe", "ctx")
    return jax.shard_map(
        body,
        mesh=mesh,
        in_specs=(
            rows,
            rows,
            rows,
            rows,
            types,
            rows,
            rows,
            rows,
            rows,
            types,
            P("pipe", None, None),
            P("pipe", None),
            P("pipe", None),
        ),
        out_specs=(rows, rows, rows, rows),
        check_vma=False,
    )
```

```python
import functools
import math

import jax
import jax.numpy as jnp
from jax import lax
from jax.experimental import pallas as pl
from jax.experimental.pallas import tpu as pltpu
from jax.sharding import PartitionSpec as P

HEAD = 128
QUAD = 4
SCALE = HEAD ** (-0.5)
EXP2_SCALE = -SCALE / math.log(2.0)
norm_eps = 1e-06

VMEM = pl.BlockSpec(memory_space=pltpu.VMEM)
HBM = pl.BlockSpec(memory_space=pltpu.HBM)
SMEM = pl.BlockSpec(memory_space=pltpu.SMEM)
MIB = 1024 * 1024

NN = (((1,), (0,)), ((), ()))
NT = (((1,), (1,)), ((), ()))
TN = (((0,), (0,)), ((), ()))


def dot(a, b, dims):
    return lax.dot_general(a, b, dims, preferred_element_type=jnp.float32)


def bf16(*shape):
    return jax.ShapeDtypeStruct(shape, jnp.bfloat16)


def place():
    index = lax.axis_index("ctx")
    return index // QUAD, index % QUAD


def columns(index, width):
    return pl.ds(pl.multiple_of(index * width, width), width)


def pack_keys(key_ref, value_ref, types_ref, table_ref, *refs):
    pieces, (keys, types, table, typed, arrived, placed) = refs[:QUAD], refs[QUAD:]
    _, member = place()
    copies = [
        pltpu.make_async_copy(source, target, arrived.at[i])
        for i, (source, target) in enumerate(
            [(types_ref, types), (table_ref.at[0], table), (key_ref.at[0], keys)]
        )
    ]
    copies += [
        pltpu.make_async_copy(
            value_ref.at[0, :, columns(member ^ d, HEAD)], pieces[d].at[:, HEAD:], placed.at[d]
        )
        for d in range(QUAD)
    ]
    for copy in copies:
        copy.start()
    for copy in copies[:3]:
        copy.wait()
    onehot = (
        lax.broadcasted_iota(jnp.int32, (table.shape[0], types.shape[1]), 0) == types[...]
    ).astype(jnp.float32).astype(jnp.bfloat16)
    type_rows = dot(onehot, table[...], TN)
    typed[...] = (keys[...].astype(jnp.float32) + type_rows).astype(jnp.bfloat16)
    for d in range(QUAD):
        pieces[d][:, :HEAD] = typed[:, columns(member ^ d, HEAD)]
    for copy in copies[3:]:
        copy.wait()


def pack_queries(query_b_ref, grad_ref, query_f_ref, *refs):
    pieces, placed = refs[:QUAD], refs[QUAD]
    _, member = place()
    width = query_b_ref.shape[2] // QUAD
    copies = [
        pltpu.make_async_copy(
            source.at[0, :, columns(member ^ d, width)],
            pieces[d].at[:, i * width : (i + 1) * width],
            placed.at[3 * d + i],
        )
        for d in reversed(range(QUAD))
        for i, source in enumerate([query_b_ref, grad_ref, query_f_ref])
    ]
    for copy in copies:
        copy.start()
    for copy in copies:
        copy.wait()


def stretch_of(order_ref, quad_index, member, d, e):
    return order_ref[0, 2 * (quad_index * QUAD + (member ^ d)) + e]


def rows_at(index, count):
    return pl.ds(pl.multiple_of(index * count, count), count)


def in_sequence(order_ref, stacks, stretch_rows, keys, values):
    z, member = place()
    nz = len(stacks)
    for s, stack in enumerate(stacks):
        source = lax.rem(z - s + nz, nz)
        for d in range(QUAD):
            for e in range(2):
                rows = rows_at(stretch_of(order_ref, source, member, d, e), stretch_rows)
                lower = (2 * d + e) * stretch_rows
                keys[rows, :] = stack[lower : lower + stretch_rows, :HEAD]
                values[rows, :] = stack[lower : lower + stretch_rows, HEAD:]


def shrink_of(stretch, stretch_rows):
    pos = stretch * stretch_rows + lax.broadcasted_iota(jnp.int32, (stretch_rows, HEAD), 0)
    return lax.rsqrt((pos + 1).astype(jnp.float32))


def step_place(first, second, step, d, groups):
    blocks = first // groups + 1
    late = step >= blocks
    row = jnp.where(late, 2 * d + 1, 2 * d)
    stretch = jnp.where(late, second, first)
    block = jnp.where(late, step - blocks, step)
    return row, stretch, block


def sigmoid_of(raw, visible):
    part = pl.reciprocal(1.0 + jnp.exp2(raw * EXP2_SCALE), approx=True)
    return jnp.where(visible, part, 0.0)


def forward_kernel(nz, order_ref, *refs):
    queries, refs = refs[:QUAD], refs[QUAD:]
    stacks, refs = refs[:nz], refs[nz:]
    outs, refs = refs[:QUAD], refs[QUAD:]
    keys, values, stacked, total, gap = refs
    z, member = place()
    stretch_rows = queries[0].shape[0] // 2
    groups = queries[0].shape[1] // (3 * HEAD)
    block_rows = groups * stretch_rows
    steps = keys.shape[0] // block_rows + 1
    in_sequence(order_ref, stacks, stretch_rows, keys, values)
    offset = 2 * groups * HEAD
    for d in range(QUAD):
        for e in range(2):
            for g in range(groups):
                stacked[2 * d + e, g * stretch_rows : (g + 1) * stretch_rows, :] = queries[d][
                    e * stretch_rows : (e + 1) * stretch_rows,
                    offset + g * HEAD : offset + (g + 1) * HEAD,
                ]
    total[...] = jnp.zeros_like(total)
    gap[...] = lax.broadcasted_iota(jnp.int32, gap.shape, 1) - lax.rem(
        lax.broadcasted_iota(jnp.int32, gap.shape, 0), stretch_rows
    )

    def advance(step, _):
        for d in range(QUAD):
            row, stretch, block = step_place(
                stretch_of(order_ref, z, member, d, 0),
                stretch_of(order_ref, z, member, d, 1),
                step,
                d,
                groups,
            )
            rows = rows_at(block, block_rows)
            raw = dot(stacked[row], keys[rows, :], NT)
            visible = gap[...] <= stretch * stretch_rows - block * block_rows
            weights = (raw * SCALE * sigmoid_of(raw, visible)).astype(jnp.bfloat16)
            total[row] += dot(weights, values[rows, :], NN)
        return 0

    lax.fori_loop(0, steps, advance, 0)
    for d in range(QUAD):
        for e in range(2):
            shrink = shrink_of(stretch_of(order_ref, z, member, d, e), stretch_rows)
            for g in range(groups):
                outs[d][e * stretch_rows : (e + 1) * stretch_rows, g * HEAD : (g + 1) * HEAD] = (
                    total[2 * d + e, g * stretch_rows : (g + 1) * stretch_rows, :] * shrink
                ).astype(jnp.bfloat16)


def backward_kernel(nz, order_ref, *refs):
    queries, refs = refs[:QUAD], refs[QUAD:]
    stacks, refs = refs[:nz], refs[nz:]
    query_outs, refs = refs[:QUAD], refs[QUAD:]
    key_outs, refs = refs[:nz], refs[nz:]
    keys, values, keys_t, stacked, grads, total_t, key_total, value_total, gap = refs
    z, member = place()
    stretch_rows = queries[0].shape[0] // 2
    groups = queries[0].shape[1] // (3 * HEAD)
    block_rows = groups * stretch_rows
    blocks = keys.shape[0] // block_rows
    steps = blocks + 1
    in_sequence(order_ref, stacks, stretch_rows, keys, values)
    for block in range(blocks):
        lower = block * block_rows
        keys_t[block] = keys[lower : lower + block_rows, :].T
    offset = groups * HEAD
    for d in range(QUAD):
        for e in range(2):
            shrink = shrink_of(stretch_of(order_ref, z, member, d, e), stretch_rows)
            rows = slice(e * stretch_rows, (e + 1) * stretch_rows)
            for g in range(groups):
                into = slice(g * stretch_rows, (g + 1) * stretch_rows)
                stacked[2 * d + e, into, :] = queries[d][rows, g * HEAD : (g + 1) * HEAD]
                grads[2 * d + e, into, :] = (
                    queries[d][rows, offset + g * HEAD : offset + (g + 1) * HEAD].astype(
                        jnp.float32
                    )
                    * shrink
                ).astype(jnp.bfloat16)
    total_t[...] = jnp.zeros_like(total_t)
    key_total[...] = jnp.zeros_like(key_total)
    value_total[...] = jnp.zeros_like(value_total)
    gap[...] = lax.broadcasted_iota(jnp.int32, gap.shape, 0) - lax.rem(
        lax.broadcasted_iota(jnp.int32, gap.shape, 1), stretch_rows
    )

    def advance(step, _):
        for d in range(QUAD):
            row, stretch, block = step_place(
                stretch_of(order_ref, z, member, d, 0),
                stretch_of(order_ref, z, member, d, 1),
                step,
                d,
                groups,
            )
            rows = rows_at(block, block_rows)
            raw = dot(keys[rows, :], stacked[row], NT)
            weight_grad = dot(values[rows, :], grads[row], NT)
            visible = gap[...] <= stretch * stretch_rows - block * block_rows
            part = sigmoid_of(raw, visible)
            weights = raw * SCALE * part
            score_grad = (weight_grad * (part + weights * (1.0 - part))).astype(jnp.bfloat16)
            weights = weights.astype(jnp.bfloat16)
            total_t[row] += dot(keys_t[block], score_grad, NN)
            key_total[rows, :] += dot(score_grad, stacked[row], NN)
            value_total[rows, :] += dot(weights, grads[row], NN)
        return 0

    lax.fori_loop(0, steps, advance, 0)
    for d in range(QUAD):
        for e in range(2):
            query_grad = (total_t[2 * d + e].T * SCALE).astype(jnp.bfloat16)
            for g in range(groups):
                query_outs[d][
                    e * stretch_rows : (e + 1) * stretch_rows, g * HEAD : (g + 1) * HEAD
                ] = query_grad[g * stretch_rows : (g + 1) * stretch_rows, :]
    for s in range(nz):
        target = lax.rem(z + s, nz)
        for d in range(QUAD):
            for e in range(2):
                rows = rows_at(stretch_of(order_ref, target, member, d, e), stretch_rows)
                lower = (2 * d + e) * stretch_rows
                key_outs[s][lower : lower + stretch_rows, :HEAD] = (
                    key_total[rows, :] * SCALE
                ).astype(jnp.bfloat16)
                key_outs[s][lower : lower + stretch_rows, HEAD:] = value_total[rows, :].astype(
                    jnp.bfloat16
                )


def sum_kernel(*refs):
    parts, pieces = refs[:3], refs[3:]
    rows = pieces[0].shape[0]
    for d in range(QUAD):
        lower = d * rows
        pieces[d][...] = sum(
            part[lower : lower + rows, :].astype(jnp.float32) for part in parts
        ).astype(jnp.bfloat16)


def key_grad_kernel(*refs):
    pieces, (key_out, value_out) = refs[:QUAD], refs[QUAD:]
    _, member = place()
    for d in range(QUAD):
        head = columns(member ^ d, HEAD)
        key_out[0, :, head] = pieces[d][:, :HEAD]
        value_out[0, :, head] = pieces[d][:, HEAD:]


def query_grad_kernel(*refs):
    pieces, out = refs[:QUAD], refs[QUAD]
    _, member = place()
    for d in range(QUAD):
        out[0, :, columns(member ^ d, pieces[d].shape[1])] = pieces[d][...]


def gate_kernel(*refs):
    pieces, (gate_ref, gain_ref, out) = refs[:QUAD], refs[QUAD:]
    _, member = place()
    attended = [piece[...].astype(jnp.float32) for piece in pieces]
    square = sum(jnp.sum(part * part, axis=1, keepdims=True) for part in attended)
    factor = lax.rsqrt(square / gate_ref.shape[2] + norm_eps)
    for d in range(QUAD):
        head = columns(member ^ d, pieces[d].shape[1])
        out[0, :, head] = (
            attended[d] * factor * gain_ref[:, head] * gate_ref[0, :, head].astype(jnp.float32)
        ).astype(jnp.bfloat16)


def call(kernel, name, out_shape, specs, *args, scratch=(), flops=0, transcendentals=0, vmem=40):
    size = sum(a.size * a.dtype.itemsize for a in args)
    size += sum(math.prod(o.shape) * o.dtype.itemsize for o in out_shape)
    return pl.pallas_call(
        kernel,
        name=name,
        out_shape=out_shape,
        in_specs=specs,
        out_specs=[VMEM] * len(out_shape),
        scratch_shapes=list(scratch),
        compiler_params=pltpu.CompilerParams(vmem_limit_bytes=vmem * MIB),
        cost_estimate=pl.CostEstimate(
            flops=flops, bytes_accessed=size, transcendentals=transcendentals
        ),
    )(*args)


def body(
    query_fwd,
    key_fwd,
    value_fwd,
    gate_fwd,
    types_fwd,
    query_bwd,
    key_bwd,
    value_bwd,
    grad_out,
    types_bwd,
    type_key,
    norm_gain,
    stretch_order,
):
    devices = lax.axis_size("ctx")
    nz = devices // QUAD
    rows = query_fwd.shape[1]
    total_rows = rows * devices
    width = query_fwd.shape[2] // QUAD
    groups = width // HEAD
    stretch_rows = rows // 2
    block_rows = groups * stretch_rows
    steps = total_rows // block_rows + 1
    pairs = steps * QUAD * block_rows * block_rows

    def swap(pieces):
        return [pieces[0]] + [
            lax.ppermute(pieces[d], "ctx", [(i, i ^ d) for i in range(devices)])
            for d in range(1, QUAD)
        ]

    def turn(block, s):
        return lax.ppermute(
            block, "ctx", [(i, (i + s * QUAD) % devices) for i in range(devices)]
        )

    def hand(block, d):
        sections = lax.axis_size("pipe")
        route = [
            (i * sections + p, (i ^ d) * sections + (p + 1) % sections)
            for i in range(devices)
            for p in range(sections)
        ]
        return lax.ppermute(block, ("ctx", "pipe"), route)

    def pack(key, value, types, name):
        return call(
            pack_keys,
            name,
            [bf16(rows, 2 * HEAD)] * QUAD,
            [HBM] * 4,
            key,
            value,
            types,
            type_key,
            scratch=[
                pltpu.VMEM(key.shape[1:], jnp.bfloat16),
                pltpu.VMEM(types.shape, jnp.int32),
                pltpu.VMEM(type_key.shape[1:], jnp.bfloat16),
                pltpu.VMEM(key.shape[1:], jnp.bfloat16),
                pltpu.SemaphoreType.DMA((3,)),
                pltpu.SemaphoreType.DMA((QUAD,)),
            ],
            vmem=60,
        )

    ahead = nz // 2

    def ring_up(block):
        return turn(block, 1)

    def ring_down(block):
        return turn(block, nz - 1)

    def gather_first(stack):
        return [stack, ring_up(stack)], [ring_down(stack)]

    def gather_rest(up, down):
        while len(up) <= ahead:
            up = up + [ring_up(up[-1])]
        while len(up) + len(down) < nz:
            down = down + [ring_down(down[-1])]
        return up + down[::-1]

    def reduce_first(parts):
        return ring_up(parts[ahead]), ring_down(parts[ahead + 1])

    def add(a, b):
        return (a.astype(jnp.float32) + b.astype(jnp.float32)).astype(jnp.bfloat16)

    def reduce_rest(parts, up, down):
        for s in range(ahead - 1, 0, -1):
            up = ring_up(add(up, parts[s]))
        for s in range(ahead + 2, nz):
            down = ring_down(add(down, parts[s]))
        return parts[0], up, down

    back_stacks = gather_rest(
        *gather_first(
            jnp.concatenate(swap(pack(key_bwd, value_bwd, types_bwd, "pack_keys_bwd")), axis=0)
        )
    )
    queries = swap(
        call(
            pack_queries,
            "pack_queries",
            [bf16(rows, 3 * width)] * QUAD,
            [HBM] * 3,
            query_bwd,
            grad_out,
            query_fwd,
            scratch=[pltpu.SemaphoreType.DMA((3 * QUAD,))],
            vmem=60,
        )
    )
    gate_before, gain_before = hand(gate_fwd, 0), hand(norm_gain, 0)
    stack = jnp.concatenate(
        swap(pack(key_fwd, value_fwd, types_fwd, "pack_keys_fwd")), axis=0
    )
    stack, back_stacks, queries, gate_before, gain_before = lax.optimization_barrier(
        (stack, back_stacks, queries, gate_before, gain_before)
    )
    stacks = gather_first(stack)

    sequence = [pltpu.VMEM((total_rows, HEAD), jnp.bfloat16)] * 2
    stacked = pltpu.VMEM((2 * QUAD, block_rows, HEAD), jnp.bfloat16)
    gap = pltpu.VMEM((block_rows, block_rows), jnp.int32)
    outs = call(
        functools.partial(backward_kernel, nz),
        "backward",
        [bf16(rows, width)] * QUAD + [bf16(QUAD * rows, 2 * HEAD)] * nz,
        [SMEM] + [VMEM] * (QUAD + nz),
        stretch_order,
        *queries,
        *back_stacks,
        scratch=sequence
        + [
            pltpu.VMEM((total_rows // block_rows, HEAD, block_rows), jnp.bfloat16),
            stacked,
            stacked,
            pltpu.VMEM((2 * QUAD, HEAD, block_rows), jnp.float32),
            pltpu.VMEM((total_rows, HEAD), jnp.float32),
            pltpu.VMEM((total_rows, HEAD), jnp.float32),
            gap,
        ],
        flops=10 * pairs * HEAD,
        transcendentals=2 * pairs,
    )
    query_pieces, key_parts = outs[:QUAD], outs[QUAD:]
    query_pieces, key_parts, stacks = lax.optimization_barrier((query_pieces, key_parts, stacks))
    stacks = gather_rest(*stacks)
    key_sums = reduce_first(key_parts)
    query_pieces = swap(query_pieces)
    stacks, query_pieces = lax.optimization_barrier((stacks, query_pieces))
    attended = call(
        functools.partial(forward_kernel, nz),
        "forward",
        [bf16(rows, width)] * QUAD,
        [SMEM] + [VMEM] * (QUAD + nz),
        stretch_order,
        *queries,
        *stacks,
        scratch=sequence
        + [stacked, pltpu.VMEM((2 * QUAD, block_rows, HEAD), jnp.float32), gap],
    )
    (handed,) = call(
        gate_kernel,
        "gate",
        [bf16(*gate_fwd.shape)],
        [VMEM] * (QUAD + 2),
        *[hand(attended[d], d) for d in range(QUAD)],
        gate_before,
        gain_before,
    )
    key_sums = reduce_rest(key_parts, *key_sums)
    key_pieces = swap(
        call(
            sum_kernel,
            "sum_key_parts",
            [bf16(rows, 2 * HEAD)] * QUAD,
            [VMEM] * 3,
            *key_sums,
        )
    )
    (query_grad,) = call(
        query_grad_kernel,
        "query_grad",
        [bf16(*query_bwd.shape)],
        [VMEM] * QUAD,
        *query_pieces,
    )
    key_grad, value_grad = call(
        key_grad_kernel,
        "key_grad",
        [bf16(*key_bwd.shape), bf16(*value_bwd.shape)],
        [VMEM] * QUAD,
        *key_pieces,
    )
    return handed, query_grad, key_grad, value_grad


def solution(mesh):
    rows = P("pipe", "ctx", None)
    types = P("pipe", "ctx")
    return jax.shard_map(
        body,
        mesh=mesh,
        in_specs=(
            rows,
            rows,
            rows,
            rows,
            types,
            rows,
            rows,
            rows,
            rows,
            types,
            P("pipe", None, None),
            P("pipe", None),
            P("pipe", None),
        ),
        out_specs=(rows, rows, rows, rows),
        check_vma=False,
    )
```

```python
import functools
import math

import jax
import jax.numpy as jnp
from jax import lax
from jax.experimental import pallas as pl
from jax.experimental.pallas import tpu as pltpu
from jax.sharding import PartitionSpec as P

HEAD = 128
QUAD = 4
SCALE = HEAD ** (-0.5)
EXP2_SCALE = -SCALE / math.log(2.0)
GAIN_ROWS = 16
norm_eps = 1e-06

VMEM = pl.BlockSpec(memory_space=pltpu.VMEM)
HBM = pl.BlockSpec(memory_space=pltpu.HBM)
SMEM = pl.BlockSpec(memory_space=pltpu.SMEM)
MIB = 1024 * 1024

NN = (((1,), (0,)), ((), ()))
NT = (((1,), (1,)), ((), ()))
TN = (((0,), (0,)), ((), ()))


def dot(a, b, dims):
    return lax.dot_general(a, b, dims, preferred_element_type=jnp.float32)


def bf16(*shape):
    return jax.ShapeDtypeStruct(shape, jnp.bfloat16)


def place():
    index = lax.axis_index("ctx")
    return index // QUAD, index % QUAD


def columns(index, width):
    return pl.ds(pl.multiple_of(index * width, width), width)


def pack_keys(key_ref, value_ref, types_ref, table_ref, *refs):
    pieces, (keys, types, table, typed, arrived, placed) = refs[:QUAD], refs[QUAD:]
    _, member = place()
    copies = [
        pltpu.make_async_copy(source, target, arrived.at[i])
        for i, (source, target) in enumerate(
            [(types_ref, types), (table_ref.at[0], table), (key_ref.at[0], keys)]
        )
    ]
    copies += [
        pltpu.make_async_copy(
            value_ref.at[0, :, columns(member ^ d, HEAD)], pieces[d].at[:, HEAD:], placed.at[d]
        )
        for d in range(QUAD)
    ]
    for copy in copies:
        copy.start()
    for copy in copies[:3]:
        copy.wait()
    onehot = (
        lax.broadcasted_iota(jnp.int32, (table.shape[0], types.shape[1]), 0) == types[...]
    ).astype(jnp.float32).astype(jnp.bfloat16)
    type_rows = dot(onehot, table[...], TN)
    typed[...] = (keys[...].astype(jnp.float32) + type_rows).astype(jnp.bfloat16)
    for d in range(QUAD):
        pieces[d][:, :HEAD] = typed[:, columns(member ^ d, HEAD)]
    for copy in copies[3:]:
        copy.wait()


def pack_queries(query_ref, grad_ref, forward_ref, *refs):
    pieces, forward_pieces, placed = refs[:QUAD], refs[QUAD : 2 * QUAD], refs[2 * QUAD]
    _, member = place()
    width = query_ref.shape[2] // QUAD
    copies = []
    for d in reversed(range(QUAD)):
        for i, (source, target) in enumerate(
            [
                (query_ref, pieces[d].at[:, :width]),
                (grad_ref, pieces[d].at[:, width:]),
                (forward_ref, forward_pieces[d]),
            ]
        ):
            source = source.at[0, :, columns(member ^ d, width)]
            copies.append(pltpu.make_async_copy(source, target, placed.at[3 * d + i]))
    for copy in copies:
        copy.start()
    for copy in copies:
        copy.wait()


def pack_gate(gate_ref, gain_ref, out, sem):
    rows = gate_ref.shape[1]
    copy = pltpu.make_async_copy(gate_ref.at[0], out.at[:rows, :], sem)
    copy.start()
    rest = gain_ref[...]
    parts = []
    for _ in range(3):
        part = rest.astype(jnp.bfloat16).astype(jnp.float32)
        parts.append(part)
        rest = rest - part
    parts.append(jnp.zeros((GAIN_ROWS - 3, rest.shape[1]), jnp.float32))
    out[rows:, :] = jnp.concatenate(parts, axis=0).astype(jnp.bfloat16)
    copy.wait()


def stretch_of(order_ref, quad_index, member, d, e):
    return order_ref[0, 2 * (quad_index * QUAD + (member ^ d)) + e]


def rows_at(index, count):
    return pl.ds(pl.multiple_of(index * count, count), count)


def in_sequence(order_ref, stacks, stretch_rows, keys, values):
    z, member = place()
    nz = len(stacks)
    for s, stack in enumerate(stacks):
        source = lax.rem(z - s + nz, nz)
        for d in range(QUAD):
            for e in range(2):
                rows = rows_at(stretch_of(order_ref, source, member, d, e), stretch_rows)
                lower = (2 * d + e) * stretch_rows
                keys[rows, :] = stack[lower : lower + stretch_rows, :HEAD]
                values[rows, :] = stack[lower : lower + stretch_rows, HEAD:]


def shrink_of(stretch, stretch_rows):
    pos = stretch * stretch_rows + lax.broadcasted_iota(jnp.int32, (stretch_rows, HEAD), 0)
    return lax.rsqrt((pos + 1).astype(jnp.float32))


def step_place(first, second, step, d, groups):
    blocks = first // groups + 1
    late = step >= blocks
    row = jnp.where(late, 2 * d + 1, 2 * d)
    stretch = jnp.where(late, second, first)
    block = jnp.where(late, step - blocks, step)
    return row, stretch, block


def sigmoid_of(raw, visible):
    part = pl.reciprocal(1.0 + jnp.exp2(raw * EXP2_SCALE), approx=True)
    return jnp.where(visible, part, 0.0)


def forward_kernel(nz, order_ref, *refs):
    queries, refs = refs[:QUAD], refs[QUAD:]
    stacks, refs = refs[:nz], refs[nz:]
    outs, refs = refs[:QUAD], refs[QUAD:]
    keys, values, stacked, total, gap = refs
    z, member = place()
    stretch_rows = queries[0].shape[0] // 2
    groups = outs[0].shape[1] // HEAD
    block_rows = groups * stretch_rows
    steps = keys.shape[0] // block_rows + 1
    in_sequence(order_ref, stacks, stretch_rows, keys, values)
    for d in range(QUAD):
        for e in range(2):
            for g in range(groups):
                stacked[2 * d + e, g * stretch_rows : (g + 1) * stretch_rows, :] = queries[d][
                    e * stretch_rows : (e + 1) * stretch_rows,
                    g * HEAD : (g + 1) * HEAD,
                ]
    total[...] = jnp.zeros_like(total)
    gap[...] = lax.broadcasted_iota(jnp.int32, gap.shape, 1) - lax.rem(
        lax.broadcasted_iota(jnp.int32, gap.shape, 0), stretch_rows
    )

    def advance(step, _):
        for d in range(QUAD):
            row, stretch, block = step_place(
                stretch_of(order_ref, z, member, d, 0),
                stretch_of(order_ref, z, member, d, 1),
                step,
                d,
                groups,
            )
            rows = rows_at(block, block_rows)
            raw = dot(stacked[row], keys[rows, :], NT)
            visible = gap[...] <= stretch * stretch_rows - block * block_rows
            weights = (raw * SCALE * sigmoid_of(raw, visible)).astype(jnp.bfloat16)
            total[row] += dot(weights, values[rows, :], NN)
        return 0

    lax.fori_loop(0, steps, advance, 0)
    for d in range(QUAD):
        for e in range(2):
            shrink = shrink_of(stretch_of(order_ref, z, member, d, e), stretch_rows)
            for g in range(groups):
                outs[d][e * stretch_rows : (e + 1) * stretch_rows, g * HEAD : (g + 1) * HEAD] = (
                    total[2 * d + e, g * stretch_rows : (g + 1) * stretch_rows, :] * shrink
                ).astype(jnp.bfloat16)


def backward_kernel(nz, order_ref, *refs):
    queries, refs = refs[:QUAD], refs[QUAD:]
    stacks, refs = refs[:nz], refs[nz:]
    query_outs, refs = refs[:QUAD], refs[QUAD:]
    key_outs, refs = refs[:nz], refs[nz:]
    keys, values, keys_t, stacked, grads, total_t, key_total, value_total, gap = refs
    z, member = place()
    stretch_rows = queries[0].shape[0] // 2
    groups = queries[0].shape[1] // (2 * HEAD)
    block_rows = groups * stretch_rows
    blocks = keys.shape[0] // block_rows
    steps = blocks + 1
    in_sequence(order_ref, stacks, stretch_rows, keys, values)
    for block in range(blocks):
        lower = block * block_rows
        keys_t[block] = keys[lower : lower + block_rows, :].T
    offset = groups * HEAD
    for d in range(QUAD):
        for e in range(2):
            shrink = shrink_of(stretch_of(order_ref, z, member, d, e), stretch_rows)
            rows = slice(e * stretch_rows, (e + 1) * stretch_rows)
            for g in range(groups):
                into = slice(g * stretch_rows, (g + 1) * stretch_rows)
                stacked[2 * d + e, into, :] = queries[d][rows, g * HEAD : (g + 1) * HEAD]
                grads[2 * d + e, into, :] = (
                    queries[d][rows, offset + g * HEAD : offset + (g + 1) * HEAD].astype(
                        jnp.float32
                    )
                    * shrink
                ).astype(jnp.bfloat16)
    total_t[...] = jnp.zeros_like(total_t)
    key_total[...] = jnp.zeros_like(key_total)
    value_total[...] = jnp.zeros_like(value_total)
    gap[...] = lax.broadcasted_iota(jnp.int32, gap.shape, 0) - lax.rem(
        lax.broadcasted_iota(jnp.int32, gap.shape, 1), stretch_rows
    )

    def advance(step, _):
        for d in range(QUAD):
            row, stretch, block = step_place(
                stretch_of(order_ref, z, member, d, 0),
                stretch_of(order_ref, z, member, d, 1),
                step,
                d,
                groups,
            )
            rows = rows_at(block, block_rows)
            raw = dot(keys[rows, :], stacked[row], NT)
            weight_grad = dot(values[rows, :], grads[row], NT)
            visible = gap[...] <= stretch * stretch_rows - block * block_rows
            part = sigmoid_of(raw, visible)
            weights = raw * SCALE * part
            score_grad = (weight_grad * (part + weights * (1.0 - part))).astype(jnp.bfloat16)
            weights = weights.astype(jnp.bfloat16)
            total_t[row] += dot(keys_t[block], score_grad, NN)
            key_total[rows, :] += dot(score_grad, stacked[row], NN)
            value_total[rows, :] += dot(weights, grads[row], NN)
        return 0

    lax.fori_loop(0, steps, advance, 0)
    for d in range(QUAD):
        for e in range(2):
            query_grad = (total_t[2 * d + e].T * SCALE).astype(jnp.bfloat16)
            for g in range(groups):
                query_outs[d][
                    e * stretch_rows : (e + 1) * stretch_rows, g * HEAD : (g + 1) * HEAD
                ] = query_grad[g * stretch_rows : (g + 1) * stretch_rows, :]
    for s in range(nz):
        target = lax.rem(z + s, nz)
        for d in range(QUAD):
            for e in range(2):
                rows = rows_at(stretch_of(order_ref, target, member, d, e), stretch_rows)
                lower = (2 * d + e) * stretch_rows
                key_outs[s][lower : lower + stretch_rows, :HEAD] = (
                    key_total[rows, :] * SCALE
                ).astype(jnp.bfloat16)
                key_outs[s][lower : lower + stretch_rows, HEAD:] = value_total[rows, :].astype(
                    jnp.bfloat16
                )


def sum_kernel(*refs):
    parts, pieces = refs[:3], refs[3:]
    rows = pieces[0].shape[0]
    for d in range(QUAD):
        lower = d * rows
        pieces[d][...] = sum(
            part[lower : lower + rows, :].astype(jnp.float32) for part in parts
        ).astype(jnp.bfloat16)


def key_grad_kernel(*refs):
    pieces, (key_out, value_out) = refs[:QUAD], refs[QUAD:]
    _, member = place()
    for d in range(QUAD):
        head = columns(member ^ d, HEAD)
        key_out[0, :, head] = pieces[d][:, :HEAD]
        value_out[0, :, head] = pieces[d][:, HEAD:]


def query_grad_kernel(*refs):
    pieces, out = refs[:QUAD], refs[QUAD]
    _, member = place()
    for d in range(QUAD):
        out[0, :, columns(member ^ d, pieces[d].shape[1])] = pieces[d][...]


def gate_kernel(*refs):
    pieces, (gate_ref, out) = refs[:QUAD], refs[QUAD:]
    _, member = place()
    rows = out.shape[1]
    attended = [piece[...].astype(jnp.float32) for piece in pieces]
    square = sum(jnp.sum(part * part, axis=1, keepdims=True) for part in attended)
    factor = lax.rsqrt(square / out.shape[2] + norm_eps)
    for d in range(QUAD):
        head = columns(member ^ d, pieces[d].shape[1])
        gain = sum(gate_ref[rows : rows + GAIN_ROWS, head].astype(jnp.float32)[i : i + 1] for i in range(3))
        out[0, :, head] = (
            attended[d] * factor * gain * gate_ref[:rows, head].astype(jnp.float32)
        ).astype(jnp.bfloat16)


def call(kernel, name, out_shape, specs, *args, scratch=(), flops=0, transcendentals=0, vmem=40):
    size = sum(a.size * a.dtype.itemsize for a in args)
    size += sum(math.prod(o.shape) * o.dtype.itemsize for o in out_shape)
    return pl.pallas_call(
        kernel,
        name=name,
        out_shape=out_shape,
        in_specs=specs,
        out_specs=[VMEM] * len(out_shape),
        scratch_shapes=list(scratch),
        compiler_params=pltpu.CompilerParams(vmem_limit_bytes=vmem * MIB),
        cost_estimate=pl.CostEstimate(
            flops=flops, bytes_accessed=size, transcendentals=transcendentals
        ),
    )(*args)


def body(
    query_fwd,
    key_fwd,
    value_fwd,
    gate_fwd,
    types_fwd,
    query_bwd,
    key_bwd,
    value_bwd,
    grad_out,
    types_bwd,
    type_key,
    norm_gain,
    stretch_order,
):
    devices = lax.axis_size("ctx")
    nz = devices // QUAD
    rows = query_fwd.shape[1]
    total_rows = rows * devices
    width = query_fwd.shape[2] // QUAD
    groups = width // HEAD
    stretch_rows = rows // 2
    block_rows = groups * stretch_rows
    steps = total_rows // block_rows + 1
    pairs = steps * QUAD * block_rows * block_rows

    def swap(pieces):
        return [pieces[0]] + [
            lax.ppermute(pieces[d], "ctx", [(i, i ^ d) for i in range(devices)])
            for d in range(1, QUAD)
        ]

    def turn(block, s):
        return lax.ppermute(
            block, "ctx", [(i, (i + s * QUAD) % devices) for i in range(devices)]
        )

    def hand(block, d):
        sections = lax.axis_size("pipe")
        route = [
            (i * sections + p, (i ^ d) * sections + (p + 1) % sections)
            for i in range(devices)
            for p in range(sections)
        ]
        return lax.ppermute(block, ("ctx", "pipe"), route)

    def pack(key, value, types, name):
        return call(
            pack_keys,
            name,
            [bf16(rows, 2 * HEAD)] * QUAD,
            [HBM] * 4,
            key,
            value,
            types,
            type_key,
            scratch=[
                pltpu.VMEM(key.shape[1:], jnp.bfloat16),
                pltpu.VMEM(types.shape, jnp.int32),
                pltpu.VMEM(type_key.shape[1:], jnp.bfloat16),
                pltpu.VMEM(key.shape[1:], jnp.bfloat16),
                pltpu.SemaphoreType.DMA((3,)),
                pltpu.SemaphoreType.DMA((QUAD,)),
            ],
            vmem=60,
        )

    ahead = nz // 2

    def ring_up(block):
        return turn(block, 1)

    def ring_down(block):
        return turn(block, nz - 1)

    def gather_first(stack):
        return [stack, ring_up(stack)], [ring_down(stack)]

    def gather_rest(up, down):
        while len(up) <= ahead:
            up = up + [ring_up(up[-1])]
        while len(up) + len(down) < nz:
            down = down + [ring_down(down[-1])]
        return up + down[::-1]

    def reduce_first(parts):
        return ring_up(parts[ahead]), ring_down(parts[ahead + 1])

    def add(a, b):
        return (a.astype(jnp.float32) + b.astype(jnp.float32)).astype(jnp.bfloat16)

    def reduce_rest(parts, up, down):
        for s in range(ahead - 1, 0, -1):
            up = ring_up(add(up, parts[s]))
        for s in range(ahead + 2, nz):
            down = ring_down(add(down, parts[s]))
        return parts[0], up, down

    back_pieces = swap(pack(key_bwd, value_bwd, types_bwd, "pack_keys_bwd"))
    packed = call(
        pack_queries,
        "pack_queries",
        [bf16(rows, 2 * width)] * QUAD + [bf16(rows, width)] * QUAD,
        [HBM] * 3,
        query_bwd,
        grad_out,
        query_fwd,
        scratch=[pltpu.SemaphoreType.DMA((3 * QUAD,))],
        vmem=60,
    )
    back_pieces, packed = lax.optimization_barrier((back_pieces, packed))
    back_queries, queries = swap(packed[:QUAD]), packed[QUAD:]
    back_stacks = gather_first(jnp.concatenate(back_pieces, axis=0))
    pieces = pack(key_fwd, value_fwd, types_fwd, "pack_keys_fwd")
    back_stacks, back_queries, pieces = lax.optimization_barrier(
        (back_stacks, back_queries, pieces)
    )
    back_stacks = gather_rest(*back_stacks)
    stack = jnp.concatenate(swap(pieces), axis=0)
    (gate_before,) = call(
        pack_gate,
        "pack_gate",
        [bf16(rows + GAIN_ROWS, QUAD * width)],
        [HBM, VMEM],
        gate_fwd,
        norm_gain,
        scratch=[pltpu.SemaphoreType.DMA],
        vmem=60,
    )
    gate_before = hand(gate_before, 0)
    stack, queries, back_stacks, gate_before = lax.optimization_barrier(
        (stack, queries, back_stacks, gate_before)
    )
    stacks = gather_first(stack)
    queries = swap(queries)

    sequence = [pltpu.VMEM((total_rows, HEAD), jnp.bfloat16)] * 2
    stacked = pltpu.VMEM((2 * QUAD, block_rows, HEAD), jnp.bfloat16)
    gap = pltpu.VMEM((block_rows, block_rows), jnp.int32)
    outs = call(
        functools.partial(backward_kernel, nz),
        "backward",
        [bf16(rows, width)] * QUAD + [bf16(QUAD * rows, 2 * HEAD)] * nz,
        [SMEM] + [VMEM] * (QUAD + nz),
        stretch_order,
        *back_queries,
        *back_stacks,
        scratch=sequence
        + [
            pltpu.VMEM((total_rows // block_rows, HEAD, block_rows), jnp.bfloat16),
            stacked,
            stacked,
            pltpu.VMEM((2 * QUAD, HEAD, block_rows), jnp.float32),
            pltpu.VMEM((total_rows, HEAD), jnp.float32),
            pltpu.VMEM((total_rows, HEAD), jnp.float32),
            gap,
        ],
        flops=10 * pairs * HEAD,
        transcendentals=2 * pairs,
    )
    query_pieces, key_parts = outs[:QUAD], outs[QUAD:]
    query_pieces, key_parts, stacks, queries = lax.optimization_barrier(
        (query_pieces, key_parts, stacks, queries)
    )
    stacks = gather_rest(*stacks)
    query_pieces = swap(query_pieces)
    stacks, query_pieces, key_parts = lax.optimization_barrier((stacks, query_pieces, key_parts))
    key_sums = reduce_first(key_parts)
    attended = call(
        functools.partial(forward_kernel, nz),
        "forward",
        [bf16(rows, width)] * QUAD,
        [SMEM] + [VMEM] * (QUAD + nz),
        stretch_order,
        *queries,
        *stacks,
        scratch=sequence
        + [stacked, pltpu.VMEM((2 * QUAD, block_rows, HEAD), jnp.float32), gap],
    )
    attended, key_up = lax.optimization_barrier((attended, key_sums[0]))
    (handed,) = call(
        gate_kernel,
        "gate",
        [bf16(*gate_fwd.shape)],
        [VMEM] * (QUAD + 1),
        *[hand(attended[d], d) for d in range(QUAD)],
        gate_before,
    )
    key_sums = reduce_rest(key_parts, key_up, key_sums[1])
    key_pieces = swap(
        call(
            sum_kernel,
            "sum_key_parts",
            [bf16(rows, 2 * HEAD)] * QUAD,
            [VMEM] * 3,
            *key_sums,
        )
    )
    (query_grad,) = call(
        query_grad_kernel,
        "query_grad",
        [bf16(*query_bwd.shape)],
        [VMEM] * QUAD,
        *query_pieces,
    )
    key_grad, value_grad = call(
        key_grad_kernel,
        "key_grad",
        [bf16(*key_bwd.shape), bf16(*value_bwd.shape)],
        [VMEM] * QUAD,
        *key_pieces,
    )
    return handed, query_grad, key_grad, value_grad


def solution(mesh):
    rows = P("pipe", "ctx", None)
    types = P("pipe", "ctx")
    return jax.shard_map(
        body,
        mesh=mesh,
        in_specs=(
            rows,
            rows,
            rows,
            rows,
            types,
            rows,
            rows,
            rows,
            rows,
            types,
            P("pipe", None, None),
            P("pipe", None),
            P("pipe", None),
        ),
        out_specs=(rows, rows, rows, rows),
        check_vma=False,
    )
```

```python
import functools
import math

import jax
import jax.numpy as jnp
from jax import lax
from jax.experimental import pallas as pl
from jax.experimental.pallas import tpu as pltpu
from jax.sharding import PartitionSpec as P

HEAD = 128
QUAD = 4
SCALE = HEAD ** (-0.5)
EXP2_SCALE = -SCALE / math.log(2.0)
GAIN_ROWS = 16
norm_eps = 1e-06

VMEM = pl.BlockSpec(memory_space=pltpu.VMEM)
HBM = pl.BlockSpec(memory_space=pltpu.HBM)
SMEM = pl.BlockSpec(memory_space=pltpu.SMEM)
MIB = 1024 * 1024

NN = (((1,), (0,)), ((), ()))
NT = (((1,), (1,)), ((), ()))
TN = (((0,), (0,)), ((), ()))


def dot(a, b, dims):
    return lax.dot_general(a, b, dims, preferred_element_type=jnp.float32)


def bf16(*shape):
    return jax.ShapeDtypeStruct(shape, jnp.bfloat16)


def place():
    index = lax.axis_index("ctx")
    return index // QUAD, index % QUAD


def columns(index, width):
    return pl.ds(pl.multiple_of(index * width, width), width)


def pack_keys(key_ref, value_ref, types_ref, table_ref, *refs):
    pieces, (keys, types, table, typed, arrived, placed) = refs[:QUAD], refs[QUAD:]
    _, member = place()
    copies = [
        pltpu.make_async_copy(source, target, arrived.at[i])
        for i, (source, target) in enumerate(
            [(types_ref, types), (table_ref.at[0], table), (key_ref.at[0], keys)]
        )
    ]
    copies += [
        pltpu.make_async_copy(
            value_ref.at[0, :, columns(member ^ d, HEAD)], pieces[d].at[:, HEAD:], placed.at[d]
        )
        for d in range(QUAD)
    ]
    for copy in copies:
        copy.start()
    for copy in copies[:3]:
        copy.wait()
    onehot = (
        lax.broadcasted_iota(jnp.int32, (table.shape[0], types.shape[1]), 0) == types[...]
    ).astype(jnp.float32).astype(jnp.bfloat16)
    type_rows = dot(onehot, table[...], TN)
    typed[...] = (keys[...].astype(jnp.float32) + type_rows).astype(jnp.bfloat16)
    for d in range(QUAD):
        pieces[d][:, :HEAD] = typed[:, columns(member ^ d, HEAD)]
    for copy in copies[3:]:
        copy.wait()


def pack_queries(query_ref, grad_ref, forward_ref, gate_ref, gain_ref, *refs):
    pieces, forward_pieces, (gate_out, placed) = refs[:QUAD], refs[QUAD : 2 * QUAD], refs[2 * QUAD :]
    _, member = place()
    width = query_ref.shape[2] // QUAD
    rows = gate_ref.shape[1]
    copies = []
    for d in reversed(range(QUAD)):
        for i, (source, target) in enumerate(
            [
                (query_ref, pieces[d].at[:, :width]),
                (grad_ref, pieces[d].at[:, width:]),
                (forward_ref, forward_pieces[d]),
            ]
        ):
            source = source.at[0, :, columns(member ^ d, width)]
            copies.append(pltpu.make_async_copy(source, target, placed.at[3 * d + i]))
    copies.append(
        pltpu.make_async_copy(gate_ref.at[0], gate_out.at[:rows, :], placed.at[3 * QUAD])
    )
    for copy in copies:
        copy.start()
    rest = gain_ref[...]
    parts = []
    for _ in range(3):
        part = rest.astype(jnp.bfloat16).astype(jnp.float32)
        parts.append(part)
        rest = rest - part
    parts.append(jnp.zeros((GAIN_ROWS - 3, rest.shape[1]), jnp.float32))
    gate_out[rows:, :] = jnp.concatenate(parts, axis=0).astype(jnp.bfloat16)
    for copy in copies:
        copy.wait()


def stretch_of(order_ref, quad_index, member, d, e):
    return order_ref[0, 2 * (quad_index * QUAD + (member ^ d)) + e]


def rows_at(index, count):
    return pl.ds(pl.multiple_of(index * count, count), count)


def in_sequence(order_ref, stacks, stretch_rows, keys, values):
    z, member = place()
    nz = len(stacks)
    for s, stack in enumerate(stacks):
        source = lax.rem(z - s + nz, nz)
        for d in range(QUAD):
            for e in range(2):
                rows = rows_at(stretch_of(order_ref, source, member, d, e), stretch_rows)
                lower = (2 * d + e) * stretch_rows
                keys[rows, :] = stack[lower : lower + stretch_rows, :HEAD]
                values[rows, :] = stack[lower : lower + stretch_rows, HEAD:]


def shrink_of(stretch, stretch_rows):
    pos = stretch * stretch_rows + lax.broadcasted_iota(jnp.int32, (stretch_rows, HEAD), 0)
    return lax.rsqrt((pos + 1).astype(jnp.float32))


def step_place(first, second, step, d, groups):
    blocks = first // groups + 1
    late = step >= blocks
    row = jnp.where(late, 2 * d + 1, 2 * d)
    stretch = jnp.where(late, second, first)
    block = jnp.where(late, step - blocks, step)
    return row, stretch, block


def sigmoid_of(raw, visible):
    part = pl.reciprocal(1.0 + jnp.exp2(raw * EXP2_SCALE), approx=True)
    return jnp.where(visible, part, 0.0)


def forward_kernel(nz, order_ref, *refs):
    queries, refs = refs[:QUAD], refs[QUAD:]
    stacks, refs = refs[:nz], refs[nz:]
    outs, refs = refs[:QUAD], refs[QUAD:]
    keys, values, stacked, total, gap = refs
    z, member = place()
    stretch_rows = queries[0].shape[0] // 2
    groups = outs[0].shape[1] // HEAD
    block_rows = groups * stretch_rows
    steps = keys.shape[0] // block_rows + 1
    in_sequence(order_ref, stacks, stretch_rows, keys, values)
    for d in range(QUAD):
        for e in range(2):
            for g in range(groups):
                stacked[2 * d + e, g * stretch_rows : (g + 1) * stretch_rows, :] = queries[d][
                    e * stretch_rows : (e + 1) * stretch_rows,
                    g * HEAD : (g + 1) * HEAD,
                ]
    total[...] = jnp.zeros_like(total)
    gap[...] = lax.broadcasted_iota(jnp.int32, gap.shape, 1) - lax.rem(
        lax.broadcasted_iota(jnp.int32, gap.shape, 0), stretch_rows
    )

    def advance(step, _):
        for d in range(QUAD):
            row, stretch, block = step_place(
                stretch_of(order_ref, z, member, d, 0),
                stretch_of(order_ref, z, member, d, 1),
                step,
                d,
                groups,
            )
            rows = rows_at(block, block_rows)
            raw = dot(stacked[row], keys[rows, :], NT)
            visible = gap[...] <= stretch * stretch_rows - block * block_rows
            weights = (raw * SCALE * sigmoid_of(raw, visible)).astype(jnp.bfloat16)
            total[row] += dot(weights, values[rows, :], NN)
        return 0

    lax.fori_loop(0, steps, advance, 0)
    for d in range(QUAD):
        for e in range(2):
            shrink = shrink_of(stretch_of(order_ref, z, member, d, e), stretch_rows)
            for g in range(groups):
                outs[d][e * stretch_rows : (e + 1) * stretch_rows, g * HEAD : (g + 1) * HEAD] = (
                    total[2 * d + e, g * stretch_rows : (g + 1) * stretch_rows, :] * shrink
                ).astype(jnp.bfloat16)


def backward_kernel(nz, order_ref, *refs):
    queries, refs = refs[:QUAD], refs[QUAD:]
    stacks, refs = refs[:nz], refs[nz:]
    query_outs, refs = refs[:QUAD], refs[QUAD:]
    key_outs, refs = refs[:nz], refs[nz:]
    keys, values, keys_t, stacked, grads, total_t, key_total, value_total, gap = refs
    z, member = place()
    stretch_rows = queries[0].shape[0] // 2
    groups = queries[0].shape[1] // (2 * HEAD)
    block_rows = groups * stretch_rows
    blocks = keys.shape[0] // block_rows
    steps = blocks + 1
    in_sequence(order_ref, stacks, stretch_rows, keys, values)
    for block in range(blocks):
        lower = block * block_rows
        keys_t[block] = keys[lower : lower + block_rows, :].T
    offset = groups * HEAD
    for d in range(QUAD):
        for e in range(2):
            shrink = shrink_of(stretch_of(order_ref, z, member, d, e), stretch_rows)
            rows = slice(e * stretch_rows, (e + 1) * stretch_rows)
            for g in range(groups):
                into = slice(g * stretch_rows, (g + 1) * stretch_rows)
                stacked[2 * d + e, into, :] = queries[d][rows, g * HEAD : (g + 1) * HEAD]
                grads[2 * d + e, into, :] = (
                    queries[d][rows, offset + g * HEAD : offset + (g + 1) * HEAD].astype(
                        jnp.float32
                    )
                    * shrink
                ).astype(jnp.bfloat16)
    total_t[...] = jnp.zeros_like(total_t)
    key_total[...] = jnp.zeros_like(key_total)
    value_total[...] = jnp.zeros_like(value_total)
    gap[...] = lax.broadcasted_iota(jnp.int32, gap.shape, 0) - lax.rem(
        lax.broadcasted_iota(jnp.int32, gap.shape, 1), stretch_rows
    )

    def advance(step, _):
        for d in range(QUAD):
            row, stretch, block = step_place(
                stretch_of(order_ref, z, member, d, 0),
                stretch_of(order_ref, z, member, d, 1),
                step,
                d,
                groups,
            )
            rows = rows_at(block, block_rows)
            raw = dot(keys[rows, :], stacked[row], NT)
            weight_grad = dot(values[rows, :], grads[row], NT)
            visible = gap[...] <= stretch * stretch_rows - block * block_rows
            part = sigmoid_of(raw, visible)
            weights = raw * SCALE * part
            score_grad = (weight_grad * (part + weights * (1.0 - part))).astype(jnp.bfloat16)
            weights = weights.astype(jnp.bfloat16)
            total_t[row] += dot(keys_t[block], score_grad, NN)
            key_total[rows, :] += dot(score_grad, stacked[row], NN)
            value_total[rows, :] += dot(weights, grads[row], NN)
        return 0

    lax.fori_loop(0, steps, advance, 0)
    for d in range(QUAD):
        for e in range(2):
            query_grad = (total_t[2 * d + e].T * SCALE).astype(jnp.bfloat16)
            for g in range(groups):
                query_outs[d][
                    e * stretch_rows : (e + 1) * stretch_rows, g * HEAD : (g + 1) * HEAD
                ] = query_grad[g * stretch_rows : (g + 1) * stretch_rows, :]
    for s in range(nz):
        target = lax.rem(z + s, nz)
        for d in range(QUAD):
            for e in range(2):
                rows = rows_at(stretch_of(order_ref, target, member, d, e), stretch_rows)
                lower = (2 * d + e) * stretch_rows
                key_outs[s][lower : lower + stretch_rows, :HEAD] = (
                    key_total[rows, :] * SCALE
                ).astype(jnp.bfloat16)
                key_outs[s][lower : lower + stretch_rows, HEAD:] = value_total[rows, :].astype(
                    jnp.bfloat16
                )


def sum_kernel(*refs):
    parts, pieces = refs[:3], refs[3:]
    rows = pieces[0].shape[0]
    for d in range(QUAD):
        lower = d * rows
        pieces[d][...] = sum(
            part[lower : lower + rows, :].astype(jnp.float32) for part in parts
        ).astype(jnp.bfloat16)


def key_grad_kernel(*refs):
    pieces, (key_out, value_out) = refs[:QUAD], refs[QUAD:]
    _, member = place()
    for d in range(QUAD):
        head = columns(member ^ d, HEAD)
        key_out[0, :, head] = pieces[d][:, :HEAD]
        value_out[0, :, head] = pieces[d][:, HEAD:]


def query_grad_kernel(*refs):
    pieces, out = refs[:QUAD], refs[QUAD]
    _, member = place()
    for d in range(QUAD):
        out[0, :, columns(member ^ d, pieces[d].shape[1])] = pieces[d][...]


def gate_kernel(*refs):
    pieces, (gate_ref, out) = refs[:QUAD], refs[QUAD:]
    _, member = place()
    rows = out.shape[1]
    attended = [piece[...].astype(jnp.float32) for piece in pieces]
    square = sum(jnp.sum(part * part, axis=1, keepdims=True) for part in attended)
    factor = lax.rsqrt(square / out.shape[2] + norm_eps)
    for d in range(QUAD):
        head = columns(member ^ d, pieces[d].shape[1])
        gain = sum(gate_ref[rows : rows + GAIN_ROWS, head].astype(jnp.float32)[i : i + 1] for i in range(3))
        out[0, :, head] = (
            attended[d] * factor * gain * gate_ref[:rows, head].astype(jnp.float32)
        ).astype(jnp.bfloat16)


def call(kernel, name, out_shape, specs, *args, scratch=(), flops=0, transcendentals=0, vmem=40):
    size = sum(a.size * a.dtype.itemsize for a in args)
    size += sum(math.prod(o.shape) * o.dtype.itemsize for o in out_shape)
    return pl.pallas_call(
        kernel,
        name=name,
        out_shape=out_shape,
        in_specs=specs,
        out_specs=[VMEM] * len(out_shape),
        scratch_shapes=list(scratch),
        compiler_params=pltpu.CompilerParams(vmem_limit_bytes=vmem * MIB),
        cost_estimate=pl.CostEstimate(
            flops=flops, bytes_accessed=size, transcendentals=transcendentals
        ),
    )(*args)


def body(
    query_fwd,
    key_fwd,
    value_fwd,
    gate_fwd,
    types_fwd,
    query_bwd,
    key_bwd,
    value_bwd,
    grad_out,
    types_bwd,
    type_key,
    norm_gain,
    stretch_order,
):
    devices = lax.axis_size("ctx")
    nz = devices // QUAD
    rows = query_fwd.shape[1]
    total_rows = rows * devices
    width = query_fwd.shape[2] // QUAD
    groups = width // HEAD
    stretch_rows = rows // 2
    block_rows = groups * stretch_rows
    steps = total_rows // block_rows + 1
    pairs = steps * QUAD * block_rows * block_rows

    def swap(pieces):
        return [pieces[0]] + [
            lax.ppermute(pieces[d], "ctx", [(i, i ^ d) for i in range(devices)])
            for d in range(1, QUAD)
        ]

    def turn(block, s):
        return lax.ppermute(
            block, "ctx", [(i, (i + s * QUAD) % devices) for i in range(devices)]
        )

    def hand(block, d):
        sections = lax.axis_size("pipe")
        route = [
            (i * sections + p, (i ^ d) * sections + (p + 1) % sections)
            for i in range(devices)
            for p in range(sections)
        ]
        return lax.ppermute(block, ("ctx", "pipe"), route)

    def pack(key, value, types, name):
        return call(
            pack_keys,
            name,
            [bf16(rows, 2 * HEAD)] * QUAD,
            [HBM] * 4,
            key,
            value,
            types,
            type_key,
            scratch=[
                pltpu.VMEM(key.shape[1:], jnp.bfloat16),
                pltpu.VMEM(types.shape, jnp.int32),
                pltpu.VMEM(type_key.shape[1:], jnp.bfloat16),
                pltpu.VMEM(key.shape[1:], jnp.bfloat16),
                pltpu.SemaphoreType.DMA((3,)),
                pltpu.SemaphoreType.DMA((QUAD,)),
            ],
            vmem=60,
        )

    ahead = nz // 2

    def ring_up(block):
        return turn(block, 1)

    def ring_down(block):
        return turn(block, nz - 1)

    def gather_first(stack):
        return [stack, ring_up(stack)], [ring_down(stack)]

    def gather_rest(up, down):
        while len(up) <= ahead:
            up = up + [ring_up(up[-1])]
        while len(up) + len(down) < nz:
            down = down + [ring_down(down[-1])]
        return up + down[::-1]

    def reduce_first(parts):
        return ring_up(parts[ahead]), ring_down(parts[ahead + 1])

    def add(a, b):
        return (a.astype(jnp.float32) + b.astype(jnp.float32)).astype(jnp.bfloat16)

    def reduce_rest(parts, up, down):
        for s in range(ahead - 1, 0, -1):
            up = ring_up(add(up, parts[s]))
        for s in range(ahead + 2, nz):
            down = ring_down(add(down, parts[s]))
        return parts[0], up, down

    back_pieces = swap(pack(key_bwd, value_bwd, types_bwd, "pack_keys_bwd"))
    packed = call(
        pack_queries,
        "pack_queries",
        [bf16(rows, 2 * width)] * QUAD
        + [bf16(rows, width)] * QUAD
        + [bf16(rows + GAIN_ROWS, QUAD * width)],
        [HBM] * 4 + [VMEM],
        query_bwd,
        grad_out,
        query_fwd,
        gate_fwd,
        norm_gain,
        scratch=[pltpu.SemaphoreType.DMA((3 * QUAD + 1,))],
        vmem=60,
    )
    back_pieces, packed = lax.optimization_barrier((back_pieces, packed))
    back_queries, queries, gate_before = swap(packed[:QUAD]), packed[QUAD:-1], packed[-1]
    back_stacks = gather_rest(*gather_first(jnp.concatenate(back_pieces, axis=0)))
    pieces = pack(key_fwd, value_fwd, types_fwd, "pack_keys_fwd")
    gate_before = hand(gate_before, 0)
    back_queries, pieces, queries = lax.optimization_barrier((back_queries, pieces, queries))
    stack = jnp.concatenate(swap(pieces), axis=0)
    stack, queries, back_stacks, gate_before = lax.optimization_barrier(
        (stack, queries, back_stacks, gate_before)
    )
    stacks = [stack] + [turn(stack, s) for s in range(1, nz)]
    queries = swap(queries)

    sequence = [pltpu.VMEM((total_rows, HEAD), jnp.bfloat16)] * 2
    stacked = pltpu.VMEM((2 * QUAD, block_rows, HEAD), jnp.bfloat16)
    gap = pltpu.VMEM((block_rows, block_rows), jnp.int32)
    outs = call(
        functools.partial(backward_kernel, nz),
        "backward",
        [bf16(rows, width)] * QUAD + [bf16(QUAD * rows, 2 * HEAD)] * nz,
        [SMEM] + [VMEM] * (QUAD + nz),
        stretch_order,
        *back_queries,
        *back_stacks,
        scratch=sequence
        + [
            pltpu.VMEM((total_rows // block_rows, HEAD, block_rows), jnp.bfloat16),
            stacked,
            stacked,
            pltpu.VMEM((2 * QUAD, HEAD, block_rows), jnp.float32),
            pltpu.VMEM((total_rows, HEAD), jnp.float32),
            pltpu.VMEM((total_rows, HEAD), jnp.float32),
            gap,
        ],
        flops=10 * pairs * HEAD,
        transcendentals=2 * pairs,
    )
    query_pieces, key_parts = outs[:QUAD], outs[QUAD:]
    query_pieces, key_parts, stacks, queries = lax.optimization_barrier(
        (query_pieces, key_parts, stacks, queries)
    )
    key_sums = reduce_first(key_parts)
    query_pieces = swap(query_pieces)
    attended = call(
        functools.partial(forward_kernel, nz),
        "forward",
        [bf16(rows, width)] * QUAD,
        [SMEM] + [VMEM] * (QUAD + nz),
        stretch_order,
        *queries,
        *stacks,
        scratch=sequence
        + [stacked, pltpu.VMEM((2 * QUAD, block_rows, HEAD), jnp.float32), gap],
    )
    attended, key_up = lax.optimization_barrier((attended, key_sums[0]))
    (handed,) = call(
        gate_kernel,
        "gate",
        [bf16(*gate_fwd.shape)],
        [VMEM] * (QUAD + 1),
        *[hand(attended[d], d) for d in range(QUAD)],
        gate_before,
    )
    key_sums = reduce_rest(key_parts, key_up, key_sums[1])
    key_pieces = swap(
        call(
            sum_kernel,
            "sum_key_parts",
            [bf16(rows, 2 * HEAD)] * QUAD,
            [VMEM] * 3,
            *key_sums,
        )
    )
    handed, query_pieces = lax.optimization_barrier((handed, query_pieces))
    (query_grad,) = call(
        query_grad_kernel,
        "query_grad",
        [bf16(*query_bwd.shape)],
        [VMEM] * QUAD,
        *query_pieces,
    )
    key_grad, value_grad = call(
        key_grad_kernel,
        "key_grad",
        [bf16(*key_bwd.shape), bf16(*value_bwd.shape)],
        [VMEM] * QUAD,
        *key_pieces,
    )
    return handed, query_grad, key_grad, value_grad


def solution(mesh):
    rows = P("pipe", "ctx", None)
    types = P("pipe", "ctx")
    return jax.shard_map(
        body,
        mesh=mesh,
        in_specs=(
            rows,
            rows,
            rows,
            rows,
            types,
            rows,
            rows,
            rows,
            rows,
            types,
            P("pipe", None, None),
            P("pipe", None),
            P("pipe", None),
        ),
        out_specs=(rows, rows, rows, rows),
        check_vma=False,
    )
```

```python
import functools
import math

import jax
import jax.numpy as jnp
from jax import lax
from jax.experimental import pallas as pl
from jax.experimental.pallas import tpu as pltpu
from jax.sharding import PartitionSpec as P

HEAD = 128
QUAD = 4
SCALE = HEAD ** (-0.5)
EXP2_SCALE = -SCALE / math.log(2.0)
GAIN_ROWS = 16
norm_eps = 1e-06

VMEM = pl.BlockSpec(memory_space=pltpu.VMEM)
HBM = pl.BlockSpec(memory_space=pltpu.HBM)
SMEM = pl.BlockSpec(memory_space=pltpu.SMEM)
MIB = 1024 * 1024

NN = (((1,), (0,)), ((), ()))
NT = (((1,), (1,)), ((), ()))
TN = (((0,), (0,)), ((), ()))


def dot(a, b, dims):
    return lax.dot_general(a, b, dims, preferred_element_type=jnp.float32)


def bf16(*shape):
    return jax.ShapeDtypeStruct(shape, jnp.bfloat16)


def place():
    index = lax.axis_index("ctx")
    return index // QUAD, index % QUAD


def columns(index, width):
    return pl.ds(pl.multiple_of(index * width, width), width)


def pack_keys(
    key_ref, value_ref, types_ref, table_ref, pieces, keys, types, table, typed, arrived, placed
):
    copies = [
        pltpu.make_async_copy(source, target, arrived.at[i])
        for i, (source, target) in enumerate(
            [(types_ref, types), (table_ref.at[0], table), (key_ref.at[0], keys)]
        )
    ]
    copies += [
        pltpu.make_async_copy(
            value_ref.at[0, :, d * HEAD : (d + 1) * HEAD],
            pieces.at[d, :, HEAD:],
            placed.at[d],
        )
        for d in range(QUAD)
    ]
    for copy in copies:
        copy.start()
    for copy in copies[:3]:
        copy.wait()
    onehot = (
        lax.broadcasted_iota(jnp.int32, (table.shape[0], types.shape[1]), 0) == types[...]
    ).astype(jnp.float32).astype(jnp.bfloat16)
    type_rows = dot(onehot, table[...], TN)
    typed[...] = (keys[...].astype(jnp.float32) + type_rows).astype(jnp.bfloat16)
    for d in range(QUAD):
        pieces[d, :, :HEAD] = typed[:, d * HEAD : (d + 1) * HEAD]
    for copy in copies[3:]:
        copy.wait()


def pack_queries(
    query_ref, grad_ref, forward_ref, gate_ref, gain_ref, pieces, forward_pieces, gate_out, placed
):
    width = query_ref.shape[2] // QUAD
    rows = gate_ref.shape[1]
    copies = []
    for d in range(QUAD):
        for i, (source, target) in enumerate(
            [
                (query_ref, pieces.at[d, :, :width]),
                (grad_ref, pieces.at[d, :, width:]),
                (forward_ref, forward_pieces.at[d]),
            ]
        ):
            source = source.at[0, :, d * width : (d + 1) * width]
            copies.append(pltpu.make_async_copy(source, target, placed.at[3 * d + i]))
    copies.append(
        pltpu.make_async_copy(gate_ref.at[0], gate_out.at[:rows, :], placed.at[3 * QUAD])
    )
    for copy in copies:
        copy.start()
    rest = gain_ref[...]
    parts = []
    for _ in range(3):
        part = rest.astype(jnp.bfloat16).astype(jnp.float32)
        parts.append(part)
        rest = rest - part
    parts.append(jnp.zeros((GAIN_ROWS - 3, rest.shape[1]), jnp.float32))
    gate_out[rows:, :] = jnp.concatenate(parts, axis=0).astype(jnp.bfloat16)
    for copy in copies:
        copy.wait()


def stretch_of(order_ref, quad_index, d, e):
    return order_ref[0, 2 * (quad_index * QUAD + d) + e]


def rows_at(index, count):
    return pl.ds(pl.multiple_of(index * count, count), count)


def in_sequence(order_ref, stacks, stretch_rows, keys, values):
    z, _ = place()
    nz = len(stacks)
    for s, stack in enumerate(stacks):
        source = lax.rem(z - s + nz, nz)
        for d in range(QUAD):
            for e in range(2):
                rows = rows_at(stretch_of(order_ref, source, d, e), stretch_rows)
                keys[rows, :] = stack[d, e * stretch_rows : (e + 1) * stretch_rows, :HEAD]
                values[rows, :] = stack[d, e * stretch_rows : (e + 1) * stretch_rows, HEAD:]


def shrink_of(stretch, stretch_rows):
    pos = stretch * stretch_rows + lax.broadcasted_iota(jnp.int32, (stretch_rows, HEAD), 0)
    return lax.rsqrt((pos + 1).astype(jnp.float32))


def step_place(first, second, step, d, groups):
    blocks = first // groups + 1
    late = step >= blocks
    row = jnp.where(late, 2 * d + 1, 2 * d)
    stretch = jnp.where(late, second, first)
    block = jnp.where(late, step - blocks, step)
    return row, stretch, block


def sigmoid_of(raw, visible):
    part = pl.reciprocal(1.0 + jnp.exp2(raw * EXP2_SCALE), approx=True)
    return jnp.where(visible, part, 0.0)


def forward_kernel(nz, order_ref, *refs):
    queries, refs = refs[0], refs[1:]
    stacks, refs = refs[:nz], refs[nz:]
    outs, refs = refs[:QUAD], refs[QUAD:]
    keys, values, stacked, total, gap = refs
    z, member = place()
    stretch_rows = queries.shape[1] // 2
    groups = outs[0].shape[1] // HEAD
    block_rows = groups * stretch_rows
    steps = keys.shape[0] // block_rows + 1
    in_sequence(order_ref, stacks, stretch_rows, keys, values)
    for d in range(QUAD):
        for e in range(2):
            for g in range(groups):
                stacked[2 * d + e, g * stretch_rows : (g + 1) * stretch_rows, :] = queries[
                    member ^ d,
                    e * stretch_rows : (e + 1) * stretch_rows,
                    g * HEAD : (g + 1) * HEAD,
                ]
    total[...] = jnp.zeros_like(total)
    gap[...] = lax.broadcasted_iota(jnp.int32, gap.shape, 1) - lax.rem(
        lax.broadcasted_iota(jnp.int32, gap.shape, 0), stretch_rows
    )

    def advance(step, _):
        for d in range(QUAD):
            row, stretch, block = step_place(
                stretch_of(order_ref, z, member ^ d, 0),
                stretch_of(order_ref, z, member ^ d, 1),
                step,
                d,
                groups,
            )
            rows = rows_at(block, block_rows)
            raw = dot(stacked[row], keys[rows, :], NT)
            visible = gap[...] <= stretch * stretch_rows - block * block_rows
            weights = (raw * SCALE * sigmoid_of(raw, visible)).astype(jnp.bfloat16)
            total[row] += dot(weights, values[rows, :], NN)
        return 0

    lax.fori_loop(0, steps, advance, 0)
    for d in range(QUAD):
        for e in range(2):
            shrink = shrink_of(stretch_of(order_ref, z, member ^ d, e), stretch_rows)
            for g in range(groups):
                outs[d][e * stretch_rows : (e + 1) * stretch_rows, g * HEAD : (g + 1) * HEAD] = (
                    total[2 * d + e, g * stretch_rows : (g + 1) * stretch_rows, :] * shrink
                ).astype(jnp.bfloat16)


def backward_kernel(nz, order_ref, *refs):
    queries, refs = refs[0], refs[1:]
    stacks, refs = refs[:nz], refs[nz:]
    query_out, refs = refs[0], refs[1:]
    key_outs, refs = refs[:nz], refs[nz:]
    keys, values, keys_t, stacked, grads, total_t, key_total, value_total, gap = refs
    z, _ = place()
    stretch_rows = queries.shape[1] // 2
    groups = queries.shape[2] // (2 * HEAD)
    block_rows = groups * stretch_rows
    blocks = keys.shape[0] // block_rows
    steps = blocks + 1
    in_sequence(order_ref, stacks, stretch_rows, keys, values)
    for block in range(blocks):
        lower = block * block_rows
        keys_t[block] = keys[lower : lower + block_rows, :].T
    offset = groups * HEAD
    for d in range(QUAD):
        for e in range(2):
            shrink = shrink_of(stretch_of(order_ref, z, d, e), stretch_rows)
            rows = slice(e * stretch_rows, (e + 1) * stretch_rows)
            for g in range(groups):
                into = slice(g * stretch_rows, (g + 1) * stretch_rows)
                stacked[2 * d + e, into, :] = queries[d, rows, g * HEAD : (g + 1) * HEAD]
                grads[2 * d + e, into, :] = (
                    queries[d, rows, offset + g * HEAD : offset + (g + 1) * HEAD].astype(
                        jnp.float32
                    )
                    * shrink
                ).astype(jnp.bfloat16)
    total_t[...] = jnp.zeros_like(total_t)
    key_total[...] = jnp.zeros_like(key_total)
    value_total[...] = jnp.zeros_like(value_total)
    gap[...] = lax.broadcasted_iota(jnp.int32, gap.shape, 0) - lax.rem(
        lax.broadcasted_iota(jnp.int32, gap.shape, 1), stretch_rows
    )

    def advance(step, _):
        for d in range(QUAD):
            row, stretch, block = step_place(
                stretch_of(order_ref, z, d, 0),
                stretch_of(order_ref, z, d, 1),
                step,
                d,
                groups,
            )
            rows = rows_at(block, block_rows)
            raw = dot(keys[rows, :], stacked[row], NT)
            weight_grad = dot(values[rows, :], grads[row], NT)
            visible = gap[...] <= stretch * stretch_rows - block * block_rows
            part = sigmoid_of(raw, visible)
            weights = raw * SCALE * part
            score_grad = (weight_grad * (part + weights * (1.0 - part))).astype(jnp.bfloat16)
            weights = weights.astype(jnp.bfloat16)
            total_t[row] += dot(keys_t[block], score_grad, NN)
            key_total[rows, :] += dot(score_grad, stacked[row], NN)
            value_total[rows, :] += dot(weights, grads[row], NN)
        return 0

    lax.fori_loop(0, steps, advance, 0)
    for d in range(QUAD):
        for e in range(2):
            query_grad = (total_t[2 * d + e].T * SCALE).astype(jnp.bfloat16)
            for g in range(groups):
                query_out[
                    d, e * stretch_rows : (e + 1) * stretch_rows, g * HEAD : (g + 1) * HEAD
                ] = query_grad[g * stretch_rows : (g + 1) * stretch_rows, :]
    for s in range(nz):
        target = lax.rem(z + s, nz)
        for d in range(QUAD):
            for e in range(2):
                rows = rows_at(stretch_of(order_ref, target, d, e), stretch_rows)
                into = slice(e * stretch_rows, (e + 1) * stretch_rows)
                key_outs[s][d, into, :HEAD] = (
                    key_total[rows, :] * SCALE
                ).astype(jnp.bfloat16)
                key_outs[s][d, into, HEAD:] = value_total[rows, :].astype(
                    jnp.bfloat16
                )


def sum_kernel(a, b, c, out):
    out[...] = (
        a[...].astype(jnp.float32) + b[...].astype(jnp.float32) + c[...].astype(jnp.float32)
    ).astype(jnp.bfloat16)


def key_grad_kernel(pieces, key_out, value_out):
    for d in range(QUAD):
        key_out[0, :, d * HEAD : (d + 1) * HEAD] = pieces[d, :, :HEAD]
        value_out[0, :, d * HEAD : (d + 1) * HEAD] = pieces[d, :, HEAD:]


def query_grad_kernel(pieces, out):
    width = pieces.shape[2]
    for d in range(QUAD):
        out[0, :, d * width : (d + 1) * width] = pieces[d]


def gate_kernel(*refs):
    pieces, (gate_ref, out) = refs[:QUAD], refs[QUAD:]
    _, member = place()
    rows = out.shape[1]
    attended = [piece[...].astype(jnp.float32) for piece in pieces]
    square = sum(jnp.sum(part * part, axis=1, keepdims=True) for part in attended)
    factor = lax.rsqrt(square / out.shape[2] + norm_eps)
    for d in range(QUAD):
        head = columns(member ^ d, pieces[d].shape[1])
        gain = sum(gate_ref[rows : rows + GAIN_ROWS, head].astype(jnp.float32)[i : i + 1] for i in range(3))
        out[0, :, head] = (
            attended[d] * factor * gain * gate_ref[:rows, head].astype(jnp.float32)
        ).astype(jnp.bfloat16)


def call(kernel, name, out_shape, specs, *args, scratch=(), flops=0, transcendentals=0, vmem=40):
    size = sum(a.size * a.dtype.itemsize for a in args)
    size += sum(math.prod(o.shape) * o.dtype.itemsize for o in out_shape)
    return pl.pallas_call(
        kernel,
        name=name,
        out_shape=out_shape,
        in_specs=specs,
        out_specs=[VMEM] * len(out_shape),
        scratch_shapes=list(scratch),
        compiler_params=pltpu.CompilerParams(vmem_limit_bytes=vmem * MIB),
        cost_estimate=pl.CostEstimate(
            flops=flops, bytes_accessed=size, transcendentals=transcendentals
        ),
    )(*args)


def body(
    query_fwd,
    key_fwd,
    value_fwd,
    gate_fwd,
    types_fwd,
    query_bwd,
    key_bwd,
    value_bwd,
    grad_out,
    types_bwd,
    type_key,
    norm_gain,
    stretch_order,
):
    devices = lax.axis_size("ctx")
    nz = devices // QUAD
    rows = query_fwd.shape[1]
    total_rows = rows * devices
    width = query_fwd.shape[2] // QUAD
    groups = width // HEAD
    stretch_rows = rows // 2
    block_rows = groups * stretch_rows
    steps = total_rows // block_rows + 1
    pairs = steps * QUAD * block_rows * block_rows

    quads = [[z * QUAD + d for d in range(QUAD)] for z in range(nz)]

    def swap(pieces):
        return lax.all_to_all(pieces, "ctx", 0, 0, axis_index_groups=quads)

    def turn(block, s):
        return lax.ppermute(
            block, "ctx", [(i, (i + s * QUAD) % devices) for i in range(devices)]
        )

    def hand(block, d):
        sections = lax.axis_size("pipe")
        route = [
            (i * sections + p, (i ^ d) * sections + (p + 1) % sections)
            for i in range(devices)
            for p in range(sections)
        ]
        return lax.ppermute(block, ("ctx", "pipe"), route)

    def pack(key, value, types, name):
        return call(
            pack_keys,
            name,
            [bf16(QUAD, rows, 2 * HEAD)],
            [HBM] * 4,
            key,
            value,
            types,
            type_key,
            scratch=[
                pltpu.VMEM(key.shape[1:], jnp.bfloat16),
                pltpu.VMEM(types.shape, jnp.int32),
                pltpu.VMEM(type_key.shape[1:], jnp.bfloat16),
                pltpu.VMEM(key.shape[1:], jnp.bfloat16),
                pltpu.SemaphoreType.DMA((3,)),
                pltpu.SemaphoreType.DMA((QUAD,)),
            ],
            vmem=60,
        )[0]

    ahead = nz // 2

    def ring_up(block):
        return turn(block, 1)

    def ring_down(block):
        return turn(block, nz - 1)

    def gather_first(stack):
        return [stack, ring_up(stack)], [ring_down(stack)]

    def gather_rest(up, down):
        up, down = lax.optimization_barrier((up, down))
        while len(up) <= ahead:
            up = up + [ring_up(up[-1])]
        while len(up) + len(down) < nz:
            down = down + [ring_down(down[-1])]
        return up + down[::-1]

    def reduce_first(parts):
        return ring_up(parts[ahead]), ring_down(parts[ahead + 1])

    def add(a, b):
        return (a.astype(jnp.float32) + b.astype(jnp.float32)).astype(jnp.bfloat16)

    def reduce_rest(parts, up, down):
        for s in range(ahead - 1, 0, -1):
            up = ring_up(add(up, parts[s]))
        for s in range(ahead + 2, nz):
            down = ring_down(add(down, parts[s]))
        return parts[0], up, down

    back_pieces = swap(pack(key_bwd, value_bwd, types_bwd, "pack_keys_bwd"))
    packed = call(
        pack_queries,
        "pack_queries",
        [bf16(QUAD, rows, 2 * width), bf16(QUAD, rows, width)]
        + [bf16(rows + GAIN_ROWS, QUAD * width)],
        [HBM] * 4 + [VMEM],
        query_bwd,
        grad_out,
        query_fwd,
        gate_fwd,
        norm_gain,
        scratch=[pltpu.SemaphoreType.DMA((3 * QUAD + 1,))],
        vmem=60,
    )
    back_pieces, packed = lax.optimization_barrier((back_pieces, packed))
    back_queries, queries, gate_before = swap(packed[0]), packed[1], packed[2]
    back_stacks = gather_first(back_pieces)
    pieces = pack(key_fwd, value_fwd, types_fwd, "pack_keys_fwd")
    gate_before = hand(gate_before, 0)
    back_stacks, back_queries, pieces, queries = lax.optimization_barrier(
        (back_stacks, back_queries, pieces, queries)
    )
    back_stacks = gather_rest(*back_stacks)
    stack, queries = swap(pieces), swap(queries)
    stack, queries, back_stacks, gate_before = lax.optimization_barrier(
        (stack, queries, back_stacks, gate_before)
    )
    stacks = [stack] + [turn(stack, s) for s in range(1, nz)]

    sequence = [pltpu.VMEM((total_rows, HEAD), jnp.bfloat16)] * 2
    stacked = pltpu.VMEM((2 * QUAD, block_rows, HEAD), jnp.bfloat16)
    gap = pltpu.VMEM((block_rows, block_rows), jnp.int32)
    outs = call(
        functools.partial(backward_kernel, nz),
        "backward",
        [bf16(QUAD, rows, width)] + [bf16(QUAD, rows, 2 * HEAD)] * nz,
        [SMEM] + [VMEM] * (1 + nz),
        stretch_order,
        back_queries,
        *back_stacks,
        scratch=sequence
        + [
            pltpu.VMEM((total_rows // block_rows, HEAD, block_rows), jnp.bfloat16),
            stacked,
            stacked,
            pltpu.VMEM((2 * QUAD, HEAD, block_rows), jnp.float32),
            pltpu.VMEM((total_rows, HEAD), jnp.float32),
            pltpu.VMEM((total_rows, HEAD), jnp.float32),
            gap,
        ],
        flops=10 * pairs * HEAD,
        transcendentals=2 * pairs,
    )
    query_pieces, key_parts = outs[0], outs[1:]
    key_parts, stacks = lax.optimization_barrier((key_parts, stacks))
    key_sums = reduce_first(key_parts)
    query_pieces = swap(query_pieces)
    attended = call(
        functools.partial(forward_kernel, nz),
        "forward",
        [bf16(rows, width)] * QUAD,
        [SMEM] + [VMEM] * (1 + nz),
        stretch_order,
        queries,
        *stacks,
        scratch=sequence
        + [stacked, pltpu.VMEM((2 * QUAD, block_rows, HEAD), jnp.float32), gap],
    )
    attended, key_up = lax.optimization_barrier((attended, key_sums[0]))
    (handed,) = call(
        gate_kernel,
        "gate",
        [bf16(*gate_fwd.shape)],
        [VMEM] * (QUAD + 1),
        *[hand(attended[d], d) for d in range(QUAD)],
        gate_before,
    )
    key_sums = reduce_rest(key_parts, key_up, key_sums[1])
    key_pieces = swap(
        call(
            sum_kernel,
            "sum_key_parts",
            [bf16(QUAD, rows, 2 * HEAD)],
            [VMEM] * 3,
            *key_sums,
        )[0]
    )
    handed, query_pieces = lax.optimization_barrier((handed, query_pieces))
    (query_grad,) = call(
        query_grad_kernel,
        "query_grad",
        [bf16(*query_bwd.shape)],
        [VMEM],
        query_pieces,
    )
    key_grad, value_grad = call(
        key_grad_kernel,
        "key_grad",
        [bf16(*key_bwd.shape), bf16(*value_bwd.shape)],
        [VMEM],
        key_pieces,
    )
    return handed, query_grad, key_grad, value_grad


def solution(mesh):
    rows = P("pipe", "ctx", None)
    types = P("pipe", "ctx")
    return jax.shard_map(
        body,
        mesh=mesh,
        in_specs=(
            rows,
            rows,
            rows,
            rows,
            types,
            rows,
            rows,
            rows,
            rows,
            types,
            P("pipe", None, None),
            P("pipe", None),
            P("pipe", None),
        ),
        out_specs=(rows, rows, rows, rows),
        check_vma=False,
    )
```

```python
import functools
import math

import jax
import jax.numpy as jnp
from jax import lax
from jax.experimental import pallas as pl
from jax.experimental.pallas import tpu as pltpu
from jax.sharding import PartitionSpec as P

HEAD = 128
QUAD = 4
SCALE = HEAD ** (-0.5)
EXP2_SCALE = -SCALE / math.log(2.0)
GAIN_ROWS = 16
norm_eps = 1e-06

VMEM = pl.BlockSpec(memory_space=pltpu.VMEM)
HBM = pl.BlockSpec(memory_space=pltpu.HBM)
SMEM = pl.BlockSpec(memory_space=pltpu.SMEM)
MIB = 1024 * 1024

NN = (((1,), (0,)), ((), ()))
NT = (((1,), (1,)), ((), ()))
TN = (((0,), (0,)), ((), ()))


def dot(a, b, dims):
    return lax.dot_general(a, b, dims, preferred_element_type=jnp.float32)


def bf16(*shape):
    return jax.ShapeDtypeStruct(shape, jnp.bfloat16)


def place():
    index = lax.axis_index("ctx")
    return index // QUAD, index % QUAD


def columns(index, width):
    return pl.ds(pl.multiple_of(index * width, width), width)


def pack_keys(queries, key_ref, value_ref, types_ref, table_ref, *refs):
    query_refs, refs = refs[:queries], refs[queries:]
    pieces, (keys, types, table, typed, arrived, placed) = refs[:QUAD], refs[QUAD:]
    _, member = place()
    width = pieces[0].shape[1] - 2 * HEAD
    copies = [
        pltpu.make_async_copy(source, target, arrived.at[i])
        for i, (source, target) in enumerate(
            [(types_ref, types), (table_ref.at[0], table), (key_ref.at[0], keys)]
        )
    ]
    copies += [
        pltpu.make_async_copy(
            value_ref.at[0, :, columns(member ^ d, HEAD)],
            pieces[d].at[:, HEAD : 2 * HEAD],
            placed.at[d],
        )
        for d in range(QUAD)
    ]
    copies += [
        pltpu.make_async_copy(
            query_ref.at[0, :, columns(member ^ d, width)],
            pieces[d].at[:, 2 * HEAD :],
            placed.at[QUAD + d],
        )
        for query_ref in query_refs
        for d in range(QUAD)
    ]
    for copy in copies:
        copy.start()
    for copy in copies[:3]:
        copy.wait()
    onehot = (
        lax.broadcasted_iota(jnp.int32, (table.shape[0], types.shape[1]), 0) == types[...]
    ).astype(jnp.float32).astype(jnp.bfloat16)
    type_rows = dot(onehot, table[...], TN)
    typed[...] = (keys[...].astype(jnp.float32) + type_rows).astype(jnp.bfloat16)
    for d in range(QUAD):
        pieces[d][:, :HEAD] = typed[:, columns(member ^ d, HEAD)]
    for copy in copies[3:]:
        copy.wait()


def pack_queries(query_ref, grad_ref, *refs):
    pieces, placed = refs[:QUAD], refs[QUAD]
    _, member = place()
    width = query_ref.shape[2] // QUAD
    copies = [
        pltpu.make_async_copy(
            source.at[0, :, columns(member ^ d, width)],
            pieces[d].at[:, i * width : (i + 1) * width],
            placed.at[2 * d + i],
        )
        for d in reversed(range(QUAD))
        for i, source in enumerate([query_ref, grad_ref])
    ]
    for copy in copies:
        copy.start()
    for copy in copies:
        copy.wait()


def pack_gate(gate_ref, gain_ref, gate_out, sem):
    rows = gate_ref.shape[1]
    copy = pltpu.make_async_copy(gate_ref.at[0], gate_out.at[:rows, :], sem)
    copy.start()
    rest = gain_ref[...]
    parts = []
    for _ in range(3):
        part = rest.astype(jnp.bfloat16).astype(jnp.float32)
        parts.append(part)
        rest = rest - part
    parts.append(jnp.zeros((GAIN_ROWS - 3, rest.shape[1]), jnp.float32))
    gate_out[rows:, :] = jnp.concatenate(parts, axis=0).astype(jnp.bfloat16)
    copy.wait()


def stack_keys(*refs):
    pieces, (out, placed) = refs[:QUAD], refs[QUAD:]
    rows = pieces[0].shape[0]
    copies = [
        pltpu.make_async_copy(
            pieces[d].at[:, : 2 * HEAD], out.at[d * rows : (d + 1) * rows, :], placed.at[d]
        )
        for d in range(QUAD)
    ]
    for copy in copies:
        copy.start()
    for copy in copies:
        copy.wait()


def stretch_of(order_ref, quad_index, member, d, e):
    return order_ref[0, 2 * (quad_index * QUAD + (member ^ d)) + e]


def rows_at(index, count):
    return pl.ds(pl.multiple_of(index * count, count), count)


def in_sequence(order_ref, stacks, stretch_rows, keys, values):
    z, member = place()
    nz = len(stacks)
    for s, stack in enumerate(stacks):
        source = lax.rem(z - s + nz, nz)
        for d in range(QUAD):
            for e in range(2):
                rows = rows_at(stretch_of(order_ref, source, member, d, e), stretch_rows)
                lower = (2 * d + e) * stretch_rows
                keys[rows, :] = stack[lower : lower + stretch_rows, :HEAD]
                values[rows, :] = stack[lower : lower + stretch_rows, HEAD:]


def shrink_of(stretch, stretch_rows):
    pos = stretch * stretch_rows + lax.broadcasted_iota(jnp.int32, (stretch_rows, HEAD), 0)
    return lax.rsqrt((pos + 1).astype(jnp.float32))


def step_place(first, second, step, d, groups):
    blocks = first // groups + 1
    late = step >= blocks
    row = jnp.where(late, 2 * d + 1, 2 * d)
    stretch = jnp.where(late, second, first)
    block = jnp.where(late, step - blocks, step)
    return row, stretch, block


def sigmoid_of(raw, visible):
    part = pl.reciprocal(1.0 + jnp.exp2(raw * EXP2_SCALE), approx=True)
    return jnp.where(visible, part, 0.0)


def forward_kernel(nz, order_ref, *refs):
    queries, refs = refs[:QUAD], refs[QUAD:]
    stacks, refs = refs[:nz], refs[nz:]
    outs, refs = refs[:QUAD], refs[QUAD:]
    keys, values, stacked, total, gap = refs
    z, member = place()
    stretch_rows = queries[0].shape[0] // 2
    groups = outs[0].shape[1] // HEAD
    block_rows = groups * stretch_rows
    steps = keys.shape[0] // block_rows + 1
    in_sequence(order_ref, stacks, stretch_rows, keys, values)
    for d in range(QUAD):
        for e in range(2):
            for g in range(groups):
                stacked[2 * d + e, g * stretch_rows : (g + 1) * stretch_rows, :] = queries[d][
                    e * stretch_rows : (e + 1) * stretch_rows,
                    (2 + g) * HEAD : (3 + g) * HEAD,
                ]
    total[...] = jnp.zeros_like(total)
    gap[...] = lax.broadcasted_iota(jnp.int32, gap.shape, 1) - lax.rem(
        lax.broadcasted_iota(jnp.int32, gap.shape, 0), stretch_rows
    )

    def advance(step, _):
        for d in range(QUAD):
            row, stretch, block = step_place(
                stretch_of(order_ref, z, member, d, 0),
                stretch_of(order_ref, z, member, d, 1),
                step,
                d,
                groups,
            )
            rows = rows_at(block, block_rows)
            raw = dot(stacked[row], keys[rows, :], NT)
            visible = gap[...] <= stretch * stretch_rows - block * block_rows
            weights = (raw * SCALE * sigmoid_of(raw, visible)).astype(jnp.bfloat16)
            total[row] += dot(weights, values[rows, :], NN)
        return 0

    lax.fori_loop(0, steps, advance, 0)
    for d in range(QUAD):
        for e in range(2):
            shrink = shrink_of(stretch_of(order_ref, z, member, d, e), stretch_rows)
            for g in range(groups):
                outs[d][e * stretch_rows : (e + 1) * stretch_rows, g * HEAD : (g + 1) * HEAD] = (
                    total[2 * d + e, g * stretch_rows : (g + 1) * stretch_rows, :] * shrink
                ).astype(jnp.bfloat16)


def backward_kernel(nz, order_ref, *refs):
    queries, refs = refs[:QUAD], refs[QUAD:]
    stacks, refs = refs[:nz], refs[nz:]
    query_outs, refs = refs[:QUAD], refs[QUAD:]
    key_outs, refs = refs[:nz], refs[nz:]
    keys, values, keys_t, stacked, grads, total_t, key_total, value_total, gap = refs
    z, member = place()
    stretch_rows = queries[0].shape[0] // 2
    groups = queries[0].shape[1] // (2 * HEAD)
    block_rows = groups * stretch_rows
    blocks = keys.shape[0] // block_rows
    steps = blocks + 1
    in_sequence(order_ref, stacks, stretch_rows, keys, values)
    for block in range(blocks):
        lower = block * block_rows
        keys_t[block] = keys[lower : lower + block_rows, :].T
    offset = groups * HEAD
    for d in range(QUAD):
        for e in range(2):
            shrink = shrink_of(stretch_of(order_ref, z, member, d, e), stretch_rows)
            rows = slice(e * stretch_rows, (e + 1) * stretch_rows)
            for g in range(groups):
                into = slice(g * stretch_rows, (g + 1) * stretch_rows)
                stacked[2 * d + e, into, :] = queries[d][rows, g * HEAD : (g + 1) * HEAD]
                grads[2 * d + e, into, :] = (
                    queries[d][rows, offset + g * HEAD : offset + (g + 1) * HEAD].astype(
                        jnp.float32
                    )
                    * shrink
                ).astype(jnp.bfloat16)
    total_t[...] = jnp.zeros_like(total_t)
    key_total[...] = jnp.zeros_like(key_total)
    value_total[...] = jnp.zeros_like(value_total)
    gap[...] = lax.broadcasted_iota(jnp.int32, gap.shape, 0) - lax.rem(
        lax.broadcasted_iota(jnp.int32, gap.shape, 1), stretch_rows
    )

    def advance(step, _):
        for d in range(QUAD):
            row, stretch, block = step_place(
                stretch_of(order_ref, z, member, d, 0),
                stretch_of(order_ref, z, member, d, 1),
                step,
                d,
                groups,
            )
            rows = rows_at(block, block_rows)
            raw = dot(keys[rows, :], stacked[row], NT)
            weight_grad = dot(values[rows, :], grads[row], NT)
            visible = gap[...] <= stretch * stretch_rows - block * block_rows
            part = sigmoid_of(raw, visible)
            weights = raw * SCALE * part
            score_grad = (weight_grad * (part + weights * (1.0 - part))).astype(jnp.bfloat16)
            weights = weights.astype(jnp.bfloat16)
            total_t[row] += dot(keys_t[block], score_grad, NN)
            key_total[rows, :] += dot(score_grad, stacked[row], NN)
            value_total[rows, :] += dot(weights, grads[row], NN)
        return 0

    lax.fori_loop(0, steps, advance, 0)
    for d in range(QUAD):
        for e in range(2):
            query_grad = (total_t[2 * d + e].T * SCALE).astype(jnp.bfloat16)
            for g in range(groups):
                query_outs[d][
                    e * stretch_rows : (e + 1) * stretch_rows, g * HEAD : (g + 1) * HEAD
                ] = query_grad[g * stretch_rows : (g + 1) * stretch_rows, :]
    for s in range(nz):
        target = lax.rem(z + s, nz)
        for d in range(QUAD):
            for e in range(2):
                rows = rows_at(stretch_of(order_ref, target, member, d, e), stretch_rows)
                lower = (2 * d + e) * stretch_rows
                key_outs[s][lower : lower + stretch_rows, :HEAD] = (
                    key_total[rows, :] * SCALE
                ).astype(jnp.bfloat16)
                key_outs[s][lower : lower + stretch_rows, HEAD:] = value_total[rows, :].astype(
                    jnp.bfloat16
                )


def sum_kernel(*refs):
    parts, pieces = refs[:3], refs[3:]
    rows = pieces[0].shape[0]
    for d in range(QUAD):
        lower = d * rows
        pieces[d][...] = sum(
            part[lower : lower + rows, :].astype(jnp.float32) for part in parts
        ).astype(jnp.bfloat16)


def key_grad_kernel(*refs):
    pieces, (key_out, value_out) = refs[:QUAD], refs[QUAD:]
    _, member = place()
    for d in range(QUAD):
        head = columns(member ^ d, HEAD)
        key_out[0, :, head] = pieces[d][:, :HEAD]
        value_out[0, :, head] = pieces[d][:, HEAD:]


def query_grad_kernel(*refs):
    pieces, out = refs[:QUAD], refs[QUAD]
    _, member = place()
    for d in range(QUAD):
        out[0, :, columns(member ^ d, pieces[d].shape[1])] = pieces[d][...]


def gate_kernel(*refs):
    pieces, (gate_ref, out) = refs[:QUAD], refs[QUAD:]
    _, member = place()
    rows = out.shape[1]
    attended = [piece[...].astype(jnp.float32) for piece in pieces]
    square = sum(jnp.sum(part * part, axis=1, keepdims=True) for part in attended)
    factor = lax.rsqrt(square / out.shape[2] + norm_eps)
    for d in range(QUAD):
        head = columns(member ^ d, pieces[d].shape[1])
        gain = sum(gate_ref[rows : rows + GAIN_ROWS, head].astype(jnp.float32)[i : i + 1] for i in range(3))
        out[0, :, head] = (
            attended[d] * factor * gain * gate_ref[:rows, head].astype(jnp.float32)
        ).astype(jnp.bfloat16)


def call(kernel, name, out_shape, specs, *args, scratch=(), flops=0, transcendentals=0, vmem=40):
    size = sum(a.size * a.dtype.itemsize for a in args)
    size += sum(math.prod(o.shape) * o.dtype.itemsize for o in out_shape)
    return pl.pallas_call(
        kernel,
        name=name,
        out_shape=out_shape,
        in_specs=specs,
        out_specs=[VMEM] * len(out_shape),
        scratch_shapes=list(scratch),
        compiler_params=pltpu.CompilerParams(vmem_limit_bytes=vmem * MIB),
        cost_estimate=pl.CostEstimate(
            flops=flops, bytes_accessed=size, transcendentals=transcendentals
        ),
    )(*args)


def body(
    query_fwd,
    key_fwd,
    value_fwd,
    gate_fwd,
    types_fwd,
    query_bwd,
    key_bwd,
    value_bwd,
    grad_out,
    types_bwd,
    type_key,
    norm_gain,
    stretch_order,
):
    devices = lax.axis_size("ctx")
    nz = devices // QUAD
    rows = query_fwd.shape[1]
    total_rows = rows * devices
    width = query_fwd.shape[2] // QUAD
    groups = width // HEAD
    stretch_rows = rows // 2
    block_rows = groups * stretch_rows
    steps = total_rows // block_rows + 1
    pairs = steps * QUAD * block_rows * block_rows

    def swap(pieces):
        return [pieces[0]] + [
            lax.ppermute(pieces[d], "ctx", [(i, i ^ d) for i in range(devices)])
            for d in range(1, QUAD)
        ]

    def turn(block, s):
        return lax.ppermute(
            block, "ctx", [(i, (i + s * QUAD) % devices) for i in range(devices)]
        )

    def hand(block, d):
        sections = lax.axis_size("pipe")
        route = [
            (i * sections + p, (i ^ d) * sections + (p + 1) % sections)
            for i in range(devices)
            for p in range(sections)
        ]
        return lax.ppermute(block, ("ctx", "pipe"), route)

    def pack(key, value, types, name, *queries):
        return call(
            functools.partial(pack_keys, len(queries)),
            name,
            [bf16(rows, 2 * HEAD + len(queries) * width)] * QUAD,
            [HBM] * (4 + len(queries)),
            key,
            value,
            types,
            type_key,
            *queries,
            scratch=[
                pltpu.VMEM(key.shape[1:], jnp.bfloat16),
                pltpu.VMEM(types.shape, jnp.int32),
                pltpu.VMEM(type_key.shape[1:], jnp.bfloat16),
                pltpu.VMEM(key.shape[1:], jnp.bfloat16),
                pltpu.SemaphoreType.DMA((3,)),
                pltpu.SemaphoreType.DMA((2 * QUAD,)),
            ],
            vmem=60,
        )

    ahead = nz // 2

    def ring_up(block):
        return turn(block, 1)

    def ring_down(block):
        return turn(block, nz - 1)

    def gather_first(stack):
        return [stack, ring_up(stack)], [ring_down(stack)]

    def gather_rest(up, down):
        up, down = lax.optimization_barrier((up, down))
        while len(up) <= ahead:
            up = up + [ring_up(up[-1])]
        while len(up) + len(down) < nz:
            down = down + [ring_down(down[-1])]
        return up + down[::-1]

    def reduce_first(parts):
        return ring_up(parts[ahead]), ring_down(parts[ahead + 1])

    def add(a, b):
        return (a.astype(jnp.float32) + b.astype(jnp.float32)).astype(jnp.bfloat16)

    def reduce_rest(parts, up, down):
        for s in range(ahead - 1, 0, -1):
            up = ring_up(add(up, parts[s]))
        for s in range(ahead + 2, nz):
            down = ring_down(add(down, parts[s]))
        return parts[0], up, down

    back_pieces = swap(pack(key_bwd, value_bwd, types_bwd, "pack_keys_bwd"))
    packed = call(
        pack_queries,
        "pack_queries",
        [bf16(rows, 2 * width)] * QUAD,
        [HBM] * 2,
        query_bwd,
        grad_out,
        scratch=[pltpu.SemaphoreType.DMA((2 * QUAD,))],
        vmem=60,
    )
    pieces = pack(key_fwd, value_fwd, types_fwd, "pack_fwd", query_fwd)
    back_pieces, packed, pieces = lax.optimization_barrier((back_pieces, packed, pieces))
    back_queries = swap(packed)
    back_stacks = gather_rest(*gather_first(jnp.concatenate(back_pieces, axis=0)))
    pieces = [hand(pieces[d], d) for d in range(QUAD)]
    order_before = hand(stretch_order, 0)
    (stack,) = call(
        stack_keys,
        "stack_keys",
        [bf16(QUAD * rows, 2 * HEAD)],
        [HBM] * QUAD,
        *pieces,
        scratch=[pltpu.SemaphoreType.DMA((QUAD,))],
    )
    (gate_before,) = call(
        pack_gate,
        "pack_gate",
        [bf16(rows + GAIN_ROWS, QUAD * width)],
        [HBM, VMEM],
        gate_fwd,
        norm_gain,
        scratch=[pltpu.SemaphoreType.DMA],
        vmem=60,
    )
    stack, gate_before, order_before, back_stacks, back_queries = lax.optimization_barrier(
        (stack, gate_before, order_before, back_stacks, back_queries)
    )
    stacks = [stack] + [turn(stack, s) for s in range(1, nz)]
    gate_before = hand(gate_before, 0)

    sequence = [pltpu.VMEM((total_rows, HEAD), jnp.bfloat16)] * 2
    stacked = pltpu.VMEM((2 * QUAD, block_rows, HEAD), jnp.bfloat16)
    gap = pltpu.VMEM((block_rows, block_rows), jnp.int32)
    outs = call(
        functools.partial(backward_kernel, nz),
        "backward",
        [bf16(rows, width)] * QUAD + [bf16(QUAD * rows, 2 * HEAD)] * nz,
        [SMEM] + [VMEM] * (QUAD + nz),
        stretch_order,
        *back_queries,
        *back_stacks,
        scratch=sequence
        + [
            pltpu.VMEM((total_rows // block_rows, HEAD, block_rows), jnp.bfloat16),
            stacked,
            stacked,
            pltpu.VMEM((2 * QUAD, HEAD, block_rows), jnp.float32),
            pltpu.VMEM((total_rows, HEAD), jnp.float32),
            pltpu.VMEM((total_rows, HEAD), jnp.float32),
            gap,
        ],
        flops=10 * pairs * HEAD,
        transcendentals=2 * pairs,
    )
    query_pieces, key_parts = outs[:QUAD], outs[QUAD:]
    query_pieces, key_parts, gate_before = lax.optimization_barrier(
        (query_pieces, key_parts, gate_before)
    )
    query_pieces = swap(query_pieces)
    key_parts, stacks, query_pieces = lax.optimization_barrier((key_parts, stacks, query_pieces))
    key_sums = reduce_first(key_parts)
    attended = call(
        functools.partial(forward_kernel, nz),
        "forward",
        [bf16(rows, width)] * QUAD,
        [SMEM] + [VMEM] * (QUAD + nz),
        order_before,
        *pieces,
        *stacks,
        scratch=sequence
        + [stacked, pltpu.VMEM((2 * QUAD, block_rows, HEAD), jnp.float32), gap],
    )
    attended, key_up = lax.optimization_barrier((attended, key_sums[0]))
    (handed,) = call(
        gate_kernel,
        "gate",
        [bf16(*gate_fwd.shape)],
        [VMEM] * (QUAD + 1),
        *swap(attended),
        gate_before,
    )
    key_sums = reduce_rest(key_parts, key_up, key_sums[1])
    key_pieces = swap(
        call(
            sum_kernel,
            "sum_key_parts",
            [bf16(rows, 2 * HEAD)] * QUAD,
            [VMEM] * 3,
            *key_sums,
        )
    )
    (query_grad,) = call(
        query_grad_kernel,
        "query_grad",
        [bf16(*query_bwd.shape)],
        [VMEM] * QUAD,
        *query_pieces,
    )
    key_grad, value_grad = call(
        key_grad_kernel,
        "key_grad",
        [bf16(*key_bwd.shape), bf16(*value_bwd.shape)],
        [VMEM] * QUAD,
        *key_pieces,
    )
    return handed, query_grad, key_grad, value_grad


def solution(mesh):
    rows = P("pipe", "ctx", None)
    types = P("pipe", "ctx")
    return jax.shard_map(
        body,
        mesh=mesh,
        in_specs=(
            rows,
            rows,
            rows,
            rows,
            types,
            rows,
            rows,
            rows,
            rows,
            types,
            P("pipe", None, None),
            P("pipe", None),
            P("pipe", None),
        ),
        out_specs=(rows, rows, rows, rows),
        check_vma=False,
    )
```

```python
import functools
import math

import jax
import jax.numpy as jnp
from jax import lax
from jax.experimental import pallas as pl
from jax.experimental.pallas import tpu as pltpu
from jax.sharding import PartitionSpec as P

HEAD = 128
QUAD = 4
SCALE = HEAD ** (-0.5)
EXP2_SCALE = -SCALE / math.log(2.0)
GAIN_ROWS = 16
norm_eps = 1e-06

VMEM = pl.BlockSpec(memory_space=pltpu.VMEM)
HBM = pl.BlockSpec(memory_space=pltpu.HBM)
SMEM = pl.BlockSpec(memory_space=pltpu.SMEM)
MIB = 1024 * 1024

NN = (((1,), (0,)), ((), ()))
NT = (((1,), (1,)), ((), ()))
TN = (((0,), (0,)), ((), ()))


def dot(a, b, dims):
    return lax.dot_general(a, b, dims, preferred_element_type=jnp.float32)


def bf16(*shape):
    return jax.ShapeDtypeStruct(shape, jnp.bfloat16)


def place():
    index = lax.axis_index("ctx")
    return index // QUAD, index % QUAD


def columns(index, width):
    return pl.ds(pl.multiple_of(index * width, width), width)


def pack_keys(
    back_key, back_value, back_types, key, value, types, table_ref, *refs
):
    pieces, (keys, event_types, table, typed, arrived, placed) = refs[:QUAD], refs[QUAD:]
    _, member = place()
    copies = [pltpu.make_async_copy(table_ref.at[0], table, arrived.at[4])]
    for i, (key_ref, types_ref) in enumerate([(back_key, back_types), (key, types)]):
        copies += [
            pltpu.make_async_copy(types_ref, event_types.at[i], arrived.at[2 * i]),
            pltpu.make_async_copy(key_ref.at[0], keys.at[i], arrived.at[2 * i + 1]),
        ]
    placements = [
        pltpu.make_async_copy(
            value_ref.at[0, :, columns(member ^ d, HEAD)],
            pieces[d].at[:, (2 * i + 1) * HEAD : (2 * i + 2) * HEAD],
            placed.at[i * QUAD + d],
        )
        for i, value_ref in enumerate([back_value, value])
        for d in range(QUAD)
    ]
    for copy in copies + placements:
        copy.start()
    for copy in copies:
        copy.wait()
    for i in range(2):
        onehot = (
            lax.broadcasted_iota(jnp.int32, (table.shape[0], types.shape[1]), 0) == event_types[i]
        ).astype(jnp.float32).astype(jnp.bfloat16)
        type_rows = dot(onehot, table[...], TN)
        typed[...] = (keys[i].astype(jnp.float32) + type_rows).astype(jnp.bfloat16)
        for d in range(QUAD):
            pieces[d][:, 2 * i * HEAD : (2 * i + 1) * HEAD] = typed[:, columns(member ^ d, HEAD)]
    for copy in placements:
        copy.wait()


def stack_keys(*refs):
    pieces, (back, front, placed) = refs[:QUAD], refs[QUAD:]
    rows = pieces[0].shape[0]
    copies = [
        pltpu.make_async_copy(
            pieces[d].at[:, 2 * i * HEAD : (2 * i + 2) * HEAD],
            out.at[d * rows : (d + 1) * rows, :],
            placed.at[i * QUAD + d],
        )
        for i, out in enumerate([back, front])
        for d in range(QUAD)
    ]
    for copy in copies:
        copy.start()
    for copy in copies:
        copy.wait()


def pack_queries(query_ref, grad_ref, forward_ref, gate_ref, gain_ref, *refs):
    pieces, (gate_out, placed) = refs[:QUAD], refs[QUAD:]
    _, member = place()
    width = query_ref.shape[2] // QUAD
    rows = gate_ref.shape[1]
    copies = [
        pltpu.make_async_copy(
            source.at[0, :, columns(member ^ d, width)],
            pieces[d].at[:, i * width : (i + 1) * width],
            placed.at[3 * d + i],
        )
        for d in reversed(range(QUAD))
        for i, source in enumerate([query_ref, grad_ref, forward_ref])
    ]
    copies.append(
        pltpu.make_async_copy(gate_ref.at[0], gate_out.at[:rows, :], placed.at[3 * QUAD])
    )
    for copy in copies:
        copy.start()
    rest = gain_ref[...]
    parts = []
    for _ in range(3):
        part = rest.astype(jnp.bfloat16).astype(jnp.float32)
        parts.append(part)
        rest = rest - part
    parts.append(jnp.zeros((GAIN_ROWS - 3, rest.shape[1]), jnp.float32))
    gate_out[rows:, :] = jnp.concatenate(parts, axis=0).astype(jnp.bfloat16)
    for copy in copies:
        copy.wait()


def stretch_of(order_ref, quad_index, member, d, e):
    return order_ref[0, 2 * (quad_index * QUAD + (member ^ d)) + e]


def rows_at(index, count):
    return pl.ds(pl.multiple_of(index * count, count), count)


def in_sequence(order_ref, stacks, stretch_rows, keys, values):
    z, member = place()
    nz = len(stacks)
    for s, stack in enumerate(stacks):
        source = lax.rem(z - s + nz, nz)
        for d in range(QUAD):
            for e in range(2):
                rows = rows_at(stretch_of(order_ref, source, member, d, e), stretch_rows)
                lower = (2 * d + e) * stretch_rows
                keys[rows, :] = stack[lower : lower + stretch_rows, :HEAD]
                values[rows, :] = stack[lower : lower + stretch_rows, HEAD:]


def shrink_of(stretch, stretch_rows):
    pos = stretch * stretch_rows + lax.broadcasted_iota(jnp.int32, (stretch_rows, HEAD), 0)
    return lax.rsqrt((pos + 1).astype(jnp.float32))


def step_place(first, second, step, d, groups):
    blocks = first // groups + 1
    late = step >= blocks
    row = jnp.where(late, 2 * d + 1, 2 * d)
    stretch = jnp.where(late, second, first)
    block = jnp.where(late, step - blocks, step)
    return row, stretch, block


def sigmoid_of(raw, visible):
    part = pl.reciprocal(1.0 + jnp.exp2(raw * EXP2_SCALE), approx=True)
    return jnp.where(visible, part, 0.0)


def forward_kernel(nz, order_ref, *refs):
    queries, refs = refs[:QUAD], refs[QUAD:]
    stacks, refs = refs[:nz], refs[nz:]
    outs, refs = refs[:QUAD], refs[QUAD:]
    keys, values, stacked, total, gap = refs
    z, member = place()
    stretch_rows = queries[0].shape[0] // 2
    groups = outs[0].shape[1] // HEAD
    block_rows = groups * stretch_rows
    steps = keys.shape[0] // block_rows + 1
    in_sequence(order_ref, stacks, stretch_rows, keys, values)
    offset = 2 * groups * HEAD
    for d in range(QUAD):
        for e in range(2):
            for g in range(groups):
                stacked[2 * d + e, g * stretch_rows : (g + 1) * stretch_rows, :] = queries[d][
                    e * stretch_rows : (e + 1) * stretch_rows,
                    offset + g * HEAD : offset + (g + 1) * HEAD,
                ]
    total[...] = jnp.zeros_like(total)
    gap[...] = lax.broadcasted_iota(jnp.int32, gap.shape, 1) - lax.rem(
        lax.broadcasted_iota(jnp.int32, gap.shape, 0), stretch_rows
    )

    def advance(step, _):
        for d in range(QUAD):
            row, stretch, block = step_place(
                stretch_of(order_ref, z, member, d, 0),
                stretch_of(order_ref, z, member, d, 1),
                step,
                d,
                groups,
            )
            rows = rows_at(block, block_rows)
            raw = dot(stacked[row], keys[rows, :], NT)
            visible = gap[...] <= stretch * stretch_rows - block * block_rows
            weights = (raw * SCALE * sigmoid_of(raw, visible)).astype(jnp.bfloat16)
            total[row] += dot(weights, values[rows, :], NN)
        return 0

    lax.fori_loop(0, steps, advance, 0)
    for d in range(QUAD):
        for e in range(2):
            shrink = shrink_of(stretch_of(order_ref, z, member, d, e), stretch_rows)
            for g in range(groups):
                outs[d][e * stretch_rows : (e + 1) * stretch_rows, g * HEAD : (g + 1) * HEAD] = (
                    total[2 * d + e, g * stretch_rows : (g + 1) * stretch_rows, :] * shrink
                ).astype(jnp.bfloat16)


def backward_kernel(nz, order_ref, *refs):
    queries, refs = refs[:QUAD], refs[QUAD:]
    stacks, refs = refs[:nz], refs[nz:]
    query_outs, refs = refs[:QUAD], refs[QUAD:]
    key_outs, refs = refs[:nz], refs[nz:]
    keys, values, keys_t, stacked, grads, total_t, key_total, value_total, gap = refs
    z, member = place()
    stretch_rows = queries[0].shape[0] // 2
    groups = query_outs[0].shape[1] // HEAD
    block_rows = groups * stretch_rows
    blocks = keys.shape[0] // block_rows
    steps = blocks + 1
    in_sequence(order_ref, stacks, stretch_rows, keys, values)
    for block in range(blocks):
        lower = block * block_rows
        keys_t[block] = keys[lower : lower + block_rows, :].T
    offset = groups * HEAD
    for d in range(QUAD):
        for e in range(2):
            shrink = shrink_of(stretch_of(order_ref, z, member, d, e), stretch_rows)
            rows = slice(e * stretch_rows, (e + 1) * stretch_rows)
            for g in range(groups):
                into = slice(g * stretch_rows, (g + 1) * stretch_rows)
                stacked[2 * d + e, into, :] = queries[d][rows, g * HEAD : (g + 1) * HEAD]
                grads[2 * d + e, into, :] = (
                    queries[d][rows, offset + g * HEAD : offset + (g + 1) * HEAD].astype(
                        jnp.float32
                    )
                    * shrink
                ).astype(jnp.bfloat16)
    total_t[...] = jnp.zeros_like(total_t)
    key_total[...] = jnp.zeros_like(key_total)
    value_total[...] = jnp.zeros_like(value_total)
    gap[...] = lax.broadcasted_iota(jnp.int32, gap.shape, 0) - lax.rem(
        lax.broadcasted_iota(jnp.int32, gap.shape, 1), stretch_rows
    )

    def advance(step, _):
        for d in range(QUAD):
            row, stretch, block = step_place(
                stretch_of(order_ref, z, member, d, 0),
                stretch_of(order_ref, z, member, d, 1),
                step,
                d,
                groups,
            )
            rows = rows_at(block, block_rows)
            raw = dot(keys[rows, :], stacked[row], NT)
            weight_grad = dot(values[rows, :], grads[row], NT)
            visible = gap[...] <= stretch * stretch_rows - block * block_rows
            part = sigmoid_of(raw, visible)
            weights = raw * SCALE * part
            score_grad = (weight_grad * (part + weights * (1.0 - part))).astype(jnp.bfloat16)
            weights = weights.astype(jnp.bfloat16)
            total_t[row] += dot(keys_t[block], score_grad, NN)
            key_total[rows, :] += dot(score_grad, stacked[row], NN)
            value_total[rows, :] += dot(weights, grads[row], NN)
        return 0

    lax.fori_loop(0, steps, advance, 0)
    for d in range(QUAD):
        for e in range(2):
            query_grad = (total_t[2 * d + e].T * SCALE).astype(jnp.bfloat16)
            for g in range(groups):
                query_outs[d][
                    e * stretch_rows : (e + 1) * stretch_rows, g * HEAD : (g + 1) * HEAD
                ] = query_grad[g * stretch_rows : (g + 1) * stretch_rows, :]
    for s in range(nz):
        target = lax.rem(z + s, nz)
        for d in range(QUAD):
            for e in range(2):
                rows = rows_at(stretch_of(order_ref, target, member, d, e), stretch_rows)
                lower = (2 * d + e) * stretch_rows
                key_outs[s][lower : lower + stretch_rows, :HEAD] = (
                    key_total[rows, :] * SCALE
                ).astype(jnp.bfloat16)
                key_outs[s][lower : lower + stretch_rows, HEAD:] = value_total[rows, :].astype(
                    jnp.bfloat16
                )


def sum_kernel(*refs):
    parts, pieces = refs[:3], refs[3:]
    rows = pieces[0].shape[0]
    for d in range(QUAD):
        lower = d * rows
        pieces[d][...] = sum(
            part[lower : lower + rows, :].astype(jnp.float32) for part in parts
        ).astype(jnp.bfloat16)


def key_grad_kernel(*refs):
    pieces, (key_out, value_out) = refs[:QUAD], refs[QUAD:]
    _, member = place()
    for d in range(QUAD):
        head = columns(member ^ d, HEAD)
        key_out[0, :, head] = pieces[d][:, :HEAD]
        value_out[0, :, head] = pieces[d][:, HEAD:]


def query_grad_kernel(*refs):
    pieces, out = refs[:QUAD], refs[QUAD]
    _, member = place()
    for d in range(QUAD):
        out[0, :, columns(member ^ d, pieces[d].shape[1])] = pieces[d][...]


def gate_kernel(*refs):
    pieces, (gate_ref, out) = refs[:QUAD], refs[QUAD:]
    _, member = place()
    rows = out.shape[1]
    attended = [piece[...].astype(jnp.float32) for piece in pieces]
    square = sum(jnp.sum(part * part, axis=1, keepdims=True) for part in attended)
    factor = lax.rsqrt(square / out.shape[2] + norm_eps)
    for d in range(QUAD):
        head = columns(member ^ d, pieces[d].shape[1])
        gain = sum(gate_ref[rows : rows + GAIN_ROWS, head].astype(jnp.float32)[i : i + 1] for i in range(3))
        out[0, :, head] = (
            attended[d] * factor * gain * gate_ref[:rows, head].astype(jnp.float32)
        ).astype(jnp.bfloat16)


def call(kernel, name, out_shape, specs, *args, scratch=(), flops=0, transcendentals=0, vmem=40):
    size = sum(a.size * a.dtype.itemsize for a in args)
    size += sum(math.prod(o.shape) * o.dtype.itemsize for o in out_shape)
    return pl.pallas_call(
        kernel,
        name=name,
        out_shape=out_shape,
        in_specs=specs,
        out_specs=[VMEM] * len(out_shape),
        scratch_shapes=list(scratch),
        compiler_params=pltpu.CompilerParams(vmem_limit_bytes=vmem * MIB),
        cost_estimate=pl.CostEstimate(
            flops=flops, bytes_accessed=size, transcendentals=transcendentals
        ),
    )(*args)


def body(
    query_fwd,
    key_fwd,
    value_fwd,
    gate_fwd,
    types_fwd,
    query_bwd,
    key_bwd,
    value_bwd,
    grad_out,
    types_bwd,
    type_key,
    norm_gain,
    stretch_order,
):
    devices = lax.axis_size("ctx")
    nz = devices // QUAD
    rows = query_fwd.shape[1]
    total_rows = rows * devices
    width = query_fwd.shape[2] // QUAD
    groups = width // HEAD
    stretch_rows = rows // 2
    block_rows = groups * stretch_rows
    steps = total_rows // block_rows + 1
    pairs = steps * QUAD * block_rows * block_rows

    def swap(pieces):
        return [pieces[0]] + [
            lax.ppermute(pieces[d], "ctx", [(i, i ^ d) for i in range(devices)])
            for d in range(1, QUAD)
        ]

    def turn(block, s):
        return lax.ppermute(
            block, "ctx", [(i, (i + s * QUAD) % devices) for i in range(devices)]
        )

    def hand(block, d):
        sections = lax.axis_size("pipe")
        route = [
            (i * sections + p, (i ^ d) * sections + (p + 1) % sections)
            for i in range(devices)
            for p in range(sections)
        ]
        return lax.ppermute(block, ("ctx", "pipe"), route)

    ahead = nz // 2

    def ring_up(block):
        return turn(block, 1)

    def ring_down(block):
        return turn(block, nz - 1)

    def gather_first(stack):
        return [stack, ring_up(stack)], [ring_down(stack)]

    def gather_rest(up, down):
        up, down = lax.optimization_barrier((up, down))
        while len(up) <= ahead:
            up = up + [ring_up(up[-1])]
        while len(up) + len(down) < nz:
            down = down + [ring_down(down[-1])]
        return up + down[::-1]

    def reduce_first(parts):
        return ring_up(parts[ahead]), ring_down(parts[ahead + 1])

    def add(a, b):
        return (a.astype(jnp.float32) + b.astype(jnp.float32)).astype(jnp.bfloat16)

    def reduce_rest(parts, up, down):
        for s in range(ahead - 1, 0, -1):
            up = ring_up(add(up, parts[s]))
        for s in range(ahead + 2, nz):
            down = ring_down(add(down, parts[s]))
        return parts[0], up, down

    pieces = swap(
        call(
            pack_keys,
            "pack_keys",
            [bf16(rows, 4 * HEAD)] * QUAD,
            [HBM] * 7,
            key_bwd,
            value_bwd,
            types_bwd,
            key_fwd,
            value_fwd,
            types_fwd,
            type_key,
            scratch=[
                pltpu.VMEM((2, *key_fwd.shape[1:]), jnp.bfloat16),
                pltpu.VMEM((2, *types_fwd.shape), jnp.int32),
                pltpu.VMEM(type_key.shape[1:], jnp.bfloat16),
                pltpu.VMEM(key_fwd.shape[1:], jnp.bfloat16),
                pltpu.SemaphoreType.DMA((5,)),
                pltpu.SemaphoreType.DMA((2 * QUAD,)),
            ],
            vmem=60,
        )
    )
    packed = call(
        pack_queries,
        "pack_queries",
        [bf16(rows, 3 * width)] * QUAD + [bf16(rows + GAIN_ROWS, QUAD * width)],
        [HBM] * 4 + [VMEM],
        query_bwd,
        grad_out,
        query_fwd,
        gate_fwd,
        norm_gain,
        scratch=[pltpu.SemaphoreType.DMA((3 * QUAD + 1,))],
        vmem=60,
    )
    pieces, packed = lax.optimization_barrier((pieces, packed))
    back_stack, stack = call(
        stack_keys,
        "stack_keys",
        [bf16(QUAD * rows, 2 * HEAD)] * 2,
        [HBM] * QUAD,
        *pieces,
        scratch=[pltpu.SemaphoreType.DMA((2 * QUAD,))],
    )
    queries = swap(packed[:QUAD])
    up, down = gather_first(back_stack)
    up, down, gate_before = lax.optimization_barrier((up, down, packed[QUAD]))
    back_stacks = gather_rest(up, down)
    gate_before = hand(gate_before, 0)
    stack, back_stacks = lax.optimization_barrier((stack, back_stacks))
    stacks = [stack] + [turn(stack, s) for s in range(1, nz)]

    sequence = [pltpu.VMEM((total_rows, HEAD), jnp.bfloat16)] * 2
    stacked = pltpu.VMEM((2 * QUAD, block_rows, HEAD), jnp.bfloat16)
    gap = pltpu.VMEM((block_rows, block_rows), jnp.int32)
    outs = call(
        functools.partial(backward_kernel, nz),
        "backward",
        [bf16(rows, width)] * QUAD + [bf16(QUAD * rows, 2 * HEAD)] * nz,
        [SMEM] + [VMEM] * (QUAD + nz),
        stretch_order,
        *queries,
        *back_stacks,
        scratch=sequence
        + [
            pltpu.VMEM((total_rows // block_rows, HEAD, block_rows), jnp.bfloat16),
            stacked,
            stacked,
            pltpu.VMEM((2 * QUAD, HEAD, block_rows), jnp.float32),
            pltpu.VMEM((total_rows, HEAD), jnp.float32),
            pltpu.VMEM((total_rows, HEAD), jnp.float32),
            gap,
        ],
        flops=10 * pairs * HEAD,
        transcendentals=2 * pairs,
    )
    query_pieces, key_parts = outs[:QUAD], outs[QUAD:]
    query_pieces, key_parts, gate_before = lax.optimization_barrier(
        (query_pieces, key_parts, gate_before)
    )
    key_sums = reduce_first(key_parts)
    query_pieces = swap(query_pieces)
    query_pieces, stacks = lax.optimization_barrier((query_pieces, stacks))
    attended = call(
        functools.partial(forward_kernel, nz),
        "forward",
        [bf16(rows, width)] * QUAD,
        [SMEM] + [VMEM] * (QUAD + nz),
        stretch_order,
        *queries,
        *stacks,
        scratch=sequence
        + [stacked, pltpu.VMEM((2 * QUAD, block_rows, HEAD), jnp.float32), gap],
    )
    attended, key_up = lax.optimization_barrier((attended, key_sums[0]))
    (handed,) = call(
        gate_kernel,
        "gate",
        [bf16(*gate_fwd.shape)],
        [VMEM] * (QUAD + 1),
        *[hand(attended[d], d) for d in range(QUAD)],
        gate_before,
    )
    key_sums = reduce_rest(key_parts, key_up, key_sums[1])
    key_pieces = swap(
        call(
            sum_kernel,
            "sum_key_parts",
            [bf16(rows, 2 * HEAD)] * QUAD,
            [VMEM] * 3,
            *key_sums,
        )
    )
    (query_grad,) = call(
        query_grad_kernel,
        "query_grad",
        [bf16(*query_bwd.shape)],
        [VMEM] * QUAD,
        *query_pieces,
    )
    key_grad, value_grad = call(
        key_grad_kernel,
        "key_grad",
        [bf16(*key_bwd.shape), bf16(*value_bwd.shape)],
        [VMEM] * QUAD,
        *key_pieces,
    )
    return handed, query_grad, key_grad, value_grad


def solution(mesh):
    rows = P("pipe", "ctx", None)
    types = P("pipe", "ctx")
    return jax.shard_map(
        body,
        mesh=mesh,
        in_specs=(
            rows,
            rows,
            rows,
            rows,
            types,
            rows,
            rows,
            rows,
            rows,
            types,
            P("pipe", None, None),
            P("pipe", None),
            P("pipe", None),
        ),
        out_specs=(rows, rows, rows, rows),
        check_vma=False,
    )
```

```python
import functools
import math

import jax
import jax.numpy as jnp
from jax import lax
from jax.experimental import pallas as pl
from jax.experimental.pallas import tpu as pltpu
from jax.sharding import PartitionSpec as P

HEAD = 128
QUAD = 4
SCALE = HEAD ** (-0.5)
EXP2_SCALE = -SCALE / math.log(2.0)
GAIN_ROWS = 16
norm_eps = 1e-06

VMEM = pl.BlockSpec(memory_space=pltpu.VMEM)
HBM = pl.BlockSpec(memory_space=pltpu.HBM)
SMEM = pl.BlockSpec(memory_space=pltpu.SMEM)
MIB = 1024 * 1024

NN = (((1,), (0,)), ((), ()))
NT = (((1,), (1,)), ((), ()))
TN = (((0,), (0,)), ((), ()))


def dot(a, b, dims):
    return lax.dot_general(a, b, dims, preferred_element_type=jnp.float32)


def bf16(*shape):
    return jax.ShapeDtypeStruct(shape, jnp.bfloat16)


def place():
    index = lax.axis_index("ctx")
    return index // QUAD, index % QUAD


def columns(index, width):
    return pl.ds(pl.multiple_of(index * width, width), width)


def pack_keys(
    back_key, back_value, back_types, key, value, types, table_ref, *refs
):
    pieces, (keys, event_types, table, typed, arrived, placed) = refs[:QUAD], refs[QUAD:]
    _, member = place()
    copies = [pltpu.make_async_copy(table_ref.at[0], table, arrived.at[4])]
    for i, (key_ref, types_ref) in enumerate([(back_key, back_types), (key, types)]):
        copies += [
            pltpu.make_async_copy(types_ref, event_types.at[i], arrived.at[2 * i]),
            pltpu.make_async_copy(key_ref.at[0], keys.at[i], arrived.at[2 * i + 1]),
        ]
    placements = [
        pltpu.make_async_copy(
            value_ref.at[0, :, columns(member ^ d, HEAD)],
            pieces[d].at[:, (2 * i + 1) * HEAD : (2 * i + 2) * HEAD],
            placed.at[i * QUAD + d],
        )
        for i, value_ref in enumerate([back_value, value])
        for d in range(QUAD)
    ]
    for copy in copies + placements:
        copy.start()
    for copy in copies:
        copy.wait()
    for i in range(2):
        onehot = (
            lax.broadcasted_iota(jnp.int32, (table.shape[0], types.shape[1]), 0) == event_types[i]
        ).astype(jnp.float32).astype(jnp.bfloat16)
        type_rows = dot(onehot, table[...], TN)
        typed[...] = (keys[i].astype(jnp.float32) + type_rows).astype(jnp.bfloat16)
        for d in range(QUAD):
            pieces[d][:, 2 * i * HEAD : (2 * i + 1) * HEAD] = typed[:, columns(member ^ d, HEAD)]
    for copy in placements:
        copy.wait()


def stack_keys(*refs):
    pieces, (back, front, placed) = refs[:QUAD], refs[QUAD:]
    rows = pieces[0].shape[0]
    copies = [
        pltpu.make_async_copy(
            pieces[d].at[:, 2 * i * HEAD : (2 * i + 2) * HEAD],
            out.at[d * rows : (d + 1) * rows, :],
            placed.at[i * QUAD + d],
        )
        for i, out in enumerate([back, front])
        for d in range(QUAD)
    ]
    for copy in copies:
        copy.start()
    for copy in copies:
        copy.wait()


def pack_queries(query_ref, grad_ref, forward_ref, gate_ref, gain_ref, *refs):
    pieces, (gate_out, placed) = refs[:QUAD], refs[QUAD:]
    _, member = place()
    width = query_ref.shape[2] // QUAD
    rows = gate_ref.shape[1]
    copies = [
        pltpu.make_async_copy(
            source.at[0, :, columns(member ^ d, width)],
            pieces[d].at[:, i * width : (i + 1) * width],
            placed.at[3 * d + i],
        )
        for d in reversed(range(QUAD))
        for i, source in enumerate([query_ref, grad_ref, forward_ref])
    ]
    copies.append(
        pltpu.make_async_copy(gate_ref.at[0], gate_out.at[:rows, :], placed.at[3 * QUAD])
    )
    for copy in copies:
        copy.start()
    rest = gain_ref[...]
    parts = []
    for _ in range(3):
        part = rest.astype(jnp.bfloat16).astype(jnp.float32)
        parts.append(part)
        rest = rest - part
    parts.append(jnp.zeros((GAIN_ROWS - 3, rest.shape[1]), jnp.float32))
    gate_out[rows:, :] = jnp.concatenate(parts, axis=0).astype(jnp.bfloat16)
    for copy in copies:
        copy.wait()


def stretch_of(order_ref, quad_index, member, d, e):
    return order_ref[0, 2 * (quad_index * QUAD + (member ^ d)) + e]


def rows_at(index, count):
    return pl.ds(pl.multiple_of(index * count, count), count)


def in_sequence(order_ref, stacks, stretch_rows, keys, values):
    z, member = place()
    nz = len(stacks)
    for s, stack in enumerate(stacks):
        source = lax.rem(z - s + nz, nz)
        for d in range(QUAD):
            for e in range(2):
                rows = rows_at(stretch_of(order_ref, source, member, d, e), stretch_rows)
                lower = (2 * d + e) * stretch_rows
                keys[rows, :] = stack[lower : lower + stretch_rows, :HEAD]
                values[rows, :] = stack[lower : lower + stretch_rows, HEAD:]


def shrink_of(stretch, stretch_rows):
    pos = stretch * stretch_rows + lax.broadcasted_iota(jnp.int32, (stretch_rows, HEAD), 0)
    return lax.rsqrt((pos + 1).astype(jnp.float32))


def step_place(first, second, step, d, groups):
    blocks = first // groups + 1
    late = step >= blocks
    row = jnp.where(late, 2 * d + 1, 2 * d)
    stretch = jnp.where(late, second, first)
    block = jnp.where(late, step - blocks, step)
    return row, stretch, block


def sigmoid_of(raw, visible):
    part = pl.reciprocal(1.0 + jnp.exp2(raw * EXP2_SCALE), approx=True)
    return jnp.where(visible, part, 0.0)


def forward_kernel(nz, order_ref, *refs):
    queries, refs = refs[:QUAD], refs[QUAD:]
    stacks, refs = refs[:nz], refs[nz:]
    outs, refs = refs[:QUAD], refs[QUAD:]
    keys, values, stacked, total, gap = refs
    z, member = place()
    stretch_rows = queries[0].shape[0] // 2
    groups = outs[0].shape[1] // HEAD
    block_rows = groups * stretch_rows
    steps = keys.shape[0] // block_rows + 1
    in_sequence(order_ref, stacks, stretch_rows, keys, values)
    offset = 2 * groups * HEAD
    for d in range(QUAD):
        for e in range(2):
            for g in range(groups):
                stacked[2 * d + e, g * stretch_rows : (g + 1) * stretch_rows, :] = queries[d][
                    e * stretch_rows : (e + 1) * stretch_rows,
                    offset + g * HEAD : offset + (g + 1) * HEAD,
                ]
    total[...] = jnp.zeros_like(total)
    gap[...] = lax.broadcasted_iota(jnp.int32, gap.shape, 1) - lax.rem(
        lax.broadcasted_iota(jnp.int32, gap.shape, 0), stretch_rows
    )

    def advance(step, _):
        for d in range(QUAD):
            row, stretch, block = step_place(
                stretch_of(order_ref, z, member, d, 0),
                stretch_of(order_ref, z, member, d, 1),
                step,
                d,
                groups,
            )
            rows = rows_at(block, block_rows)
            raw = dot(stacked[row], keys[rows, :], NT)
            visible = gap[...] <= stretch * stretch_rows - block * block_rows
            weights = (raw * SCALE * sigmoid_of(raw, visible)).astype(jnp.bfloat16)
            total[row] += dot(weights, values[rows, :], NN)
        return 0

    lax.fori_loop(0, steps, advance, 0)
    for d in range(QUAD):
        for e in range(2):
            shrink = shrink_of(stretch_of(order_ref, z, member, d, e), stretch_rows)
            for g in range(groups):
                outs[d][e * stretch_rows : (e + 1) * stretch_rows, g * HEAD : (g + 1) * HEAD] = (
                    total[2 * d + e, g * stretch_rows : (g + 1) * stretch_rows, :] * shrink
                ).astype(jnp.bfloat16)


def backward_kernel(nz, order_ref, *refs):
    queries, refs = refs[:QUAD], refs[QUAD:]
    stacks, refs = refs[:nz], refs[nz:]
    query_outs, refs = refs[:QUAD], refs[QUAD:]
    key_outs, refs = refs[:nz], refs[nz:]
    keys, values, keys_t, stacked, grads, total_t, key_total, value_total, gap = refs
    z, member = place()
    stretch_rows = queries[0].shape[0] // 2
    groups = query_outs[0].shape[1] // HEAD
    block_rows = groups * stretch_rows
    blocks = keys.shape[0] // block_rows
    steps = blocks + 1
    in_sequence(order_ref, stacks, stretch_rows, keys, values)
    for block in range(blocks):
        lower = block * block_rows
        keys_t[block] = keys[lower : lower + block_rows, :].T
    offset = groups * HEAD
    for d in range(QUAD):
        for e in range(2):
            shrink = shrink_of(stretch_of(order_ref, z, member, d, e), stretch_rows)
            rows = slice(e * stretch_rows, (e + 1) * stretch_rows)
            for g in range(groups):
                into = slice(g * stretch_rows, (g + 1) * stretch_rows)
                stacked[2 * d + e, into, :] = queries[d][rows, g * HEAD : (g + 1) * HEAD]
                grads[2 * d + e, into, :] = (
                    queries[d][rows, offset + g * HEAD : offset + (g + 1) * HEAD].astype(
                        jnp.float32
                    )
                    * shrink
                ).astype(jnp.bfloat16)
    total_t[...] = jnp.zeros_like(total_t)
    key_total[...] = jnp.zeros_like(key_total)
    value_total[...] = jnp.zeros_like(value_total)
    gap[...] = lax.broadcasted_iota(jnp.int32, gap.shape, 0) - lax.rem(
        lax.broadcasted_iota(jnp.int32, gap.shape, 1), stretch_rows
    )

    def advance(step, _):
        for d in range(QUAD):
            row, stretch, block = step_place(
                stretch_of(order_ref, z, member, d, 0),
                stretch_of(order_ref, z, member, d, 1),
                step,
                d,
                groups,
            )
            rows = rows_at(block, block_rows)
            raw = dot(keys[rows, :], stacked[row], NT)
            weight_grad = dot(values[rows, :], grads[row], NT)
            visible = gap[...] <= stretch * stretch_rows - block * block_rows
            part = sigmoid_of(raw, visible)
            weights = raw * SCALE * part
            score_grad = (weight_grad * (part + weights * (1.0 - part))).astype(jnp.bfloat16)
            weights = weights.astype(jnp.bfloat16)
            total_t[row] += dot(keys_t[block], score_grad, NN)
            key_total[rows, :] += dot(score_grad, stacked[row], NN)
            value_total[rows, :] += dot(weights, grads[row], NN)
        return 0

    lax.fori_loop(0, steps, advance, 0)
    for d in range(QUAD):
        for e in range(2):
            query_grad = (total_t[2 * d + e].T * SCALE).astype(jnp.bfloat16)
            for g in range(groups):
                query_outs[d][
                    e * stretch_rows : (e + 1) * stretch_rows, g * HEAD : (g + 1) * HEAD
                ] = query_grad[g * stretch_rows : (g + 1) * stretch_rows, :]
    for s in range(nz):
        target = lax.rem(z + s, nz)
        for d in range(QUAD):
            for e in range(2):
                rows = rows_at(stretch_of(order_ref, target, member, d, e), stretch_rows)
                lower = (2 * d + e) * stretch_rows
                key_outs[s][lower : lower + stretch_rows, :HEAD] = (
                    key_total[rows, :] * SCALE
                ).astype(jnp.bfloat16)
                key_outs[s][lower : lower + stretch_rows, HEAD:] = value_total[rows, :].astype(
                    jnp.bfloat16
                )


def sum_kernel(*refs):
    parts, pieces = refs[:-QUAD], refs[-QUAD:]
    rows = pieces[0].shape[0]
    for d in range(QUAD):
        lower = d * rows
        pieces[d][...] = sum(
            part[lower : lower + rows, :].astype(jnp.float32) for part in parts
        ).astype(jnp.bfloat16)


def key_grad_kernel(*refs):
    pieces, (key_out, value_out) = refs[:QUAD], refs[QUAD:]
    _, member = place()
    for d in range(QUAD):
        head = columns(member ^ d, HEAD)
        key_out[0, :, head] = pieces[d][:, :HEAD]
        value_out[0, :, head] = pieces[d][:, HEAD:]


def query_grad_kernel(*refs):
    pieces, out = refs[:QUAD], refs[QUAD]
    _, member = place()
    for d in range(QUAD):
        out[0, :, columns(member ^ d, pieces[d].shape[1])] = pieces[d][...]


def gate_kernel(*refs):
    pieces, (gate_ref, out) = refs[:QUAD], refs[QUAD:]
    _, member = place()
    rows = out.shape[1]
    attended = [piece[...].astype(jnp.float32) for piece in pieces]
    square = sum(jnp.sum(part * part, axis=1, keepdims=True) for part in attended)
    factor = lax.rsqrt(square / out.shape[2] + norm_eps)
    for d in range(QUAD):
        head = columns(member ^ d, pieces[d].shape[1])
        gain = sum(gate_ref[rows : rows + GAIN_ROWS, head].astype(jnp.float32)[i : i + 1] for i in range(3))
        out[0, :, head] = (
            attended[d] * factor * gain * gate_ref[:rows, head].astype(jnp.float32)
        ).astype(jnp.bfloat16)


def call(kernel, name, out_shape, specs, *args, scratch=(), flops=0, transcendentals=0, vmem=40):
    size = sum(a.size * a.dtype.itemsize for a in args)
    size += sum(math.prod(o.shape) * o.dtype.itemsize for o in out_shape)
    return pl.pallas_call(
        kernel,
        name=name,
        out_shape=out_shape,
        in_specs=specs,
        out_specs=[VMEM] * len(out_shape),
        scratch_shapes=list(scratch),
        compiler_params=pltpu.CompilerParams(vmem_limit_bytes=vmem * MIB),
        cost_estimate=pl.CostEstimate(
            flops=flops, bytes_accessed=size, transcendentals=transcendentals
        ),
    )(*args)


def body(
    query_fwd,
    key_fwd,
    value_fwd,
    gate_fwd,
    types_fwd,
    query_bwd,
    key_bwd,
    value_bwd,
    grad_out,
    types_bwd,
    type_key,
    norm_gain,
    stretch_order,
):
    devices = lax.axis_size("ctx")
    nz = devices // QUAD
    rows = query_fwd.shape[1]
    total_rows = rows * devices
    width = query_fwd.shape[2] // QUAD
    groups = width // HEAD
    stretch_rows = rows // 2
    block_rows = groups * stretch_rows
    steps = total_rows // block_rows + 1
    pairs = steps * QUAD * block_rows * block_rows

    def swap(pieces):
        return [pieces[0]] + [
            lax.ppermute(pieces[d], "ctx", [(i, i ^ d) for i in range(devices)])
            for d in range(1, QUAD)
        ]

    def turn(block, s):
        return lax.ppermute(
            block, "ctx", [(i, (i + s * QUAD) % devices) for i in range(devices)]
        )

    def hand(block, d):
        sections = lax.axis_size("pipe")
        route = [
            (i * sections + p, (i ^ d) * sections + (p + 1) % sections)
            for i in range(devices)
            for p in range(sections)
        ]
        return lax.ppermute(block, ("ctx", "pipe"), route)

    def gather(stack):
        return [stack] + [turn(stack, s) for s in range(1, nz)]

    pieces = swap(
        call(
            pack_keys,
            "pack_keys",
            [bf16(rows, 4 * HEAD)] * QUAD,
            [HBM] * 7,
            key_bwd,
            value_bwd,
            types_bwd,
            key_fwd,
            value_fwd,
            types_fwd,
            type_key,
            scratch=[
                pltpu.VMEM((2, *key_fwd.shape[1:]), jnp.bfloat16),
                pltpu.VMEM((2, *types_fwd.shape), jnp.int32),
                pltpu.VMEM(type_key.shape[1:], jnp.bfloat16),
                pltpu.VMEM(key_fwd.shape[1:], jnp.bfloat16),
                pltpu.SemaphoreType.DMA((5,)),
                pltpu.SemaphoreType.DMA((2 * QUAD,)),
            ],
            vmem=60,
        )
    )
    packed = call(
        pack_queries,
        "pack_queries",
        [bf16(rows, 3 * width)] * QUAD + [bf16(rows + GAIN_ROWS, QUAD * width)],
        [HBM] * 4 + [VMEM],
        query_bwd,
        grad_out,
        query_fwd,
        gate_fwd,
        norm_gain,
        scratch=[pltpu.SemaphoreType.DMA((3 * QUAD + 1,))],
        vmem=60,
    )
    pieces, packed = lax.optimization_barrier((pieces, list(packed)))
    back_stack, stack = call(
        stack_keys,
        "stack_keys",
        [bf16(QUAD * rows, 2 * HEAD)] * 2,
        [HBM] * QUAD,
        *pieces,
        scratch=[pltpu.SemaphoreType.DMA((2 * QUAD,))],
    )
    back_stacks = gather(back_stack)
    back_stacks, packed[1] = lax.optimization_barrier((back_stacks, packed[1]))
    queries = swap(packed[:QUAD])
    gate_before = hand(packed[QUAD], 0)
    stack, back_stacks = lax.optimization_barrier((stack, back_stacks))
    stacks = gather(stack)

    sequence = [pltpu.VMEM((total_rows, HEAD), jnp.bfloat16)] * 2
    stacked = pltpu.VMEM((2 * QUAD, block_rows, HEAD), jnp.bfloat16)
    gap = pltpu.VMEM((block_rows, block_rows), jnp.int32)
    outs = call(
        functools.partial(backward_kernel, nz),
        "backward",
        [bf16(rows, width)] * QUAD + [bf16(QUAD * rows, 2 * HEAD)] * nz,
        [SMEM] + [VMEM] * (QUAD + nz),
        stretch_order,
        *queries,
        *back_stacks,
        scratch=sequence
        + [
            pltpu.VMEM((total_rows // block_rows, HEAD, block_rows), jnp.bfloat16),
            stacked,
            stacked,
            pltpu.VMEM((2 * QUAD, HEAD, block_rows), jnp.float32),
            pltpu.VMEM((total_rows, HEAD), jnp.float32),
            pltpu.VMEM((total_rows, HEAD), jnp.float32),
            gap,
        ],
        flops=10 * pairs * HEAD,
        transcendentals=2 * pairs,
    )
    query_pieces, key_parts = outs[:QUAD], outs[QUAD:]
    query_pieces, key_parts, gate_before = lax.optimization_barrier(
        (query_pieces, key_parts, gate_before)
    )
    key_parts = [key_parts[0]] + [turn(key_parts[s], s) for s in range(1, nz)]
    query_pieces = swap(query_pieces)
    attended = call(
        functools.partial(forward_kernel, nz),
        "forward",
        [bf16(rows, width)] * QUAD,
        [SMEM] + [VMEM] * (QUAD + nz),
        stretch_order,
        *queries,
        *stacks,
        scratch=sequence
        + [stacked, pltpu.VMEM((2 * QUAD, block_rows, HEAD), jnp.float32), gap],
    )
    attended, query_pieces = lax.optimization_barrier((attended, query_pieces))
    (handed,) = call(
        gate_kernel,
        "gate",
        [bf16(*gate_fwd.shape)],
        [VMEM] * (QUAD + 1),
        *[hand(attended[d], d) for d in range(QUAD)],
        gate_before,
    )
    key_pieces = swap(
        call(
            sum_kernel,
            "sum_key_parts",
            [bf16(rows, 2 * HEAD)] * QUAD,
            [VMEM] * nz,
            *key_parts,
        )
    )
    (query_grad,) = call(
        query_grad_kernel,
        "query_grad",
        [bf16(*query_bwd.shape)],
        [VMEM] * QUAD,
        *query_pieces,
    )
    key_grad, value_grad = call(
        key_grad_kernel,
        "key_grad",
        [bf16(*key_bwd.shape), bf16(*value_bwd.shape)],
        [VMEM] * QUAD,
        *key_pieces,
    )
    return handed, query_grad, key_grad, value_grad


def solution(mesh):
    rows = P("pipe", "ctx", None)
    types = P("pipe", "ctx")
    return jax.shard_map(
        body,
        mesh=mesh,
        in_specs=(
            rows,
            rows,
            rows,
            rows,
            types,
            rows,
            rows,
            rows,
            rows,
            types,
            P("pipe", None, None),
            P("pipe", None),
            P("pipe", None),
        ),
        out_specs=(rows, rows, rows, rows),
        check_vma=False,
    )
```

```python
import functools
import math

import jax
import jax.numpy as jnp
from jax import lax
from jax.experimental import pallas as pl
from jax.experimental.pallas import tpu as pltpu
from jax.sharding import PartitionSpec as P

HEAD = 128
UNROLL = 3
QUAD = 4
SCALE = HEAD ** (-0.5)
EXP2_SCALE = -SCALE / math.log(2.0)
GAIN_ROWS = 16
norm_eps = 1e-06

VMEM = pl.BlockSpec(memory_space=pltpu.VMEM)
HBM = pl.BlockSpec(memory_space=pltpu.HBM)
SMEM = pl.BlockSpec(memory_space=pltpu.SMEM)
MIB = 1024 * 1024

NN = (((1,), (0,)), ((), ()))
NT = (((1,), (1,)), ((), ()))
TN = (((0,), (0,)), ((), ()))


def dot(a, b, dims):
    return lax.dot_general(a, b, dims, preferred_element_type=jnp.float32)


def bf16(*shape):
    return jax.ShapeDtypeStruct(shape, jnp.bfloat16)


def place():
    index = lax.axis_index("ctx")
    return index // QUAD, index % QUAD


def columns(index, width):
    return pl.ds(pl.multiple_of(index * width, width), width)


def pack_keys(
    back_key, back_value, back_types, key, value, types, table_ref, *refs
):
    pieces, (keys, event_types, table, typed, arrived, placed) = refs[:QUAD], refs[QUAD:]
    _, member = place()
    copies = [pltpu.make_async_copy(table_ref.at[0], table, arrived.at[4])]
    for i, (key_ref, types_ref) in enumerate([(back_key, back_types), (key, types)]):
        copies += [
            pltpu.make_async_copy(types_ref, event_types.at[i], arrived.at[2 * i]),
            pltpu.make_async_copy(key_ref.at[0], keys.at[i], arrived.at[2 * i + 1]),
        ]
    placements = [
        pltpu.make_async_copy(
            value_ref.at[0, :, columns(member ^ d, HEAD)],
            pieces[d].at[:, (2 * i + 1) * HEAD : (2 * i + 2) * HEAD],
            placed.at[i * QUAD + d],
        )
        for i, value_ref in enumerate([back_value, value])
        for d in range(QUAD)
    ]
    for copy in copies + placements:
        copy.start()
    for copy in copies:
        copy.wait()
    for i in range(2):
        onehot = (
            lax.broadcasted_iota(jnp.int32, (table.shape[0], types.shape[1]), 0) == event_types[i]
        ).astype(jnp.float32).astype(jnp.bfloat16)
        type_rows = dot(onehot, table[...], TN)
        typed[...] = (keys[i].astype(jnp.float32) + type_rows).astype(jnp.bfloat16)
        for d in range(QUAD):
            pieces[d][:, 2 * i * HEAD : (2 * i + 1) * HEAD] = typed[:, columns(member ^ d, HEAD)]
    for copy in placements:
        copy.wait()


def stack_keys(*refs):
    pieces, (back, front, placed) = refs[:QUAD], refs[QUAD:]
    rows = pieces[0].shape[0]
    copies = [
        pltpu.make_async_copy(
            pieces[d].at[:, 2 * i * HEAD : (2 * i + 2) * HEAD],
            out.at[d * rows : (d + 1) * rows, :],
            placed.at[i * QUAD + d],
        )
        for i, out in enumerate([back, front])
        for d in range(QUAD)
    ]
    for copy in copies:
        copy.start()
    for copy in copies:
        copy.wait()


def pack_queries(query_ref, grad_ref, forward_ref, gate_ref, gain_ref, *refs):
    pieces, (gate_out, placed) = refs[:QUAD], refs[QUAD:]
    _, member = place()
    width = query_ref.shape[2] // QUAD
    rows = gate_ref.shape[1]
    copies = [
        pltpu.make_async_copy(
            source.at[0, :, columns(member ^ d, width)],
            pieces[d].at[:, i * width : (i + 1) * width],
            placed.at[3 * d + i],
        )
        for d in reversed(range(QUAD))
        for i, source in enumerate([query_ref, grad_ref, forward_ref])
    ]
    copies.append(
        pltpu.make_async_copy(gate_ref.at[0], gate_out.at[:rows, :], placed.at[3 * QUAD])
    )
    for copy in copies:
        copy.start()
    rest = gain_ref[...]
    parts = []
    for _ in range(3):
        part = rest.astype(jnp.bfloat16).astype(jnp.float32)
        parts.append(part)
        rest = rest - part
    parts.append(jnp.zeros((GAIN_ROWS - 3, rest.shape[1]), jnp.float32))
    gate_out[rows:, :] = jnp.concatenate(parts, axis=0).astype(jnp.bfloat16)
    for copy in copies:
        copy.wait()


def stretch_of(order_ref, quad_index, member, d, e):
    return order_ref[0, 2 * (quad_index * QUAD + (member ^ d)) + e]


def rows_at(index, count):
    return pl.ds(pl.multiple_of(index * count, count), count)


def in_sequence(order_ref, stacks, stretch_rows, keys, values):
    z, member = place()
    nz = len(stacks)
    for s, stack in enumerate(stacks):
        source = lax.rem(z - s + nz, nz)
        for d in range(QUAD):
            for e in range(2):
                rows = rows_at(stretch_of(order_ref, source, member, d, e), stretch_rows)
                lower = (2 * d + e) * stretch_rows
                keys[rows, :] = stack[lower : lower + stretch_rows, :HEAD]
                values[rows, :] = stack[lower : lower + stretch_rows, HEAD:]


def shrink_of(stretch, stretch_rows):
    pos = stretch * stretch_rows + lax.broadcasted_iota(jnp.int32, (stretch_rows, HEAD), 0)
    return lax.rsqrt((pos + 1).astype(jnp.float32))


def step_place(first, second, step, d, groups):
    blocks = first // groups + 1
    late = step >= blocks
    row = jnp.where(late, 2 * d + 1, 2 * d)
    stretch = jnp.where(late, second, first)
    block = jnp.where(late, step - blocks, step)
    return row, stretch, block


def sigmoid_of(raw, visible):
    part = pl.reciprocal(1.0 + jnp.exp2(raw * EXP2_SCALE), approx=True)
    return jnp.where(visible, part, 0.0)


def repeat(steps, advance):
    def several(i, _):
        for j in range(UNROLL):
            advance(i * UNROLL + j)
        return 0

    lax.fori_loop(0, steps // UNROLL, several, 0)
    for step in range(steps // UNROLL * UNROLL, steps):
        advance(step)


def forward_kernel(nz, parts, order_ref, *refs):
    queries, refs = refs[: len(parts)], refs[len(parts) :]
    stacks, refs = refs[:nz], refs[nz:]
    outs, refs = refs[: len(parts)], refs[len(parts) :]
    keys, values, stacked, total, gap = refs
    z, member = place()
    stretch_rows = queries[0].shape[0] // 2
    groups = outs[0].shape[1] // HEAD
    block_rows = groups * stretch_rows
    steps = keys.shape[0] // block_rows + 1
    in_sequence(order_ref, stacks, stretch_rows, keys, values)
    offset = 2 * groups * HEAD
    for i in range(len(parts)):
        for e in range(2):
            for g in range(groups):
                stacked[2 * i + e, g * stretch_rows : (g + 1) * stretch_rows, :] = queries[i][
                    e * stretch_rows : (e + 1) * stretch_rows,
                    offset + g * HEAD : offset + (g + 1) * HEAD,
                ]
    total[...] = jnp.zeros_like(total)
    gap[...] = lax.broadcasted_iota(jnp.int32, gap.shape, 1) - lax.rem(
        lax.broadcasted_iota(jnp.int32, gap.shape, 0), stretch_rows
    )

    def advance(step):
        for i, d in enumerate(parts):
            row, stretch, block = step_place(
                stretch_of(order_ref, z, member, d, 0),
                stretch_of(order_ref, z, member, d, 1),
                step,
                i,
                groups,
            )
            rows = rows_at(block, block_rows)
            raw = dot(stacked[row], keys[rows, :], NT)
            visible = gap[...] <= stretch * stretch_rows - block * block_rows
            weights = (raw * sigmoid_of(raw, visible)).astype(jnp.bfloat16)
            total[row] += dot(weights, values[rows, :], NN)

    repeat(steps, advance)
    for i, d in enumerate(parts):
        for e in range(2):
            shrink = SCALE * shrink_of(stretch_of(order_ref, z, member, d, e), stretch_rows)
            for g in range(groups):
                outs[i][e * stretch_rows : (e + 1) * stretch_rows, g * HEAD : (g + 1) * HEAD] = (
                    total[2 * i + e, g * stretch_rows : (g + 1) * stretch_rows, :] * shrink
                ).astype(jnp.bfloat16)


def backward_kernel(nz, order_ref, *refs):
    queries, refs = refs[:QUAD], refs[QUAD:]
    stacks, refs = refs[:nz], refs[nz:]
    query_outs, refs = refs[:QUAD], refs[QUAD:]
    key_outs, refs = refs[:nz], refs[nz:]
    keys, values, keys_t, stacked, grads, total_t, key_total, value_total, gap = refs
    z, member = place()
    stretch_rows = queries[0].shape[0] // 2
    groups = query_outs[0].shape[1] // HEAD
    block_rows = groups * stretch_rows
    blocks = keys.shape[0] // block_rows
    steps = blocks + 1
    in_sequence(order_ref, stacks, stretch_rows, keys, values)
    for block in range(blocks):
        lower = block * block_rows
        keys_t[block] = keys[lower : lower + block_rows, :].T
    offset = groups * HEAD
    for d in range(QUAD):
        for e in range(2):
            shrink = shrink_of(stretch_of(order_ref, z, member, d, e), stretch_rows)
            rows = slice(e * stretch_rows, (e + 1) * stretch_rows)
            for g in range(groups):
                into = slice(g * stretch_rows, (g + 1) * stretch_rows)
                stacked[2 * d + e, into, :] = queries[d][rows, g * HEAD : (g + 1) * HEAD]
                grads[2 * d + e, into, :] = (
                    queries[d][rows, offset + g * HEAD : offset + (g + 1) * HEAD].astype(
                        jnp.float32
                    )
                    * shrink
                ).astype(jnp.bfloat16)
    total_t[...] = jnp.zeros_like(total_t)
    key_total[...] = jnp.zeros_like(key_total)
    value_total[...] = jnp.zeros_like(value_total)
    gap[...] = lax.broadcasted_iota(jnp.int32, gap.shape, 0) - lax.rem(
        lax.broadcasted_iota(jnp.int32, gap.shape, 1), stretch_rows
    )

    def advance(step):
        for d in range(QUAD):
            row, stretch, block = step_place(
                stretch_of(order_ref, z, member, d, 0),
                stretch_of(order_ref, z, member, d, 1),
                step,
                d,
                groups,
            )
            rows = rows_at(block, block_rows)
            raw = dot(keys[rows, :], stacked[row], NT)
            weight_grad = dot(values[rows, :], grads[row], NT)
            visible = gap[...] <= stretch * stretch_rows - block * block_rows
            part = sigmoid_of(raw, visible)
            weights = raw * SCALE * part
            score_grad = (weight_grad * (part + weights * (1.0 - part))).astype(jnp.bfloat16)
            weights = weights.astype(jnp.bfloat16)
            total_t[row] += dot(keys_t[block], score_grad, NN)
            key_total[rows, :] += dot(score_grad, stacked[row], NN)
            value_total[rows, :] += dot(weights, grads[row], NN)

    repeat(steps, advance)
    for d in range(QUAD):
        for e in range(2):
            query_grad = (total_t[2 * d + e].T * SCALE).astype(jnp.bfloat16)
            for g in range(groups):
                query_outs[d][
                    e * stretch_rows : (e + 1) * stretch_rows, g * HEAD : (g + 1) * HEAD
                ] = query_grad[g * stretch_rows : (g + 1) * stretch_rows, :]
    for s in range(nz):
        target = lax.rem(z + s, nz)
        for d in range(QUAD):
            for e in range(2):
                rows = rows_at(stretch_of(order_ref, target, member, d, e), stretch_rows)
                lower = (2 * d + e) * stretch_rows
                key_outs[s][lower : lower + stretch_rows, :HEAD] = (
                    key_total[rows, :] * SCALE
                ).astype(jnp.bfloat16)
                key_outs[s][lower : lower + stretch_rows, HEAD:] = value_total[rows, :].astype(
                    jnp.bfloat16
                )


def sum_kernel(*refs):
    parts, pieces = refs[:3], refs[3:]
    rows = pieces[0].shape[0]
    for d in range(QUAD):
        lower = d * rows
        pieces[d][...] = sum(
            part[lower : lower + rows, :].astype(jnp.float32) for part in parts
        ).astype(jnp.bfloat16)


def key_grad_kernel(*refs):
    pieces, (key_out, value_out) = refs[:QUAD], refs[QUAD:]
    _, member = place()
    for d in range(QUAD):
        head = columns(member ^ d, HEAD)
        key_out[0, :, head] = pieces[d][:, :HEAD]
        value_out[0, :, head] = pieces[d][:, HEAD:]


def query_grad_kernel(*refs):
    pieces, out = refs[:QUAD], refs[QUAD]
    _, member = place()
    for d in range(QUAD):
        out[0, :, columns(member ^ d, pieces[d].shape[1])] = pieces[d][...]


def gate_kernel(*refs):
    pieces, (gate_ref, out) = refs[:QUAD], refs[QUAD:]
    _, member = place()
    rows = out.shape[1]
    attended = [piece[...].astype(jnp.float32) for piece in pieces]
    square = sum(jnp.sum(part * part, axis=1, keepdims=True) for part in attended)
    factor = lax.rsqrt(square / out.shape[2] + norm_eps)
    for d in range(QUAD):
        head = columns(member ^ d, pieces[d].shape[1])
        gain = sum(gate_ref[rows : rows + GAIN_ROWS, head].astype(jnp.float32)[i : i + 1] for i in range(3))
        out[0, :, head] = (
            attended[d] * factor * gain * gate_ref[:rows, head].astype(jnp.float32)
        ).astype(jnp.bfloat16)


def call(kernel, name, out_shape, specs, *args, scratch=(), flops=0, transcendentals=0, vmem=40):
    size = sum(a.size * a.dtype.itemsize for a in args)
    size += sum(math.prod(o.shape) * o.dtype.itemsize for o in out_shape)
    return pl.pallas_call(
        kernel,
        name=name,
        out_shape=out_shape,
        in_specs=specs,
        out_specs=[VMEM] * len(out_shape),
        scratch_shapes=list(scratch),
        compiler_params=pltpu.CompilerParams(vmem_limit_bytes=vmem * MIB),
        cost_estimate=pl.CostEstimate(
            flops=flops, bytes_accessed=size, transcendentals=transcendentals
        ),
    )(*args)


def body(
    query_fwd,
    key_fwd,
    value_fwd,
    gate_fwd,
    types_fwd,
    query_bwd,
    key_bwd,
    value_bwd,
    grad_out,
    types_bwd,
    type_key,
    norm_gain,
    stretch_order,
):
    devices = lax.axis_size("ctx")
    nz = devices // QUAD
    rows = query_fwd.shape[1]
    total_rows = rows * devices
    width = query_fwd.shape[2] // QUAD
    groups = width // HEAD
    stretch_rows = rows // 2
    block_rows = groups * stretch_rows
    steps = total_rows // block_rows + 1
    pairs = steps * QUAD * block_rows * block_rows

    def swap(pieces):
        return [pieces[0]] + [
            lax.ppermute(pieces[d], "ctx", [(i, i ^ d) for i in range(devices)])
            for d in range(1, QUAD)
        ]

    def turn(block, s):
        return lax.ppermute(
            block, "ctx", [(i, (i + s * QUAD) % devices) for i in range(devices)]
        )

    def hand(block, d):
        sections = lax.axis_size("pipe")
        route = [
            (i * sections + p, (i ^ d) * sections + (p + 1) % sections)
            for i in range(devices)
            for p in range(sections)
        ]
        return lax.ppermute(block, ("ctx", "pipe"), route)

    ahead = nz // 2

    def ring_up(block):
        return turn(block, 1)

    def ring_down(block):
        return turn(block, nz - 1)

    def gather_first(stack):
        return [stack, ring_up(stack)], [ring_down(stack)]

    def gather_rest(up, down):
        up, down = lax.optimization_barrier((up, down))
        while len(up) <= ahead:
            up = up + [ring_up(up[-1])]
        while len(up) + len(down) < nz:
            down = down + [ring_down(down[-1])]
        return up + down[::-1]

    def reduce_first(parts):
        return ring_up(parts[ahead]), ring_down(parts[ahead + 1])

    def add(a, b):
        return (a.astype(jnp.float32) + b.astype(jnp.float32)).astype(jnp.bfloat16)

    def reduce_rest(parts, up, down):
        for s in range(ahead - 1, 0, -1):
            up = ring_up(add(up, parts[s]))
        for s in range(ahead + 2, nz):
            down = ring_down(add(down, parts[s]))
        return parts[0], up, down

    pieces = swap(
        call(
            pack_keys,
            "pack_keys",
            [bf16(rows, 4 * HEAD)] * QUAD,
            [HBM] * 7,
            key_bwd,
            value_bwd,
            types_bwd,
            key_fwd,
            value_fwd,
            types_fwd,
            type_key,
            scratch=[
                pltpu.VMEM((2, *key_fwd.shape[1:]), jnp.bfloat16),
                pltpu.VMEM((2, *types_fwd.shape), jnp.int32),
                pltpu.VMEM(type_key.shape[1:], jnp.bfloat16),
                pltpu.VMEM(key_fwd.shape[1:], jnp.bfloat16),
                pltpu.SemaphoreType.DMA((5,)),
                pltpu.SemaphoreType.DMA((2 * QUAD,)),
            ],
            vmem=60,
        )
    )
    packed = call(
        pack_queries,
        "pack_queries",
        [bf16(rows, 3 * width)] * QUAD + [bf16(rows + GAIN_ROWS, QUAD * width)],
        [HBM] * 4 + [VMEM],
        query_bwd,
        grad_out,
        query_fwd,
        gate_fwd,
        norm_gain,
        scratch=[pltpu.SemaphoreType.DMA((3 * QUAD + 1,))],
        vmem=60,
    )
    pieces, packed = lax.optimization_barrier((pieces, packed))
    back_stack, stack = call(
        stack_keys,
        "stack_keys",
        [bf16(QUAD * rows, 2 * HEAD)] * 2,
        [HBM] * QUAD,
        *pieces,
        scratch=[pltpu.SemaphoreType.DMA((2 * QUAD,))],
    )
    queries = swap(packed[:QUAD])
    up, down = gather_first(back_stack)
    up, down, gate_before = lax.optimization_barrier((up, down, packed[QUAD]))
    back_stacks = gather_rest(up, down)
    gate_before = hand(gate_before, 0)
    stack, back_stacks = lax.optimization_barrier((stack, back_stacks))
    stacks = [stack] + [turn(stack, s) for s in range(1, nz)]

    sequence = [pltpu.VMEM((total_rows, HEAD), jnp.bfloat16)] * 2
    stacked = pltpu.VMEM((2 * QUAD, block_rows, HEAD), jnp.bfloat16)
    gap = pltpu.VMEM((block_rows, block_rows), jnp.int32)
    outs = call(
        functools.partial(backward_kernel, nz),
        "backward",
        [bf16(rows, width)] * QUAD + [bf16(QUAD * rows, 2 * HEAD)] * nz,
        [SMEM] + [VMEM] * (QUAD + nz),
        stretch_order,
        *queries,
        *back_stacks,
        scratch=sequence
        + [
            pltpu.VMEM((total_rows // block_rows, HEAD, block_rows), jnp.bfloat16),
            stacked,
            stacked,
            pltpu.VMEM((2 * QUAD, HEAD, block_rows), jnp.float32),
            pltpu.VMEM((total_rows, HEAD), jnp.float32),
            pltpu.VMEM((total_rows, HEAD), jnp.float32),
            gap,
        ],
        flops=10 * pairs * HEAD,
        transcendentals=2 * pairs,
    )
    query_pieces, key_parts = outs[:QUAD], outs[QUAD:]
    query_pieces, key_parts, gate_before = lax.optimization_barrier(
        (query_pieces, key_parts, gate_before)
    )
    key_sums = reduce_first(key_parts)
    query_pieces = swap(query_pieces)
    def attend(parts, name):
        return call(
            functools.partial(forward_kernel, nz, parts),
            name,
            [bf16(rows, width)] * len(parts),
            [SMEM] + [VMEM] * (len(parts) + nz),
            stretch_order,
            *[queries[d] for d in parts],
            *stacks,
            scratch=sequence
            + [
                pltpu.VMEM((2 * len(parts), block_rows, HEAD), jnp.bfloat16),
                pltpu.VMEM((2 * len(parts), block_rows, HEAD), jnp.float32),
                gap,
            ],
        )

    far = attend((2, 3), "forward_far")
    far, query_pieces, key_sums = lax.optimization_barrier((far, query_pieces, key_sums))
    far = [hand(piece, d) for d, piece in zip((2, 3), far)]
    far, stacks = lax.optimization_barrier((far, stacks))
    near = attend((0, 1), "forward_near")
    near = [hand(piece, d) for d, piece in zip((0, 1), near)]
    (handed,) = call(
        gate_kernel,
        "gate",
        [bf16(*gate_fwd.shape)],
        [VMEM] * (QUAD + 1),
        *near,
        *far,
        gate_before,
    )
    key_sums = reduce_rest(key_parts, *key_sums)
    key_pieces = swap(
        call(
            sum_kernel,
            "sum_key_parts",
            [bf16(rows, 2 * HEAD)] * QUAD,
            [VMEM] * 3,
            *key_sums,
        )
    )
    (query_grad,) = call(
        query_grad_kernel,
        "query_grad",
        [bf16(*query_bwd.shape)],
        [VMEM] * QUAD,
        *query_pieces,
    )
    key_grad, value_grad = call(
        key_grad_kernel,
        "key_grad",
        [bf16(*key_bwd.shape), bf16(*value_bwd.shape)],
        [VMEM] * QUAD,
        *key_pieces,
    )
    return handed, query_grad, key_grad, value_grad


def solution(mesh):
    rows = P("pipe", "ctx", None)
    types = P("pipe", "ctx")
    return jax.shard_map(
        body,
        mesh=mesh,
        in_specs=(
            rows,
            rows,
            rows,
            rows,
            types,
            rows,
            rows,
            rows,
            rows,
            types,
            P("pipe", None, None),
            P("pipe", None),
            P("pipe", None),
        ),
        out_specs=(rows, rows, rows, rows),
        check_vma=False,
    )
```

```python
import functools
import math

import jax
import jax.numpy as jnp
from jax import lax
from jax.experimental import pallas as pl
from jax.experimental.pallas import tpu as pltpu
from jax.sharding import PartitionSpec as P

HEAD = 128
UNROLL = 3
QUAD = 4
SCALE = HEAD ** (-0.5)
EXP2_SCALE = -SCALE / math.log(2.0)
GAIN_ROWS = 16
norm_eps = 1e-06

VMEM = pl.BlockSpec(memory_space=pltpu.VMEM)
HBM = pl.BlockSpec(memory_space=pltpu.HBM)
SMEM = pl.BlockSpec(memory_space=pltpu.SMEM)
MIB = 1024 * 1024

NN = (((1,), (0,)), ((), ()))
NT = (((1,), (1,)), ((), ()))
TN = (((0,), (0,)), ((), ()))


def dot(a, b, dims):
    return lax.dot_general(a, b, dims, preferred_element_type=jnp.float32)


def bf16(*shape):
    return jax.ShapeDtypeStruct(shape, jnp.bfloat16)


def place():
    index = lax.axis_index("ctx")
    return index // QUAD, index % QUAD


def columns(index, width):
    return pl.ds(pl.multiple_of(index * width, width), width)


def pack_keys(key_ref, value_ref, types_ref, table_ref, *refs):
    pieces, (keys, types, table, typed, arrived, placed) = refs[:QUAD], refs[QUAD:]
    _, member = place()
    copies = [
        pltpu.make_async_copy(source, target, arrived.at[i])
        for i, (source, target) in enumerate(
            [(types_ref, types), (table_ref.at[0], table), (key_ref.at[0], keys)]
        )
    ]
    placements = [
        pltpu.make_async_copy(
            value_ref.at[0, :, columns(member ^ d, HEAD)], pieces[d].at[:, HEAD:], placed.at[d]
        )
        for d in range(QUAD)
    ]
    for copy in copies + placements:
        copy.start()
    for copy in copies:
        copy.wait()
    onehot = (
        lax.broadcasted_iota(jnp.int32, (table.shape[0], types.shape[1]), 0) == types[...]
    ).astype(jnp.float32).astype(jnp.bfloat16)
    type_rows = dot(onehot, table[...], TN)
    typed[...] = (keys[...].astype(jnp.float32) + type_rows).astype(jnp.bfloat16)
    for d in range(QUAD):
        pieces[d][:, :HEAD] = typed[:, columns(member ^ d, HEAD)]
    for copy in placements:
        copy.wait()


def stack_keys(*refs):
    pieces, (out, placed) = refs[:QUAD], refs[QUAD:]
    rows = pieces[0].shape[0]
    copies = [
        pltpu.make_async_copy(pieces[d], out.at[d * rows : (d + 1) * rows, :], placed.at[d])
        for d in range(QUAD)
    ]
    for copy in copies:
        copy.start()
    for copy in copies:
        copy.wait()


def pack_queries(query_ref, grad_ref, forward_ref, gate_ref, gain_ref, *refs):
    pieces, (gate_out, placed) = refs[:QUAD], refs[QUAD:]
    _, member = place()
    width = query_ref.shape[2] // QUAD
    rows = gate_ref.shape[1]
    copies = [
        pltpu.make_async_copy(
            source.at[0, :, columns(member ^ d, width)],
            pieces[d].at[:, i * width : (i + 1) * width],
            placed.at[3 * d + i],
        )
        for d in reversed(range(QUAD))
        for i, source in enumerate([query_ref, grad_ref, forward_ref])
    ]
    copies.append(
        pltpu.make_async_copy(gate_ref.at[0], gate_out.at[:rows, :], placed.at[3 * QUAD])
    )
    for copy in copies:
        copy.start()
    rest = gain_ref[...]
    parts = []
    for _ in range(3):
        part = rest.astype(jnp.bfloat16).astype(jnp.float32)
        parts.append(part)
        rest = rest - part
    parts.append(jnp.zeros((GAIN_ROWS - 3, rest.shape[1]), jnp.float32))
    gate_out[rows:, :] = jnp.concatenate(parts, axis=0).astype(jnp.bfloat16)
    for copy in copies:
        copy.wait()


def stretch_of(order_ref, quad_index, member, d, e):
    return order_ref[0, 2 * (quad_index * QUAD + (member ^ d)) + e]


def rows_at(index, count):
    return pl.ds(pl.multiple_of(index * count, count), count)


def in_sequence(order_ref, stacks, stretch_rows, keys, values):
    z, member = place()
    nz = len(stacks)
    for s, stack in enumerate(stacks):
        source = lax.rem(z - s + nz, nz)
        for d in range(QUAD):
            for e in range(2):
                rows = rows_at(stretch_of(order_ref, source, member, d, e), stretch_rows)
                lower = (2 * d + e) * stretch_rows
                keys[rows, :] = stack[lower : lower + stretch_rows, :HEAD]
                values[rows, :] = stack[lower : lower + stretch_rows, HEAD:]


def shrink_of(stretch, stretch_rows):
    pos = stretch * stretch_rows + lax.broadcasted_iota(jnp.int32, (stretch_rows, HEAD), 0)
    return lax.rsqrt((pos + 1).astype(jnp.float32))


def step_place(first, second, step, d, groups):
    blocks = first // groups + 1
    late = step >= blocks
    row = jnp.where(late, 2 * d + 1, 2 * d)
    stretch = jnp.where(late, second, first)
    block = jnp.where(late, step - blocks, step)
    return row, stretch, block


def sigmoid_of(raw, visible):
    part = pl.reciprocal(1.0 + jnp.exp2(raw * EXP2_SCALE), approx=True)
    return jnp.where(visible, part, 0.0)


def repeat(steps, advance):
    def several(i, _):
        for j in range(UNROLL):
            advance(i * UNROLL + j)
        return 0

    lax.fori_loop(0, steps // UNROLL, several, 0)
    for step in range(steps // UNROLL * UNROLL, steps):
        advance(step)


def forward_kernel(nz, parts, order_ref, *refs):
    queries, refs = refs[: len(parts)], refs[len(parts) :]
    stacks, refs = refs[:nz], refs[nz:]
    outs, refs = refs[: len(parts)], refs[len(parts) :]
    keys, values, stacked, total, gap = refs
    z, member = place()
    stretch_rows = queries[0].shape[0] // 2
    groups = outs[0].shape[1] // HEAD
    block_rows = groups * stretch_rows
    steps = keys.shape[0] // block_rows + 1
    in_sequence(order_ref, stacks, stretch_rows, keys, values)
    offset = 2 * groups * HEAD
    for i in range(len(parts)):
        for e in range(2):
            for g in range(groups):
                stacked[2 * i + e, g * stretch_rows : (g + 1) * stretch_rows, :] = queries[i][
                    e * stretch_rows : (e + 1) * stretch_rows,
                    offset + g * HEAD : offset + (g + 1) * HEAD,
                ]
    total[...] = jnp.zeros_like(total)
    gap[...] = lax.broadcasted_iota(jnp.int32, gap.shape, 1) - lax.rem(
        lax.broadcasted_iota(jnp.int32, gap.shape, 0), stretch_rows
    )

    def advance(step):
        for i, d in enumerate(parts):
            row, stretch, block = step_place(
                stretch_of(order_ref, z, member, d, 0),
                stretch_of(order_ref, z, member, d, 1),
                step,
                i,
                groups,
            )
            rows = rows_at(block, block_rows)
            raw = dot(stacked[row], keys[rows, :], NT)
            visible = gap[...] <= stretch * stretch_rows - block * block_rows
            weights = (raw * sigmoid_of(raw, visible)).astype(jnp.bfloat16)
            total[row] += dot(weights, values[rows, :], NN)

    repeat(steps, advance)
    for i, d in enumerate(parts):
        for e in range(2):
            shrink = SCALE * shrink_of(stretch_of(order_ref, z, member, d, e), stretch_rows)
            for g in range(groups):
                outs[i][e * stretch_rows : (e + 1) * stretch_rows, g * HEAD : (g + 1) * HEAD] = (
                    total[2 * i + e, g * stretch_rows : (g + 1) * stretch_rows, :] * shrink
                ).astype(jnp.bfloat16)


def backward_kernel(nz, order_ref, *refs):
    queries, refs = refs[:QUAD], refs[QUAD:]
    stacks, refs = refs[:nz], refs[nz:]
    query_outs, refs = refs[:QUAD], refs[QUAD:]
    key_outs, refs = refs[:nz], refs[nz:]
    keys, values, keys_t, stacked, grads, total_t, key_total, value_total, gap = refs
    z, member = place()
    stretch_rows = queries[0].shape[0] // 2
    groups = query_outs[0].shape[1] // HEAD
    block_rows = groups * stretch_rows
    blocks = keys.shape[0] // block_rows
    steps = blocks + 1
    in_sequence(order_ref, stacks, stretch_rows, keys, values)
    for block in range(blocks):
        lower = block * block_rows
        keys_t[block] = keys[lower : lower + block_rows, :].T
    offset = groups * HEAD
    for d in range(QUAD):
        for e in range(2):
            shrink = shrink_of(stretch_of(order_ref, z, member, d, e), stretch_rows)
            rows = slice(e * stretch_rows, (e + 1) * stretch_rows)
            for g in range(groups):
                into = slice(g * stretch_rows, (g + 1) * stretch_rows)
                stacked[2 * d + e, into, :] = queries[d][rows, g * HEAD : (g + 1) * HEAD]
                grads[2 * d + e, into, :] = (
                    queries[d][rows, offset + g * HEAD : offset + (g + 1) * HEAD].astype(
                        jnp.float32
                    )
                    * shrink
                ).astype(jnp.bfloat16)
    total_t[...] = jnp.zeros_like(total_t)
    key_total[...] = jnp.zeros_like(key_total)
    value_total[...] = jnp.zeros_like(value_total)
    gap[...] = lax.broadcasted_iota(jnp.int32, gap.shape, 0) - lax.rem(
        lax.broadcasted_iota(jnp.int32, gap.shape, 1), stretch_rows
    )

    def advance(step):
        for d in range(QUAD):
            row, stretch, block = step_place(
                stretch_of(order_ref, z, member, d, 0),
                stretch_of(order_ref, z, member, d, 1),
                step,
                d,
                groups,
            )
            rows = rows_at(block, block_rows)
            raw = dot(keys[rows, :], stacked[row], NT)
            weight_grad = dot(values[rows, :], grads[row], NT)
            visible = gap[...] <= stretch * stretch_rows - block * block_rows
            part = sigmoid_of(raw, visible)
            weights = raw * SCALE * part
            score_grad = (weight_grad * (part + weights * (1.0 - part))).astype(jnp.bfloat16)
            weights = weights.astype(jnp.bfloat16)
            total_t[row] += dot(keys_t[block], score_grad, NN)
            key_total[rows, :] += dot(score_grad, stacked[row], NN)
            value_total[rows, :] += dot(weights, grads[row], NN)

    repeat(steps, advance)
    for d in range(QUAD):
        for e in range(2):
            query_grad = (total_t[2 * d + e].T * SCALE).astype(jnp.bfloat16)
            for g in range(groups):
                query_outs[d][
                    e * stretch_rows : (e + 1) * stretch_rows, g * HEAD : (g + 1) * HEAD
                ] = query_grad[g * stretch_rows : (g + 1) * stretch_rows, :]
    for s in range(nz):
        target = lax.rem(z + s, nz)
        for d in range(QUAD):
            for e in range(2):
                rows = rows_at(stretch_of(order_ref, target, member, d, e), stretch_rows)
                lower = (2 * d + e) * stretch_rows
                key_outs[s][lower : lower + stretch_rows, :HEAD] = (
                    key_total[rows, :] * SCALE
                ).astype(jnp.bfloat16)
                key_outs[s][lower : lower + stretch_rows, HEAD:] = value_total[rows, :].astype(
                    jnp.bfloat16
                )


def sum_kernel(*refs):
    parts, pieces = refs[:3], refs[3:]
    rows = pieces[0].shape[0]
    for d in range(QUAD):
        lower = d * rows
        pieces[d][...] = sum(
            part[lower : lower + rows, :].astype(jnp.float32) for part in parts
        ).astype(jnp.bfloat16)


def key_grad_kernel(*refs):
    pieces, (key_out, value_out) = refs[:QUAD], refs[QUAD:]
    _, member = place()
    for d in range(QUAD):
        head = columns(member ^ d, HEAD)
        key_out[0, :, head] = pieces[d][:, :HEAD]
        value_out[0, :, head] = pieces[d][:, HEAD:]


def query_grad_kernel(*refs):
    pieces, out = refs[:QUAD], refs[QUAD]
    _, member = place()
    for d in range(QUAD):
        out[0, :, columns(member ^ d, pieces[d].shape[1])] = pieces[d][...]


def gate_kernel(*refs):
    pieces, (gate_ref, out) = refs[:QUAD], refs[QUAD:]
    _, member = place()
    rows = out.shape[1]
    attended = [piece[...].astype(jnp.float32) for piece in pieces]
    square = sum(jnp.sum(part * part, axis=1, keepdims=True) for part in attended)
    factor = lax.rsqrt(square / out.shape[2] + norm_eps)
    for d in range(QUAD):
        head = columns(member ^ d, pieces[d].shape[1])
        gain = sum(gate_ref[rows : rows + GAIN_ROWS, head].astype(jnp.float32)[i : i + 1] for i in range(3))
        out[0, :, head] = (
            attended[d] * factor * gain * gate_ref[:rows, head].astype(jnp.float32)
        ).astype(jnp.bfloat16)


def call(kernel, name, out_shape, specs, *args, scratch=(), flops=0, transcendentals=0, vmem=40):
    size = sum(a.size * a.dtype.itemsize for a in args)
    size += sum(math.prod(o.shape) * o.dtype.itemsize for o in out_shape)
    return pl.pallas_call(
        kernel,
        name=name,
        out_shape=out_shape,
        in_specs=specs,
        out_specs=[VMEM] * len(out_shape),
        scratch_shapes=list(scratch),
        compiler_params=pltpu.CompilerParams(vmem_limit_bytes=vmem * MIB),
        cost_estimate=pl.CostEstimate(
            flops=flops, bytes_accessed=size, transcendentals=transcendentals
        ),
    )(*args)


def body(
    query_fwd,
    key_fwd,
    value_fwd,
    gate_fwd,
    types_fwd,
    query_bwd,
    key_bwd,
    value_bwd,
    grad_out,
    types_bwd,
    type_key,
    norm_gain,
    stretch_order,
):
    devices = lax.axis_size("ctx")
    nz = devices // QUAD
    rows = query_fwd.shape[1]
    total_rows = rows * devices
    width = query_fwd.shape[2] // QUAD
    groups = width // HEAD
    stretch_rows = rows // 2
    block_rows = groups * stretch_rows
    steps = total_rows // block_rows + 1
    pairs = steps * QUAD * block_rows * block_rows

    def swap(pieces):
        return [pieces[0]] + [
            lax.ppermute(pieces[d], "ctx", [(i, i ^ d) for i in range(devices)])
            for d in range(1, QUAD)
        ]

    def turn(block, s):
        return lax.ppermute(
            block, "ctx", [(i, (i + s * QUAD) % devices) for i in range(devices)]
        )

    def hand(block, d):
        sections = lax.axis_size("pipe")
        route = [
            (i * sections + p, (i ^ d) * sections + (p + 1) % sections)
            for i in range(devices)
            for p in range(sections)
        ]
        return lax.ppermute(block, ("ctx", "pipe"), route)

    ahead = nz // 2

    def ring_up(block):
        return turn(block, 1)

    def ring_down(block):
        return turn(block, nz - 1)

    def reduce_first(parts):
        return ring_up(parts[ahead]), ring_down(parts[ahead + 1])

    def add(a, b):
        return (a.astype(jnp.float32) + b.astype(jnp.float32)).astype(jnp.bfloat16)

    def reduce_rest(parts, up, down):
        for s in range(ahead - 1, 0, -1):
            up = ring_up(add(up, parts[s]))
        for s in range(ahead + 2, nz):
            down = ring_down(add(down, parts[s]))
        return parts[0], up, down

    def gather(stack):
        return [stack] + [turn(stack, s) for s in range(1, nz)]

    def pack(key, value, types, name):
        return call(
            pack_keys,
            name,
            [bf16(rows, 2 * HEAD)] * QUAD,
            [HBM] * 4,
            key,
            value,
            types,
            type_key,
            scratch=[
                pltpu.VMEM(key.shape[1:], jnp.bfloat16),
                pltpu.VMEM(types.shape, jnp.int32),
                pltpu.VMEM(type_key.shape[1:], jnp.bfloat16),
                pltpu.VMEM(key.shape[1:], jnp.bfloat16),
                pltpu.SemaphoreType.DMA((3,)),
                pltpu.SemaphoreType.DMA((QUAD,)),
            ],
            vmem=60,
        )

    def stacked_keys(pieces, name):
        return call(
            stack_keys,
            name,
            [bf16(QUAD * rows, 2 * HEAD)],
            [HBM] * QUAD,
            *pieces,
            scratch=[pltpu.SemaphoreType.DMA((QUAD,))],
        )[0]

    back_pieces = swap(pack(key_bwd, value_bwd, types_bwd, "pack_keys_bwd"))
    packed = call(
        pack_queries,
        "pack_queries",
        [bf16(rows, 3 * width)] * QUAD + [bf16(rows + GAIN_ROWS, QUAD * width)],
        [HBM] * 4 + [VMEM],
        query_bwd,
        grad_out,
        query_fwd,
        gate_fwd,
        norm_gain,
        scratch=[pltpu.SemaphoreType.DMA((3 * QUAD + 1,))],
        vmem=60,
    )
    back_pieces, packed = lax.optimization_barrier((back_pieces, list(packed)))
    back_stacks = gather(stacked_keys(back_pieces, "stack_keys_bwd"))
    pieces = swap(pack(key_fwd, value_fwd, types_fwd, "pack_keys_fwd"))
    pieces, packed[2:QUAD] = lax.optimization_barrier((pieces, packed[2:QUAD]))
    back_stacks, packed[1] = lax.optimization_barrier((back_stacks, packed[1]))
    queries = swap(packed[:QUAD])
    stack = stacked_keys(pieces, "stack_keys_fwd")
    stack, back_stacks = lax.optimization_barrier((stack, back_stacks))
    stacks = gather(stack)
    gate_before = hand(packed[QUAD], 0)

    sequence = [pltpu.VMEM((total_rows, HEAD), jnp.bfloat16)] * 2
    stacked = pltpu.VMEM((2 * QUAD, block_rows, HEAD), jnp.bfloat16)
    gap = pltpu.VMEM((block_rows, block_rows), jnp.int32)
    outs = call(
        functools.partial(backward_kernel, nz),
        "backward",
        [bf16(rows, width)] * QUAD + [bf16(QUAD * rows, 2 * HEAD)] * nz,
        [SMEM] + [VMEM] * (QUAD + nz),
        stretch_order,
        *queries,
        *back_stacks,
        scratch=sequence
        + [
            pltpu.VMEM((total_rows // block_rows, HEAD, block_rows), jnp.bfloat16),
            stacked,
            stacked,
            pltpu.VMEM((2 * QUAD, HEAD, block_rows), jnp.float32),
            pltpu.VMEM((total_rows, HEAD), jnp.float32),
            pltpu.VMEM((total_rows, HEAD), jnp.float32),
            gap,
        ],
        flops=10 * pairs * HEAD,
        transcendentals=2 * pairs,
    )
    query_pieces, key_parts = outs[:QUAD], outs[QUAD:]
    query_pieces, key_parts, gate_before = lax.optimization_barrier(
        (query_pieces, key_parts, gate_before)
    )
    query_pieces = swap(query_pieces)
    stacks, key_parts, query_pieces = lax.optimization_barrier((stacks, key_parts, query_pieces))
    key_sums = reduce_first(key_parts)
    parts = tuple(range(QUAD))
    attended = call(
        functools.partial(forward_kernel, nz, parts),
        "forward",
        [bf16(rows, width)] * QUAD,
        [SMEM] + [VMEM] * (QUAD + nz),
        stretch_order,
        *queries,
        *stacks,
        scratch=sequence
        + [stacked, pltpu.VMEM((2 * QUAD, block_rows, HEAD), jnp.float32), gap],
    )
    attended, key_up = lax.optimization_barrier((attended, key_sums[0]))
    (handed,) = call(
        gate_kernel,
        "gate",
        [bf16(*gate_fwd.shape)],
        [VMEM] * (QUAD + 1),
        *[hand(attended[d], d) for d in range(QUAD)],
        gate_before,
    )
    key_sums = reduce_rest(key_parts, key_up, key_sums[1])
    key_pieces = swap(
        call(
            sum_kernel,
            "sum_key_parts",
            [bf16(rows, 2 * HEAD)] * QUAD,
            [VMEM] * 3,
            *key_sums,
        )
    )
    (query_grad,) = call(
        query_grad_kernel,
        "query_grad",
        [bf16(*query_bwd.shape)],
        [VMEM] * QUAD,
        *query_pieces,
    )
    key_grad, value_grad = call(
        key_grad_kernel,
        "key_grad",
        [bf16(*key_bwd.shape), bf16(*value_bwd.shape)],
        [VMEM] * QUAD,
        *key_pieces,
    )
    return handed, query_grad, key_grad, value_grad


def solution(mesh):
    rows = P("pipe", "ctx", None)
    types = P("pipe", "ctx")
    return jax.shard_map(
        body,
        mesh=mesh,
        in_specs=(
            rows,
            rows,
            rows,
            rows,
            types,
            rows,
            rows,
            rows,
            rows,
            types,
            P("pipe", None, None),
            P("pipe", None),
            P("pipe", None),
        ),
        out_specs=(rows, rows, rows, rows),
        check_vma=False,
    )
```

```python
import functools
import math

import jax
import jax.numpy as jnp
from jax import lax
from jax.experimental import pallas as pl
from jax.experimental.pallas import tpu as pltpu
from jax.sharding import PartitionSpec as P

HEAD = 128
QUAD = 4
SCALE = HEAD ** (-0.5)
EXP2_SCALE = -SCALE / math.log(2.0)
GAIN_ROWS = 16
norm_eps = 1e-06

VMEM = pl.BlockSpec(memory_space=pltpu.VMEM)
HBM = pl.BlockSpec(memory_space=pltpu.HBM)
SMEM = pl.BlockSpec(memory_space=pltpu.SMEM)
MIB = 1024 * 1024

NN = (((1,), (0,)), ((), ()))
NT = (((1,), (1,)), ((), ()))
TN = (((0,), (0,)), ((), ()))


def dot(a, b, dims):
    return lax.dot_general(a, b, dims, preferred_element_type=jnp.float32)


def bf16(*shape):
    return jax.ShapeDtypeStruct(shape, jnp.bfloat16)


def place():
    index = lax.axis_index("ctx")
    return index // QUAD, index % QUAD


def columns(index, width):
    return pl.ds(pl.multiple_of(index * width, width), width)


def pack_keys(key_ref, value_ref, types_ref, table_ref, *refs):
    pieces, (keys, types, table, typed, arrived, placed) = refs[:QUAD], refs[QUAD:]
    _, member = place()
    copies = [
        pltpu.make_async_copy(source, target, arrived.at[i])
        for i, (source, target) in enumerate(
            [(types_ref, types), (table_ref.at[0], table), (key_ref.at[0], keys)]
        )
    ]
    placements = [
        pltpu.make_async_copy(
            value_ref.at[0, :, columns(member ^ d, HEAD)], pieces[d].at[:, HEAD:], placed.at[d]
        )
        for d in range(QUAD)
    ]
    for copy in copies + placements:
        copy.start()
    for copy in copies:
        copy.wait()
    onehot = (
        lax.broadcasted_iota(jnp.int32, (table.shape[0], types.shape[1]), 0) == types[...]
    ).astype(jnp.float32).astype(jnp.bfloat16)
    type_rows = dot(onehot, table[...], TN)
    typed[...] = (keys[...].astype(jnp.float32) + type_rows).astype(jnp.bfloat16)
    for d in range(QUAD):
        pieces[d][:, :HEAD] = typed[:, columns(member ^ d, HEAD)]
    for copy in placements:
        copy.wait()


def stack_keys(*refs):
    pieces, (out, placed) = refs[:QUAD], refs[QUAD:]
    rows = pieces[0].shape[0]
    copies = [
        pltpu.make_async_copy(pieces[d], out.at[d * rows : (d + 1) * rows, :], placed.at[d])
        for d in range(QUAD)
    ]
    for copy in copies:
        copy.start()
    for copy in copies:
        copy.wait()


def pack_queries(query_ref, grad_ref, forward_ref, gate_ref, gain_ref, *refs):
    pieces, (gate_out, placed) = refs[:QUAD], refs[QUAD:]
    _, member = place()
    width = query_ref.shape[2] // QUAD
    rows = gate_ref.shape[1]
    copies = [
        pltpu.make_async_copy(
            source.at[0, :, columns(member ^ d, width)],
            pieces[d].at[:, i * width : (i + 1) * width],
            placed.at[3 * d + i],
        )
        for d in reversed(range(QUAD))
        for i, source in enumerate([query_ref, grad_ref, forward_ref])
    ]
    copies.append(
        pltpu.make_async_copy(gate_ref.at[0], gate_out.at[:rows, :], placed.at[3 * QUAD])
    )
    for copy in copies:
        copy.start()
    rest = gain_ref[...]
    parts = []
    for _ in range(3):
        part = rest.astype(jnp.bfloat16).astype(jnp.float32)
        parts.append(part)
        rest = rest - part
    parts.append(jnp.zeros((GAIN_ROWS - 3, rest.shape[1]), jnp.float32))
    gate_out[rows:, :] = jnp.concatenate(parts, axis=0).astype(jnp.bfloat16)
    for copy in copies:
        copy.wait()


def stretch_of(order_ref, quad_index, member, d, e):
    return order_ref[0, 2 * (quad_index * QUAD + (member ^ d)) + e]


def rows_at(index, count):
    return pl.ds(pl.multiple_of(index * count, count), count)


def in_sequence(order_ref, stacks, stretch_rows, keys, values):
    z, member = place()
    nz = len(stacks)
    for s, stack in enumerate(stacks):
        source = lax.rem(z - s + nz, nz)
        for d in range(QUAD):
            for e in range(2):
                rows = rows_at(stretch_of(order_ref, source, member, d, e), stretch_rows)
                lower = (2 * d + e) * stretch_rows
                keys[rows, :] = stack[lower : lower + stretch_rows, :HEAD]
                values[rows, :] = stack[lower : lower + stretch_rows, HEAD:]


def shrink_of(stretch, stretch_rows):
    pos = stretch * stretch_rows + lax.broadcasted_iota(jnp.int32, (stretch_rows, HEAD), 0)
    return lax.rsqrt((pos + 1).astype(jnp.float32))


def step_place(first, second, step, d, groups):
    blocks = first // groups + 1
    late = step >= blocks
    row = jnp.where(late, 2 * d + 1, 2 * d)
    stretch = jnp.where(late, second, first)
    block = jnp.where(late, step - blocks, step)
    return row, stretch, block


def sigmoid_of(raw, visible):
    part = pl.reciprocal(1.0 + jnp.exp2(raw * EXP2_SCALE), approx=True)
    return jnp.where(visible, part, 0.0)


def repeat(steps, together, advance):
    def several(i, _):
        for j in range(together):
            advance(i * together + j)
        return 0

    lax.fori_loop(0, steps // together, several, 0)
    for step in range(steps // together * together, steps):
        advance(step)


def forward_kernel(nz, parts, order_ref, *refs):
    queries, refs = refs[: len(parts)], refs[len(parts) :]
    stacks, refs = refs[:nz], refs[nz:]
    outs, refs = refs[: len(parts)], refs[len(parts) :]
    keys, values, stacked, total, gap = refs
    z, member = place()
    stretch_rows = queries[0].shape[0] // 2
    groups = outs[0].shape[1] // HEAD
    block_rows = groups * stretch_rows
    steps = keys.shape[0] // block_rows + 1
    in_sequence(order_ref, stacks, stretch_rows, keys, values)
    offset = 2 * groups * HEAD
    for i in range(len(parts)):
        for e in range(2):
            for g in range(groups):
                stacked[2 * i + e, g * stretch_rows : (g + 1) * stretch_rows, :] = queries[i][
                    e * stretch_rows : (e + 1) * stretch_rows,
                    offset + g * HEAD : offset + (g + 1) * HEAD,
                ]
    total[...] = jnp.zeros_like(total)
    gap[...] = lax.broadcasted_iota(jnp.int32, gap.shape, 1) - lax.rem(
        lax.broadcasted_iota(jnp.int32, gap.shape, 0), stretch_rows
    )

    def advance(step):
        for i, d in enumerate(parts):
            row, stretch, block = step_place(
                stretch_of(order_ref, z, member, d, 0),
                stretch_of(order_ref, z, member, d, 1),
                step,
                i,
                groups,
            )
            rows = rows_at(block, block_rows)
            raw = dot(stacked[row], keys[rows, :], NT)
            visible = gap[...] <= stretch * stretch_rows - block * block_rows
            weights = (raw * sigmoid_of(raw, visible)).astype(jnp.bfloat16)
            total[row] += dot(weights, values[rows, :], NN)

    repeat(steps, 9, advance)
    for i, d in enumerate(parts):
        for e in range(2):
            shrink = SCALE * shrink_of(stretch_of(order_ref, z, member, d, e), stretch_rows)
            for g in range(groups):
                outs[i][e * stretch_rows : (e + 1) * stretch_rows, g * HEAD : (g + 1) * HEAD] = (
                    total[2 * i + e, g * stretch_rows : (g + 1) * stretch_rows, :] * shrink
                ).astype(jnp.bfloat16)


def backward_kernel(nz, order_ref, *refs):
    queries, refs = refs[:QUAD], refs[QUAD:]
    stacks, refs = refs[:nz], refs[nz:]
    query_outs, refs = refs[:QUAD], refs[QUAD:]
    key_outs, refs = refs[:nz], refs[nz:]
    keys, values, keys_t, stacked, grads, total_t, key_total, value_total, gap = refs
    z, member = place()
    stretch_rows = queries[0].shape[0] // 2
    groups = query_outs[0].shape[1] // HEAD
    block_rows = groups * stretch_rows
    blocks = keys.shape[0] // block_rows
    steps = blocks + 1
    in_sequence(order_ref, stacks, stretch_rows, keys, values)
    for block in range(blocks):
        lower = block * block_rows
        keys_t[block] = keys[lower : lower + block_rows, :].T
    offset = groups * HEAD
    for d in range(QUAD):
        for e in range(2):
            shrink = shrink_of(stretch_of(order_ref, z, member, d, e), stretch_rows)
            rows = slice(e * stretch_rows, (e + 1) * stretch_rows)
            for g in range(groups):
                into = slice(g * stretch_rows, (g + 1) * stretch_rows)
                stacked[2 * d + e, into, :] = queries[d][rows, g * HEAD : (g + 1) * HEAD]
                grads[2 * d + e, into, :] = (
                    queries[d][rows, offset + g * HEAD : offset + (g + 1) * HEAD].astype(
                        jnp.float32
                    )
                    * shrink
                ).astype(jnp.bfloat16)
    total_t[...] = jnp.zeros_like(total_t)
    key_total[...] = jnp.zeros_like(key_total)
    value_total[...] = jnp.zeros_like(value_total)
    gap[...] = lax.broadcasted_iota(jnp.int32, gap.shape, 0) - lax.rem(
        lax.broadcasted_iota(jnp.int32, gap.shape, 1), stretch_rows
    )

    def advance(step):
        for d in range(QUAD):
            row, stretch, block = step_place(
                stretch_of(order_ref, z, member, d, 0),
                stretch_of(order_ref, z, member, d, 1),
                step,
                d,
                groups,
            )
            rows = rows_at(block, block_rows)
            raw = dot(keys[rows, :], stacked[row], NT)
            weight_grad = dot(values[rows, :], grads[row], NT)
            visible = gap[...] <= stretch * stretch_rows - block * block_rows
            part = sigmoid_of(raw, visible)
            weights = raw * SCALE * part
            score_grad = (weight_grad * (part + weights * (1.0 - part))).astype(jnp.bfloat16)
            weights = weights.astype(jnp.bfloat16)
            total_t[row] += dot(keys_t[block], score_grad, NN)
            key_total[rows, :] += dot(score_grad, stacked[row], NN)
            value_total[rows, :] += dot(weights, grads[row], NN)

    repeat(steps, 3, advance)
    for d in range(QUAD):
        for e in range(2):
            query_grad = (total_t[2 * d + e].T * SCALE).astype(jnp.bfloat16)
            for g in range(groups):
                query_outs[d][
                    e * stretch_rows : (e + 1) * stretch_rows, g * HEAD : (g + 1) * HEAD
                ] = query_grad[g * stretch_rows : (g + 1) * stretch_rows, :]
    for s in range(nz):
        target = lax.rem(z + s, nz)
        for d in range(QUAD):
            for e in range(2):
                rows = rows_at(stretch_of(order_ref, target, member, d, e), stretch_rows)
                lower = (2 * d + e) * stretch_rows
                key_outs[s][lower : lower + stretch_rows, :HEAD] = (
                    key_total[rows, :] * SCALE
                ).astype(jnp.bfloat16)
                key_outs[s][lower : lower + stretch_rows, HEAD:] = value_total[rows, :].astype(
                    jnp.bfloat16
                )


def sum_kernel(*refs):
    parts, pieces = refs[:3], refs[3:]
    rows = pieces[0].shape[0]
    for d in range(QUAD):
        lower = d * rows
        pieces[d][...] = sum(
            part[lower : lower + rows, :].astype(jnp.float32) for part in parts
        ).astype(jnp.bfloat16)


def key_grad_kernel(*refs):
    pieces, (key_out, value_out) = refs[:QUAD], refs[QUAD:]
    _, member = place()
    for d in range(QUAD):
        head = columns(member ^ d, HEAD)
        key_out[0, :, head] = pieces[d][:, :HEAD]
        value_out[0, :, head] = pieces[d][:, HEAD:]


def query_grad_kernel(*refs):
    pieces, out = refs[:QUAD], refs[QUAD]
    _, member = place()
    for d in range(QUAD):
        out[0, :, columns(member ^ d, pieces[d].shape[1])] = pieces[d][...]


def gate_kernel(*refs):
    pieces, (gate_ref, out) = refs[:QUAD], refs[QUAD:]
    _, member = place()
    rows = out.shape[1]
    attended = [piece[...].astype(jnp.float32) for piece in pieces]
    square = sum(jnp.sum(part * part, axis=1, keepdims=True) for part in attended)
    factor = lax.rsqrt(square / out.shape[2] + norm_eps)
    for d in range(QUAD):
        head = columns(member ^ d, pieces[d].shape[1])
        gain = sum(gate_ref[rows : rows + GAIN_ROWS, head].astype(jnp.float32)[i : i + 1] for i in range(3))
        out[0, :, head] = (
            attended[d] * factor * gain * gate_ref[:rows, head].astype(jnp.float32)
        ).astype(jnp.bfloat16)


def call(kernel, name, out_shape, specs, *args, scratch=(), flops=0, transcendentals=0, vmem=40):
    size = sum(a.size * a.dtype.itemsize for a in args)
    size += sum(math.prod(o.shape) * o.dtype.itemsize for o in out_shape)
    return pl.pallas_call(
        kernel,
        name=name,
        out_shape=out_shape,
        in_specs=specs,
        out_specs=[VMEM] * len(out_shape),
        scratch_shapes=list(scratch),
        compiler_params=pltpu.CompilerParams(vmem_limit_bytes=vmem * MIB),
        cost_estimate=pl.CostEstimate(
            flops=flops, bytes_accessed=size, transcendentals=transcendentals
        ),
    )(*args)


def body(
    query_fwd,
    key_fwd,
    value_fwd,
    gate_fwd,
    types_fwd,
    query_bwd,
    key_bwd,
    value_bwd,
    grad_out,
    types_bwd,
    type_key,
    norm_gain,
    stretch_order,
):
    devices = lax.axis_size("ctx")
    nz = devices // QUAD
    rows = query_fwd.shape[1]
    total_rows = rows * devices
    width = query_fwd.shape[2] // QUAD
    groups = width // HEAD
    stretch_rows = rows // 2
    block_rows = groups * stretch_rows
    steps = total_rows // block_rows + 1
    pairs = steps * QUAD * block_rows * block_rows

    def swap_one(piece, d):
        return lax.ppermute(piece, "ctx", [(i, i ^ d) for i in range(devices)])

    def swap(pieces):
        return [pieces[0]] + [swap_one(pieces[d], d) for d in range(1, QUAD)]

    def turn(block, s):
        return lax.ppermute(
            block, "ctx", [(i, (i + s * QUAD) % devices) for i in range(devices)]
        )

    def hand(block, d):
        sections = lax.axis_size("pipe")
        route = [
            (i * sections + p, (i ^ d) * sections + (p + 1) % sections)
            for i in range(devices)
            for p in range(sections)
        ]
        return lax.ppermute(block, ("ctx", "pipe"), route)

    ahead = nz // 2

    def ring_up(block):
        return turn(block, 1)

    def ring_down(block):
        return turn(block, nz - 1)

    def reduce_first(parts):
        return ring_up(parts[ahead]), ring_down(parts[ahead + 1])

    def add(a, b):
        return (a.astype(jnp.float32) + b.astype(jnp.float32)).astype(jnp.bfloat16)

    def reduce_rest(parts, up, down):
        for s in range(ahead - 1, 0, -1):
            up = ring_up(add(up, parts[s]))
        for s in range(ahead + 2, nz):
            down = ring_down(add(down, parts[s]))
        return parts[0], up, down

    def gather(stack):
        return [stack] + [turn(stack, s) for s in range(1, nz)]

    def pack(key, value, types, name):
        return call(
            pack_keys,
            name,
            [bf16(rows, 2 * HEAD)] * QUAD,
            [HBM] * 4,
            key,
            value,
            types,
            type_key,
            scratch=[
                pltpu.VMEM(key.shape[1:], jnp.bfloat16),
                pltpu.VMEM(types.shape, jnp.int32),
                pltpu.VMEM(type_key.shape[1:], jnp.bfloat16),
                pltpu.VMEM(key.shape[1:], jnp.bfloat16),
                pltpu.SemaphoreType.DMA((3,)),
                pltpu.SemaphoreType.DMA((QUAD,)),
            ],
            vmem=60,
        )

    def stacked_keys(pieces, name):
        return call(
            stack_keys,
            name,
            [bf16(QUAD * rows, 2 * HEAD)],
            [HBM] * QUAD,
            *pieces,
            scratch=[pltpu.SemaphoreType.DMA((QUAD,))],
        )[0]

    back_pieces = swap(pack(key_bwd, value_bwd, types_bwd, "pack_keys_bwd"))
    packed = call(
        pack_queries,
        "pack_queries",
        [bf16(rows, 3 * width)] * QUAD + [bf16(rows + GAIN_ROWS, QUAD * width)],
        [HBM] * 4 + [VMEM],
        query_bwd,
        grad_out,
        query_fwd,
        gate_fwd,
        norm_gain,
        scratch=[pltpu.SemaphoreType.DMA((3 * QUAD + 1,))],
        vmem=60,
    )
    back_pieces, packed = lax.optimization_barrier((back_pieces, list(packed)))
    back_stacks = gather(stacked_keys(back_pieces, "stack_keys_bwd"))
    pieces = swap(pack(key_fwd, value_fwd, types_fwd, "pack_keys_fwd"))
    pieces, packed[2:QUAD] = lax.optimization_barrier((pieces, packed[2:QUAD]))
    back_stacks, packed[1] = lax.optimization_barrier((back_stacks, packed[1]))
    queries = swap(packed[:QUAD])
    stack = stacked_keys(pieces, "stack_keys_fwd")
    stack, back_stacks = lax.optimization_barrier((stack, back_stacks))
    stacks = gather(stack)
    gate_before = hand(packed[QUAD], 0)

    sequence = [pltpu.VMEM((total_rows, HEAD), jnp.bfloat16)] * 2
    stacked = pltpu.VMEM((2 * QUAD, block_rows, HEAD), jnp.bfloat16)
    gap = pltpu.VMEM((block_rows, block_rows), jnp.int32)
    outs = call(
        functools.partial(backward_kernel, nz),
        "backward",
        [bf16(rows, width)] * QUAD + [bf16(QUAD * rows, 2 * HEAD)] * nz,
        [SMEM] + [VMEM] * (QUAD + nz),
        stretch_order,
        *queries,
        *back_stacks,
        scratch=sequence
        + [
            pltpu.VMEM((total_rows // block_rows, HEAD, block_rows), jnp.bfloat16),
            stacked,
            stacked,
            pltpu.VMEM((2 * QUAD, HEAD, block_rows), jnp.float32),
            pltpu.VMEM((total_rows, HEAD), jnp.float32),
            pltpu.VMEM((total_rows, HEAD), jnp.float32),
            gap,
        ],
        flops=10 * pairs * HEAD,
        transcendentals=2 * pairs,
    )
    query_pieces, key_parts = outs[:QUAD], outs[QUAD:]
    query_pieces, key_parts, gate_before = lax.optimization_barrier(
        (query_pieces, key_parts, gate_before)
    )
    query_pieces = list(query_pieces)
    query_pieces[2:] = [swap_one(query_pieces[d], d) for d in range(2, QUAD)]
    stacks, key_parts = lax.optimization_barrier((stacks, key_parts))
    key_sums = reduce_first(key_parts)
    parts = tuple(range(QUAD))
    attended = call(
        functools.partial(forward_kernel, nz, parts),
        "forward",
        [bf16(rows, width)] * QUAD,
        [SMEM] + [VMEM] * (QUAD + nz),
        stretch_order,
        *queries,
        *stacks,
        scratch=sequence
        + [stacked, pltpu.VMEM((2 * QUAD, block_rows, HEAD), jnp.float32), gap],
    )
    attended, key_up, query_pieces = lax.optimization_barrier(
        (attended, key_sums[0], query_pieces)
    )
    query_pieces[1] = swap_one(query_pieces[1], 1)
    (handed,) = call(
        gate_kernel,
        "gate",
        [bf16(*gate_fwd.shape)],
        [VMEM] * (QUAD + 1),
        *[hand(attended[d], d) for d in range(QUAD)],
        gate_before,
    )
    key_sums = reduce_rest(key_parts, key_up, key_sums[1])
    key_pieces = swap(
        call(
            sum_kernel,
            "sum_key_parts",
            [bf16(rows, 2 * HEAD)] * QUAD,
            [VMEM] * 3,
            *key_sums,
        )
    )
    (query_grad,) = call(
        query_grad_kernel,
        "query_grad",
        [bf16(*query_bwd.shape)],
        [VMEM] * QUAD,
        *query_pieces,
    )
    key_grad, value_grad = call(
        key_grad_kernel,
        "key_grad",
        [bf16(*key_bwd.shape), bf16(*value_bwd.shape)],
        [VMEM] * QUAD,
        *key_pieces,
    )
    return handed, query_grad, key_grad, value_grad


def solution(mesh):
    rows = P("pipe", "ctx", None)
    types = P("pipe", "ctx")
    return jax.shard_map(
        body,
        mesh=mesh,
        in_specs=(
            rows,
            rows,
            rows,
            rows,
            types,
            rows,
            rows,
            rows,
            rows,
            types,
            P("pipe", None, None),
            P("pipe", None),
            P("pipe", None),
        ),
        out_specs=(rows, rows, rows, rows),
        check_vma=False,
    )
```

```python
import functools
import math

import jax
import jax.numpy as jnp
from jax import lax
from jax.experimental import pallas as pl
from jax.experimental.pallas import tpu as pltpu
from jax.sharding import PartitionSpec as P

HEAD = 128
QUAD = 4
SCALE = HEAD ** (-0.5)
EXP2_SCALE = -SCALE / math.log(2.0)
GAIN_ROWS = 16
norm_eps = 1e-06

VMEM = pl.BlockSpec(memory_space=pltpu.VMEM)
HBM = pl.BlockSpec(memory_space=pltpu.HBM)
SMEM = pl.BlockSpec(memory_space=pltpu.SMEM)
MIB = 1024 * 1024

NN = (((1,), (0,)), ((), ()))
NT = (((1,), (1,)), ((), ()))
TN = (((0,), (0,)), ((), ()))


def dot(a, b, dims):
    return lax.dot_general(a, b, dims, preferred_element_type=jnp.float32)


def bf16(*shape):
    return jax.ShapeDtypeStruct(shape, jnp.bfloat16)


def place():
    index = lax.axis_index("ctx")
    return index // QUAD, index % QUAD


def columns(index, width):
    return pl.ds(pl.multiple_of(index * width, width), width)


def pack_keys(key_ref, value_ref, types_ref, table_ref, *refs):
    pieces, (keys, types, table, typed, arrived, placed) = refs[:QUAD], refs[QUAD:]
    _, member = place()
    copies = [
        pltpu.make_async_copy(source, target, arrived.at[i])
        for i, (source, target) in enumerate(
            [(types_ref, types), (table_ref.at[0], table), (key_ref.at[0], keys)]
        )
    ]
    placements = [
        pltpu.make_async_copy(
            value_ref.at[0, :, columns(member ^ d, HEAD)], pieces[d].at[:, HEAD:], placed.at[d]
        )
        for d in range(QUAD)
    ]
    for copy in copies + placements:
        copy.start()
    for copy in copies:
        copy.wait()
    onehot = (
        lax.broadcasted_iota(jnp.int32, (table.shape[0], types.shape[1]), 0) == types[...]
    ).astype(jnp.float32).astype(jnp.bfloat16)
    type_rows = dot(onehot, table[...], TN)
    typed[...] = (keys[...].astype(jnp.float32) + type_rows).astype(jnp.bfloat16)
    for d in range(QUAD):
        pieces[d][:, :HEAD] = typed[:, columns(member ^ d, HEAD)]
    for copy in placements:
        copy.wait()


def stack_keys(*refs):
    pieces, (out, placed) = refs[:QUAD], refs[QUAD:]
    rows = pieces[0].shape[0]
    copies = [
        pltpu.make_async_copy(pieces[d], out.at[d * rows : (d + 1) * rows, :], placed.at[d])
        for d in range(QUAD)
    ]
    for copy in copies:
        copy.start()
    for copy in copies:
        copy.wait()


def pack_queries(query_ref, grad_ref, forward_ref, gate_ref, gain_ref, *refs):
    pieces, (gate_out, placed) = refs[:QUAD], refs[QUAD:]
    _, member = place()
    width = query_ref.shape[2] // QUAD
    rows = gate_ref.shape[1]
    copies = [
        pltpu.make_async_copy(
            source.at[0, :, columns(member ^ d, width)],
            pieces[d].at[:, i * width : (i + 1) * width],
            placed.at[3 * d + i],
        )
        for d in reversed(range(QUAD))
        for i, source in enumerate([query_ref, grad_ref, forward_ref])
    ]
    copies.append(
        pltpu.make_async_copy(gate_ref.at[0], gate_out.at[:rows, :], placed.at[3 * QUAD])
    )
    for copy in copies:
        copy.start()
    rest = gain_ref[...]
    parts = []
    for _ in range(3):
        part = rest.astype(jnp.bfloat16).astype(jnp.float32)
        parts.append(part)
        rest = rest - part
    parts.append(jnp.zeros((GAIN_ROWS - 3, rest.shape[1]), jnp.float32))
    gate_out[rows:, :] = jnp.concatenate(parts, axis=0).astype(jnp.bfloat16)
    for copy in copies:
        copy.wait()


def stretch_of(order_ref, quad_index, member, d, e):
    return order_ref[0, 2 * (quad_index * QUAD + (member ^ d)) + e]


def rows_at(index, count):
    return pl.ds(pl.multiple_of(index * count, count), count)


def in_sequence(order_ref, stacks, stretch_rows, keys, values):
    z, member = place()
    nz = len(stacks)
    for s, stack in enumerate(stacks):
        source = lax.rem(z - s + nz, nz)
        for d in range(QUAD):
            for e in range(2):
                rows = rows_at(stretch_of(order_ref, source, member, d, e), stretch_rows)
                lower = (2 * d + e) * stretch_rows
                keys[rows, :] = stack[lower : lower + stretch_rows, :HEAD]
                values[rows, :] = stack[lower : lower + stretch_rows, HEAD:]


def shrink_of(stretch, stretch_rows):
    pos = stretch * stretch_rows + lax.broadcasted_iota(jnp.int32, (stretch_rows, HEAD), 0)
    return lax.rsqrt((pos + 1).astype(jnp.float32))


def step_place(first, second, step, d, groups):
    blocks = first // groups + 1
    late = step >= blocks
    row = jnp.where(late, 2 * d + 1, 2 * d)
    stretch = jnp.where(late, second, first)
    block = jnp.where(late, step - blocks, step)
    return row, stretch, block


def sigmoid_of(raw, visible):
    part = pl.reciprocal(1.0 + jnp.exp2(raw * EXP2_SCALE), approx=True)
    return jnp.where(visible, part, 0.0)


def repeat(steps, together, advance):
    def several(i, _):
        for j in range(together):
            advance(i * together + j)
        return 0

    lax.fori_loop(0, steps // together, several, 0)
    for step in range(steps // together * together, steps):
        advance(step)


def forward_kernel(nz, parts, order_ref, *refs):
    queries, refs = refs[: len(parts)], refs[len(parts) :]
    stacks, refs = refs[:nz], refs[nz:]
    outs, refs = refs[: len(parts)], refs[len(parts) :]
    keys, values, stacked, total, gap = refs
    z, member = place()
    stretch_rows = queries[0].shape[0] // 2
    groups = outs[0].shape[1] // HEAD
    block_rows = groups * stretch_rows
    steps = keys.shape[0] // block_rows + 1
    in_sequence(order_ref, stacks, stretch_rows, keys, values)
    offset = 2 * groups * HEAD
    for i in range(len(parts)):
        for e in range(2):
            for g in range(groups):
                stacked[2 * i + e, g * stretch_rows : (g + 1) * stretch_rows, :] = queries[i][
                    e * stretch_rows : (e + 1) * stretch_rows,
                    offset + g * HEAD : offset + (g + 1) * HEAD,
                ]
    total[...] = jnp.zeros_like(total)
    gap[...] = lax.broadcasted_iota(jnp.int32, gap.shape, 1) - lax.rem(
        lax.broadcasted_iota(jnp.int32, gap.shape, 0), stretch_rows
    )

    def advance(step):
        for i, d in enumerate(parts):
            row, stretch, block = step_place(
                stretch_of(order_ref, z, member, d, 0),
                stretch_of(order_ref, z, member, d, 1),
                step,
                i,
                groups,
            )
            rows = rows_at(block, block_rows)
            raw = dot(stacked[row], keys[rows, :], NT)
            visible = gap[...] <= stretch * stretch_rows - block * block_rows
            weights = (raw * sigmoid_of(raw, visible)).astype(jnp.bfloat16)
            total[row] += dot(weights, values[rows, :], NN)

    repeat(steps, 9, advance)
    for i, d in enumerate(parts):
        for e in range(2):
            shrink = SCALE * shrink_of(stretch_of(order_ref, z, member, d, e), stretch_rows)
            for g in range(groups):
                outs[i][e * stretch_rows : (e + 1) * stretch_rows, g * HEAD : (g + 1) * HEAD] = (
                    total[2 * i + e, g * stretch_rows : (g + 1) * stretch_rows, :] * shrink
                ).astype(jnp.bfloat16)


def backward_kernel(nz, order_ref, *refs):
    queries, refs = refs[:QUAD], refs[QUAD:]
    stacks, refs = refs[:nz], refs[nz:]
    query_outs, refs = refs[:QUAD], refs[QUAD:]
    key_outs, refs = refs[:nz], refs[nz:]
    keys, values, keys_t, stacked, grads, total_t, key_total, value_total, gap = refs
    z, member = place()
    stretch_rows = queries[0].shape[0] // 2
    groups = query_outs[0].shape[1] // HEAD
    block_rows = groups * stretch_rows
    blocks = keys.shape[0] // block_rows
    steps = blocks + 1
    in_sequence(order_ref, stacks, stretch_rows, keys, values)
    for block in range(blocks):
        lower = block * block_rows
        keys_t[block] = keys[lower : lower + block_rows, :].T
    offset = groups * HEAD
    for d in range(QUAD):
        for e in range(2):
            shrink = shrink_of(stretch_of(order_ref, z, member, d, e), stretch_rows)
            rows = slice(e * stretch_rows, (e + 1) * stretch_rows)
            for g in range(groups):
                into = slice(g * stretch_rows, (g + 1) * stretch_rows)
                stacked[2 * d + e, into, :] = queries[d][rows, g * HEAD : (g + 1) * HEAD]
                grads[2 * d + e, into, :] = (
                    queries[d][rows, offset + g * HEAD : offset + (g + 1) * HEAD].astype(
                        jnp.float32
                    )
                    * shrink
                ).astype(jnp.bfloat16)
    total_t[...] = jnp.zeros_like(total_t)
    key_total[...] = jnp.zeros_like(key_total)
    value_total[...] = jnp.zeros_like(value_total)
    gap[...] = lax.broadcasted_iota(jnp.int32, gap.shape, 0) - lax.rem(
        lax.broadcasted_iota(jnp.int32, gap.shape, 1), stretch_rows
    )

    def advance(step):
        for d in range(QUAD):
            row, stretch, block = step_place(
                stretch_of(order_ref, z, member, d, 0),
                stretch_of(order_ref, z, member, d, 1),
                step,
                d,
                groups,
            )
            rows = rows_at(block, block_rows)
            raw = dot(keys[rows, :], stacked[row], NT)
            weight_grad = dot(values[rows, :], grads[row], NT)
            visible = gap[...] <= stretch * stretch_rows - block * block_rows
            part = sigmoid_of(raw, visible)
            weights = raw * SCALE * part
            score_grad = (weight_grad * (part + weights * (1.0 - part))).astype(jnp.bfloat16)
            weights = weights.astype(jnp.bfloat16)
            total_t[row] += dot(keys_t[block], score_grad, NN)
            key_total[rows, :] += dot(score_grad, stacked[row], NN)
            value_total[rows, :] += dot(weights, grads[row], NN)

    repeat(steps, 3, advance)
    for d in range(QUAD):
        for e in range(2):
            query_grad = (total_t[2 * d + e].T * SCALE).astype(jnp.bfloat16)
            for g in range(groups):
                query_outs[d][
                    e * stretch_rows : (e + 1) * stretch_rows, g * HEAD : (g + 1) * HEAD
                ] = query_grad[g * stretch_rows : (g + 1) * stretch_rows, :]
    for s in range(nz):
        target = lax.rem(z + s, nz)
        for d in range(QUAD):
            for e in range(2):
                rows = rows_at(stretch_of(order_ref, target, member, d, e), stretch_rows)
                lower = (2 * d + e) * stretch_rows
                key_outs[s][lower : lower + stretch_rows, :HEAD] = (
                    key_total[rows, :] * SCALE
                ).astype(jnp.bfloat16)
                key_outs[s][lower : lower + stretch_rows, HEAD:] = value_total[rows, :].astype(
                    jnp.bfloat16
                )


def sum_kernel(*refs):
    parts, pieces = refs[:3], refs[3:]
    rows = pieces[0].shape[0]
    for d in range(QUAD):
        lower = d * rows
        pieces[d][...] = sum(
            part[lower : lower + rows, :].astype(jnp.float32) for part in parts
        ).astype(jnp.bfloat16)


def key_grad_kernel(*refs):
    pieces, (key_out, value_out) = refs[:QUAD], refs[QUAD:]
    _, member = place()
    for d in range(QUAD):
        head = columns(member ^ d, HEAD)
        key_out[0, :, head] = pieces[d][:, :HEAD]
        value_out[0, :, head] = pieces[d][:, HEAD:]


def query_grad_kernel(*refs):
    pieces, out = refs[:QUAD], refs[QUAD]
    _, member = place()
    for d in range(QUAD):
        out[0, :, columns(member ^ d, pieces[d].shape[1])] = pieces[d][...]


def gate_kernel(*refs):
    pieces, (gate_ref, out) = refs[:QUAD], refs[QUAD:]
    _, member = place()
    rows = out.shape[1]
    attended = [piece[...].astype(jnp.float32) for piece in pieces]
    square = sum(jnp.sum(part * part, axis=1, keepdims=True) for part in attended)
    factor = lax.rsqrt(square / out.shape[2] + norm_eps)
    for d in range(QUAD):
        head = columns(member ^ d, pieces[d].shape[1])
        gain = sum(gate_ref[rows : rows + GAIN_ROWS, head].astype(jnp.float32)[i : i + 1] for i in range(3))
        out[0, :, head] = (
            attended[d] * factor * gain * gate_ref[:rows, head].astype(jnp.float32)
        ).astype(jnp.bfloat16)


def call(kernel, name, out_shape, specs, *args, scratch=(), flops=0, transcendentals=0, vmem=40):
    size = sum(a.size * a.dtype.itemsize for a in args)
    size += sum(math.prod(o.shape) * o.dtype.itemsize for o in out_shape)
    return pl.pallas_call(
        kernel,
        name=name,
        out_shape=out_shape,
        in_specs=specs,
        out_specs=[VMEM] * len(out_shape),
        scratch_shapes=list(scratch),
        compiler_params=pltpu.CompilerParams(vmem_limit_bytes=vmem * MIB),
        cost_estimate=pl.CostEstimate(
            flops=flops, bytes_accessed=size, transcendentals=transcendentals
        ),
    )(*args)


def body(
    query_fwd,
    key_fwd,
    value_fwd,
    gate_fwd,
    types_fwd,
    query_bwd,
    key_bwd,
    value_bwd,
    grad_out,
    types_bwd,
    type_key,
    norm_gain,
    stretch_order,
):
    devices = lax.axis_size("ctx")
    nz = devices // QUAD
    rows = query_fwd.shape[1]
    total_rows = rows * devices
    width = query_fwd.shape[2] // QUAD
    groups = width // HEAD
    stretch_rows = rows // 2
    block_rows = groups * stretch_rows
    steps = total_rows // block_rows + 1
    pairs = steps * QUAD * block_rows * block_rows

    def swap_one(piece, d):
        return lax.ppermute(piece, "ctx", [(i, i ^ d) for i in range(devices)])

    def swap(pieces):
        return [pieces[0]] + [swap_one(pieces[d], d) for d in range(1, QUAD)]

    def turn(block, s):
        return lax.ppermute(
            block, "ctx", [(i, (i + s * QUAD) % devices) for i in range(devices)]
        )

    def hand(block, d):
        sections = lax.axis_size("pipe")
        route = [
            (i * sections + p, (i ^ d) * sections + (p + 1) % sections)
            for i in range(devices)
            for p in range(sections)
        ]
        return lax.ppermute(block, ("ctx", "pipe"), route)

    ahead = nz // 2

    def ring_up(block):
        return turn(block, 1)

    def ring_down(block):
        return turn(block, nz - 1)

    def reduce_first(parts):
        return ring_up(parts[ahead]), ring_down(parts[ahead + 1])

    def add(a, b):
        return (a.astype(jnp.float32) + b.astype(jnp.float32)).astype(jnp.bfloat16)

    def reduce_rest(parts, up, down):
        for s in range(ahead - 1, 0, -1):
            up = ring_up(add(up, parts[s]))
        for s in range(ahead + 2, nz):
            down = ring_down(add(down, parts[s]))
        return parts[0], up, down

    def gather(stack):
        return [stack] + [turn(stack, s) for s in range(1, nz)]

    def gather_ring(up):
        down = [ring_down(up[0])]
        while len(up) <= ahead:
            up.append(ring_up(up[-1]))
        while len(up) + len(down) < nz:
            down.append(ring_down(down[-1]))
        return up + down[::-1]

    def pack(key, value, types, name):
        return call(
            pack_keys,
            name,
            [bf16(rows, 2 * HEAD)] * QUAD,
            [HBM] * 4,
            key,
            value,
            types,
            type_key,
            scratch=[
                pltpu.VMEM(key.shape[1:], jnp.bfloat16),
                pltpu.VMEM(types.shape, jnp.int32),
                pltpu.VMEM(type_key.shape[1:], jnp.bfloat16),
                pltpu.VMEM(key.shape[1:], jnp.bfloat16),
                pltpu.SemaphoreType.DMA((3,)),
                pltpu.SemaphoreType.DMA((QUAD,)),
            ],
            vmem=60,
        )

    def stacked_keys(pieces, name):
        return call(
            stack_keys,
            name,
            [bf16(QUAD * rows, 2 * HEAD)],
            [HBM] * QUAD,
            *pieces,
            scratch=[pltpu.SemaphoreType.DMA((QUAD,))],
        )[0]

    back_pieces = swap(pack(key_bwd, value_bwd, types_bwd, "pack_keys_bwd"))
    pieces = pack(key_fwd, value_fwd, types_fwd, "pack_keys_fwd")
    back_pieces, pieces = lax.optimization_barrier((back_pieces, pieces))
    pieces = swap(pieces)
    packed = call(
        pack_queries,
        "pack_queries",
        [bf16(rows, 3 * width)] * QUAD + [bf16(rows + GAIN_ROWS, QUAD * width)],
        [HBM] * 4 + [VMEM],
        query_bwd,
        grad_out,
        query_fwd,
        gate_fwd,
        norm_gain,
        scratch=[pltpu.SemaphoreType.DMA((3 * QUAD + 1,))],
        vmem=60,
    )
    packed = list(packed)
    back_stack = stacked_keys(back_pieces, "stack_keys_bwd")
    up = [back_stack, ring_up(back_stack)]
    up, pieces, packed = lax.optimization_barrier((up, pieces, packed))
    back_stacks = gather_ring(up)
    stack = stacked_keys(pieces, "stack_keys_fwd")
    back_stacks, stack, packed[1], packed[QUAD] = lax.optimization_barrier(
        (back_stacks, stack, packed[1], packed[QUAD])
    )
    queries = swap(packed[:QUAD])
    stacks = gather(stack)
    gate_before = hand(packed[QUAD], 0)

    sequence = [pltpu.VMEM((total_rows, HEAD), jnp.bfloat16)] * 2
    stacked = pltpu.VMEM((2 * QUAD, block_rows, HEAD), jnp.bfloat16)
    gap = pltpu.VMEM((block_rows, block_rows), jnp.int32)
    outs = call(
        functools.partial(backward_kernel, nz),
        "backward",
        [bf16(rows, width)] * QUAD + [bf16(QUAD * rows, 2 * HEAD)] * nz,
        [SMEM] + [VMEM] * (QUAD + nz),
        stretch_order,
        *queries,
        *back_stacks,
        scratch=sequence
        + [
            pltpu.VMEM((total_rows // block_rows, HEAD, block_rows), jnp.bfloat16),
            stacked,
            stacked,
            pltpu.VMEM((2 * QUAD, HEAD, block_rows), jnp.float32),
            pltpu.VMEM((total_rows, HEAD), jnp.float32),
            pltpu.VMEM((total_rows, HEAD), jnp.float32),
            gap,
        ],
        flops=10 * pairs * HEAD,
        transcendentals=2 * pairs,
    )
    query_pieces, key_parts = outs[:QUAD], outs[QUAD:]
    query_pieces, key_parts, gate_before = lax.optimization_barrier(
        (query_pieces, key_parts, gate_before)
    )
    query_pieces = list(query_pieces)
    query_pieces[2:] = [swap_one(query_pieces[d], d) for d in range(2, QUAD)]
    stacks, key_parts = lax.optimization_barrier((stacks, key_parts))
    key_sums = reduce_first(key_parts)
    parts = tuple(range(QUAD))
    attended = call(
        functools.partial(forward_kernel, nz, parts),
        "forward",
        [bf16(rows, width)] * QUAD,
        [SMEM] + [VMEM] * (QUAD + nz),
        stretch_order,
        *queries,
        *stacks,
        scratch=sequence
        + [stacked, pltpu.VMEM((2 * QUAD, block_rows, HEAD), jnp.float32), gap],
    )
    attended, key_up, query_pieces = lax.optimization_barrier(
        (attended, key_sums[0], query_pieces)
    )
    attended = [hand(attended[d], d) for d in range(QUAD)]
    attended[0], query_pieces[1] = lax.optimization_barrier((attended[0], query_pieces[1]))
    query_pieces[1] = swap_one(query_pieces[1], 1)
    (handed,) = call(
        gate_kernel,
        "gate",
        [bf16(*gate_fwd.shape)],
        [VMEM] * (QUAD + 1),
        *attended,
        gate_before,
    )
    key_sums = reduce_rest(key_parts, key_up, key_sums[1])
    key_pieces = swap(
        call(
            sum_kernel,
            "sum_key_parts",
            [bf16(rows, 2 * HEAD)] * QUAD,
            [VMEM] * 3,
            *key_sums,
        )
    )
    (query_grad,) = call(
        query_grad_kernel,
        "query_grad",
        [bf16(*query_bwd.shape)],
        [VMEM] * QUAD,
        *query_pieces,
    )
    key_grad, value_grad = call(
        key_grad_kernel,
        "key_grad",
        [bf16(*key_bwd.shape), bf16(*value_bwd.shape)],
        [VMEM] * QUAD,
        *key_pieces,
    )
    return handed, query_grad, key_grad, value_grad


def solution(mesh):
    rows = P("pipe", "ctx", None)
    types = P("pipe", "ctx")
    return jax.shard_map(
        body,
        mesh=mesh,
        in_specs=(
            rows,
            rows,
            rows,
            rows,
            types,
            rows,
            rows,
            rows,
            rows,
            types,
            P("pipe", None, None),
            P("pipe", None),
            P("pipe", None),
        ),
        out_specs=(rows, rows, rows, rows),
        check_vma=False,
    )
```

```python
import functools
import math

import jax
import jax.numpy as jnp
from jax import lax
from jax.experimental import pallas as pl
from jax.experimental.pallas import tpu as pltpu
from jax.sharding import PartitionSpec as P

HEAD = 128
QUAD = 4
SCALE = HEAD ** (-0.5)
EXP2_SCALE = -SCALE / math.log(2.0)
GAIN_ROWS = 16
norm_eps = 1e-06

VMEM = pl.BlockSpec(memory_space=pltpu.VMEM)
HBM = pl.BlockSpec(memory_space=pltpu.HBM)
SMEM = pl.BlockSpec(memory_space=pltpu.SMEM)
MIB = 1024 * 1024

NN = (((1,), (0,)), ((), ()))
NT = (((1,), (1,)), ((), ()))
TN = (((0,), (0,)), ((), ()))


def dot(a, b, dims):
    return lax.dot_general(a, b, dims, preferred_element_type=jnp.float32)


def bf16(*shape):
    return jax.ShapeDtypeStruct(shape, jnp.bfloat16)


def place():
    index = lax.axis_index("ctx")
    return index // QUAD, index % QUAD


def columns(index, width):
    return pl.ds(pl.multiple_of(index * width, width), width)


def pack_keys(key_ref, value_ref, types_ref, table_ref, *refs):
    pieces, (keys, types, table, typed, arrived, placed) = refs[:QUAD], refs[QUAD:]
    _, member = place()
    copies = [
        pltpu.make_async_copy(source, target, arrived.at[i])
        for i, (source, target) in enumerate(
            [(types_ref, types), (table_ref.at[0], table), (key_ref.at[0], keys)]
        )
    ]
    placements = [
        pltpu.make_async_copy(
            value_ref.at[0, :, columns(member ^ d, HEAD)], pieces[d].at[:, HEAD:], placed.at[d]
        )
        for d in range(QUAD)
    ]
    for copy in copies + placements:
        copy.start()
    for copy in copies:
        copy.wait()
    onehot = (
        lax.broadcasted_iota(jnp.int32, (table.shape[0], types.shape[1]), 0) == types[...]
    ).astype(jnp.float32).astype(jnp.bfloat16)
    type_rows = dot(onehot, table[...], TN)
    typed[...] = (keys[...].astype(jnp.float32) + type_rows).astype(jnp.bfloat16)
    for d in range(QUAD):
        pieces[d][:, :HEAD] = typed[:, columns(member ^ d, HEAD)]
    for copy in placements:
        copy.wait()


def stack_keys(*refs):
    pieces, (out, placed) = refs[:QUAD], refs[QUAD:]
    rows = pieces[0].shape[0]
    copies = [
        pltpu.make_async_copy(pieces[d], out.at[d * rows : (d + 1) * rows, :], placed.at[d])
        for d in range(QUAD)
    ]
    for copy in copies:
        copy.start()
    for copy in copies:
        copy.wait()


def pack_queries(query_ref, grad_ref, forward_ref, gate_ref, gain_ref, *refs):
    pieces, (gate_out, placed) = refs[:QUAD], refs[QUAD:]
    _, member = place()
    width = query_ref.shape[2] // QUAD
    rows = gate_ref.shape[1]
    copies = [
        pltpu.make_async_copy(
            source.at[0, :, columns(member ^ d, width)],
            pieces[d].at[:, i * width : (i + 1) * width],
            placed.at[3 * d + i],
        )
        for d in reversed(range(QUAD))
        for i, source in enumerate([query_ref, grad_ref, forward_ref])
    ]
    copies.append(
        pltpu.make_async_copy(gate_ref.at[0], gate_out.at[:rows, :], placed.at[3 * QUAD])
    )
    for copy in copies:
        copy.start()
    rest = gain_ref[...]
    parts = []
    for _ in range(3):
        part = rest.astype(jnp.bfloat16).astype(jnp.float32)
        parts.append(part)
        rest = rest - part
    parts.append(jnp.zeros((GAIN_ROWS - 3, rest.shape[1]), jnp.float32))
    gate_out[rows:, :] = jnp.concatenate(parts, axis=0).astype(jnp.bfloat16)
    for copy in copies:
        copy.wait()


def stretch_of(order_ref, quad_index, member, d, e):
    return order_ref[0, 2 * (quad_index * QUAD + (member ^ d)) + e]


def rows_at(index, count):
    return pl.ds(pl.multiple_of(index * count, count), count)


def in_sequence(order_ref, stacks, stretch_rows, keys, values):
    z, member = place()
    nz = len(stacks)
    for s, stack in enumerate(stacks):
        source = lax.rem(z - s + nz, nz)
        for d in range(QUAD):
            for e in range(2):
                rows = rows_at(stretch_of(order_ref, source, member, d, e), stretch_rows)
                lower = (2 * d + e) * stretch_rows
                keys[rows, :] = stack[lower : lower + stretch_rows, :HEAD]
                values[rows, :] = stack[lower : lower + stretch_rows, HEAD:]


def shrink_of(stretch, stretch_rows):
    pos = stretch * stretch_rows + lax.broadcasted_iota(jnp.int32, (stretch_rows, HEAD), 0)
    return lax.rsqrt((pos + 1).astype(jnp.float32))


def step_place(first, second, step, d, groups):
    blocks = first // groups + 1
    late = step >= blocks
    row = jnp.where(late, 2 * d + 1, 2 * d)
    stretch = jnp.where(late, second, first)
    block = jnp.where(late, step - blocks, step)
    return row, stretch, block


def sigmoid_of(raw, visible):
    part = pl.reciprocal(1.0 + jnp.exp2(raw * EXP2_SCALE), approx=True)
    return jnp.where(visible, part, 0.0)


def repeat(steps, together, advance):
    def several(i, _):
        for j in range(together):
            advance(i * together + j)
        return 0

    lax.fori_loop(0, steps // together, several, 0)
    for step in range(steps // together * together, steps):
        advance(step)


def forward_kernel(nz, parts, order_ref, *refs):
    queries, refs = refs[: len(parts)], refs[len(parts) :]
    stacks, refs = refs[:nz], refs[nz:]
    outs, refs = refs[: len(parts)], refs[len(parts) :]
    keys, values, stacked, total, gap = refs
    z, member = place()
    stretch_rows = queries[0].shape[0] // 2
    groups = outs[0].shape[1] // HEAD
    block_rows = groups * stretch_rows
    steps = keys.shape[0] // block_rows + 1
    in_sequence(order_ref, stacks, stretch_rows, keys, values)
    offset = 2 * groups * HEAD
    for i in range(len(parts)):
        for e in range(2):
            for g in range(groups):
                stacked[2 * i + e, g * stretch_rows : (g + 1) * stretch_rows, :] = queries[i][
                    e * stretch_rows : (e + 1) * stretch_rows,
                    offset + g * HEAD : offset + (g + 1) * HEAD,
                ]
    total[...] = jnp.zeros_like(total)
    gap[...] = lax.broadcasted_iota(jnp.int32, gap.shape, 1) - lax.rem(
        lax.broadcasted_iota(jnp.int32, gap.shape, 0), stretch_rows
    )

    def advance(step):
        for i, d in enumerate(parts):
            row, stretch, block = step_place(
                stretch_of(order_ref, z, member, d, 0),
                stretch_of(order_ref, z, member, d, 1),
                step,
                i,
                groups,
            )
            rows = rows_at(block, block_rows)
            raw = dot(stacked[row], keys[rows, :], NT)
            visible = gap[...] <= stretch * stretch_rows - block * block_rows
            weights = (raw * sigmoid_of(raw, visible)).astype(jnp.bfloat16)
            total[row] += dot(weights, values[rows, :], NN)

    repeat(steps, 9, advance)
    for i, d in enumerate(parts):
        for e in range(2):
            shrink = SCALE * shrink_of(stretch_of(order_ref, z, member, d, e), stretch_rows)
            for g in range(groups):
                outs[i][e * stretch_rows : (e + 1) * stretch_rows, g * HEAD : (g + 1) * HEAD] = (
                    total[2 * i + e, g * stretch_rows : (g + 1) * stretch_rows, :] * shrink
                ).astype(jnp.bfloat16)


def backward_kernel(nz, order_ref, *refs):
    queries, refs = refs[:QUAD], refs[QUAD:]
    stacks, refs = refs[:nz], refs[nz:]
    query_outs, refs = refs[:QUAD], refs[QUAD:]
    key_outs, refs = refs[:nz], refs[nz:]
    keys, values, keys_t, stacked, grads, total_t, key_total, value_total, gap = refs
    z, member = place()
    stretch_rows = queries[0].shape[0] // 2
    groups = query_outs[0].shape[1] // HEAD
    block_rows = groups * stretch_rows
    blocks = keys.shape[0] // block_rows
    steps = blocks + 1
    in_sequence(order_ref, stacks, stretch_rows, keys, values)
    for block in range(blocks):
        lower = block * block_rows
        keys_t[block] = keys[lower : lower + block_rows, :].T
    offset = groups * HEAD
    for d in range(QUAD):
        for e in range(2):
            shrink = shrink_of(stretch_of(order_ref, z, member, d, e), stretch_rows)
            rows = slice(e * stretch_rows, (e + 1) * stretch_rows)
            for g in range(groups):
                into = slice(g * stretch_rows, (g + 1) * stretch_rows)
                stacked[2 * d + e, into, :] = queries[d][rows, g * HEAD : (g + 1) * HEAD]
                grads[2 * d + e, into, :] = (
                    queries[d][rows, offset + g * HEAD : offset + (g + 1) * HEAD].astype(
                        jnp.float32
                    )
                    * shrink
                ).astype(jnp.bfloat16)
    total_t[...] = jnp.zeros_like(total_t)
    key_total[...] = jnp.zeros_like(key_total)
    value_total[...] = jnp.zeros_like(value_total)
    gap[...] = lax.broadcasted_iota(jnp.int32, gap.shape, 0) - lax.rem(
        lax.broadcasted_iota(jnp.int32, gap.shape, 1), stretch_rows
    )

    def advance(step):
        for d in range(QUAD):
            row, stretch, block = step_place(
                stretch_of(order_ref, z, member, d, 0),
                stretch_of(order_ref, z, member, d, 1),
                step,
                d,
                groups,
            )
            rows = rows_at(block, block_rows)
            raw = dot(keys[rows, :], stacked[row], NT)
            weight_grad = dot(values[rows, :], grads[row], NT)
            visible = gap[...] <= stretch * stretch_rows - block * block_rows
            part = sigmoid_of(raw, visible)
            weights = raw * SCALE * part
            score_grad = (weight_grad * (part + weights * (1.0 - part))).astype(jnp.bfloat16)
            weights = weights.astype(jnp.bfloat16)
            total_t[row] += dot(keys_t[block], score_grad, NN)
            key_total[rows, :] += dot(score_grad, stacked[row], NN)
            value_total[rows, :] += dot(weights, grads[row], NN)

    repeat(steps, 3, advance)
    for d in range(QUAD):
        for e in range(2):
            query_grad = (total_t[2 * d + e].T * SCALE).astype(jnp.bfloat16)
            for g in range(groups):
                query_outs[d][
                    e * stretch_rows : (e + 1) * stretch_rows, g * HEAD : (g + 1) * HEAD
                ] = query_grad[g * stretch_rows : (g + 1) * stretch_rows, :]
    for s in range(nz):
        target = lax.rem(z + s, nz)
        for d in range(QUAD):
            for e in range(2):
                rows = rows_at(stretch_of(order_ref, target, member, d, e), stretch_rows)
                lower = (2 * d + e) * stretch_rows
                key_outs[s][lower : lower + stretch_rows, :HEAD] = (
                    key_total[rows, :] * SCALE
                ).astype(jnp.bfloat16)
                key_outs[s][lower : lower + stretch_rows, HEAD:] = value_total[rows, :].astype(
                    jnp.bfloat16
                )


def sum_kernel(*refs):
    parts, pieces = refs[:3], refs[3:]
    rows = pieces[0].shape[0]
    for d in range(QUAD):
        lower = d * rows
        pieces[d][...] = sum(
            part[lower : lower + rows, :].astype(jnp.float32) for part in parts
        ).astype(jnp.bfloat16)


def key_grad_kernel(*refs):
    pieces, (key_out, value_out) = refs[:QUAD], refs[QUAD:]
    _, member = place()
    for d in range(QUAD):
        head = columns(member ^ d, HEAD)
        key_out[0, :, head] = pieces[d][:, :HEAD]
        value_out[0, :, head] = pieces[d][:, HEAD:]


def query_grad_kernel(*refs):
    pieces, out = refs[:QUAD], refs[QUAD]
    _, member = place()
    for d in range(QUAD):
        out[0, :, columns(member ^ d, pieces[d].shape[1])] = pieces[d][...]


def gate_kernel(*refs):
    pieces, (gate_ref, out) = refs[:QUAD], refs[QUAD:]
    _, member = place()
    rows = out.shape[1]
    attended = [piece[...].astype(jnp.float32) for piece in pieces]
    square = sum(jnp.sum(part * part, axis=1, keepdims=True) for part in attended)
    factor = lax.rsqrt(square / out.shape[2] + norm_eps)
    for d in range(QUAD):
        head = columns(member ^ d, pieces[d].shape[1])
        gain = sum(gate_ref[rows : rows + GAIN_ROWS, head].astype(jnp.float32)[i : i + 1] for i in range(3))
        out[0, :, head] = (
            attended[d] * factor * gain * gate_ref[:rows, head].astype(jnp.float32)
        ).astype(jnp.bfloat16)


def call(kernel, name, out_shape, specs, *args, scratch=(), flops=0, transcendentals=0, vmem=40):
    size = sum(a.size * a.dtype.itemsize for a in args)
    size += sum(math.prod(o.shape) * o.dtype.itemsize for o in out_shape)
    return pl.pallas_call(
        kernel,
        name=name,
        out_shape=out_shape,
        in_specs=specs,
        out_specs=[VMEM] * len(out_shape),
        scratch_shapes=list(scratch),
        compiler_params=pltpu.CompilerParams(vmem_limit_bytes=vmem * MIB),
        cost_estimate=pl.CostEstimate(
            flops=flops, bytes_accessed=size, transcendentals=transcendentals
        ),
    )(*args)


def body(
    query_fwd,
    key_fwd,
    value_fwd,
    gate_fwd,
    types_fwd,
    query_bwd,
    key_bwd,
    value_bwd,
    grad_out,
    types_bwd,
    type_key,
    norm_gain,
    stretch_order,
):
    devices = lax.axis_size("ctx")
    nz = devices // QUAD
    rows = query_fwd.shape[1]
    total_rows = rows * devices
    width = query_fwd.shape[2] // QUAD
    groups = width // HEAD
    stretch_rows = rows // 2
    block_rows = groups * stretch_rows
    steps = total_rows // block_rows + 1
    pairs = steps * QUAD * block_rows * block_rows

    def swap_one(piece, d):
        return lax.ppermute(piece, "ctx", [(i, i ^ d) for i in range(devices)])

    def swap(pieces):
        return [pieces[0]] + [swap_one(pieces[d], d) for d in range(1, QUAD)]

    def turn(block, s):
        return lax.ppermute(
            block, "ctx", [(i, (i + s * QUAD) % devices) for i in range(devices)]
        )

    def hand(block, d):
        sections = lax.axis_size("pipe")
        route = [
            (i * sections + p, (i ^ d) * sections + (p + 1) % sections)
            for i in range(devices)
            for p in range(sections)
        ]
        return lax.ppermute(block, ("ctx", "pipe"), route)

    ahead = nz // 2

    def ring_up(block):
        return turn(block, 1)

    def ring_down(block):
        return turn(block, nz - 1)

    def reduce_first(parts):
        return ring_up(parts[ahead]), ring_down(parts[ahead + 1])

    def add(a, b):
        return (a.astype(jnp.float32) + b.astype(jnp.float32)).astype(jnp.bfloat16)

    def reduce_rest(parts, up, down):
        for s in range(ahead - 1, 0, -1):
            up = ring_up(add(up, parts[s]))
        for s in range(ahead + 2, nz):
            down = ring_down(add(down, parts[s]))
        return parts[0], up, down

    def gather(stack):
        return [stack] + [turn(stack, s) for s in range(1, nz)]

    def gather_ring(up):
        down = [ring_down(up[0])]
        while len(up) <= ahead:
            up.append(ring_up(up[-1]))
        while len(up) + len(down) < nz:
            down.append(ring_down(down[-1]))
        return up + down[::-1]

    def pack(key, value, types, name):
        return call(
            pack_keys,
            name,
            [bf16(rows, 2 * HEAD)] * QUAD,
            [HBM] * 4,
            key,
            value,
            types,
            type_key,
            scratch=[
                pltpu.VMEM(key.shape[1:], jnp.bfloat16),
                pltpu.VMEM(types.shape, jnp.int32),
                pltpu.VMEM(type_key.shape[1:], jnp.bfloat16),
                pltpu.VMEM(key.shape[1:], jnp.bfloat16),
                pltpu.SemaphoreType.DMA((3,)),
                pltpu.SemaphoreType.DMA((QUAD,)),
            ],
            vmem=60,
        )

    def stacked_keys(pieces, name):
        return call(
            stack_keys,
            name,
            [bf16(QUAD * rows, 2 * HEAD)],
            [HBM] * QUAD,
            *pieces,
            scratch=[pltpu.SemaphoreType.DMA((QUAD,))],
        )[0]

    back_pieces = swap(pack(key_bwd, value_bwd, types_bwd, "pack_keys_bwd"))
    pieces = pack(key_fwd, value_fwd, types_fwd, "pack_keys_fwd")
    back_pieces, pieces = lax.optimization_barrier((back_pieces, pieces))
    pieces = swap(pieces)
    back_stack = stacked_keys(back_pieces, "stack_keys_bwd")
    packed = call(
        pack_queries,
        "pack_queries",
        [bf16(rows, 3 * width)] * QUAD + [bf16(rows + GAIN_ROWS, QUAD * width)],
        [HBM] * 4 + [VMEM],
        query_bwd,
        grad_out,
        query_fwd,
        gate_fwd,
        norm_gain,
        scratch=[pltpu.SemaphoreType.DMA((3 * QUAD + 1,))],
        vmem=60,
    )
    packed = list(packed)
    up = [back_stack, ring_up(back_stack)]
    up, pieces, packed = lax.optimization_barrier((up, pieces, packed))
    back_stacks = gather_ring(up)
    stack = stacked_keys(pieces, "stack_keys_fwd")
    queries = swap(packed[:QUAD])
    back_stacks, stack, queries[1], gate_before = lax.optimization_barrier(
        (back_stacks, stack, queries[1], packed[QUAD])
    )
    stacks = gather(stack)
    gate_before = hand(gate_before, 0)

    sequence = [pltpu.VMEM((total_rows, HEAD), jnp.bfloat16)] * 2
    stacked = pltpu.VMEM((2 * QUAD, block_rows, HEAD), jnp.bfloat16)
    gap = pltpu.VMEM((block_rows, block_rows), jnp.int32)
    outs = call(
        functools.partial(backward_kernel, nz),
        "backward",
        [bf16(rows, width)] * QUAD + [bf16(QUAD * rows, 2 * HEAD)] * nz,
        [SMEM] + [VMEM] * (QUAD + nz),
        stretch_order,
        *queries,
        *back_stacks,
        scratch=sequence
        + [
            pltpu.VMEM((total_rows // block_rows, HEAD, block_rows), jnp.bfloat16),
            stacked,
            stacked,
            pltpu.VMEM((2 * QUAD, HEAD, block_rows), jnp.float32),
            pltpu.VMEM((total_rows, HEAD), jnp.float32),
            pltpu.VMEM((total_rows, HEAD), jnp.float32),
            gap,
        ],
        flops=10 * pairs * HEAD,
        transcendentals=2 * pairs,
    )
    query_pieces, key_parts = outs[:QUAD], outs[QUAD:]
    query_pieces, key_parts, gate_before = lax.optimization_barrier(
        (query_pieces, key_parts, gate_before)
    )
    query_pieces = list(query_pieces)
    query_pieces[2:] = [swap_one(query_pieces[d], d) for d in range(2, QUAD)]
    stacks, key_parts = lax.optimization_barrier((stacks, key_parts))
    key_sums = reduce_first(key_parts)
    parts = tuple(range(QUAD))
    attended = call(
        functools.partial(forward_kernel, nz, parts),
        "forward",
        [bf16(rows, width)] * QUAD,
        [SMEM] + [VMEM] * (QUAD + nz),
        stretch_order,
        *queries,
        *stacks,
        scratch=sequence
        + [stacked, pltpu.VMEM((2 * QUAD, block_rows, HEAD), jnp.float32), gap],
    )
    attended, key_up, query_pieces = lax.optimization_barrier(
        (attended, key_sums[0], query_pieces)
    )
    attended = list(attended)
    attended[3], key_down = lax.optimization_barrier((attended[3], key_sums[1]))
    attended = [hand(attended[d], d) for d in range(QUAD)]
    attended[0], query_pieces[1] = lax.optimization_barrier((attended[0], query_pieces[1]))
    query_pieces[1] = swap_one(query_pieces[1], 1)
    (handed,) = call(
        gate_kernel,
        "gate",
        [bf16(*gate_fwd.shape)],
        [VMEM] * (QUAD + 1),
        *attended,
        gate_before,
    )
    key_sums = reduce_rest(key_parts, key_up, key_down)
    key_pieces = swap(
        call(
            sum_kernel,
            "sum_key_parts",
            [bf16(rows, 2 * HEAD)] * QUAD,
            [VMEM] * 3,
            *key_sums,
        )
    )
    (query_grad,) = call(
        query_grad_kernel,
        "query_grad",
        [bf16(*query_bwd.shape)],
        [VMEM] * QUAD,
        *query_pieces,
    )
    key_grad, value_grad = call(
        key_grad_kernel,
        "key_grad",
        [bf16(*key_bwd.shape), bf16(*value_bwd.shape)],
        [VMEM] * QUAD,
        *key_pieces,
    )
    return handed, query_grad, key_grad, value_grad


def solution(mesh):
    rows = P("pipe", "ctx", None)
    types = P("pipe", "ctx")
    return jax.shard_map(
        body,
        mesh=mesh,
        in_specs=(
            rows,
            rows,
            rows,
            rows,
            types,
            rows,
            rows,
            rows,
            rows,
            types,
            P("pipe", None, None),
            P("pipe", None),
            P("pipe", None),
        ),
        out_specs=(rows, rows, rows, rows),
        check_vma=False,
    )
```

```python
import functools
import math

import jax
import jax.numpy as jnp
from jax import lax
from jax.experimental import pallas as pl
from jax.experimental.pallas import tpu as pltpu
from jax.sharding import PartitionSpec as P

HEAD = 128
QUAD = 4
SCALE = HEAD ** (-0.5)
EXP2_SCALE = -SCALE / math.log(2.0)
norm_eps = 1e-06

VMEM = pl.BlockSpec(memory_space=pltpu.VMEM)
HBM = pl.BlockSpec(memory_space=pltpu.HBM)
SMEM = pl.BlockSpec(memory_space=pltpu.SMEM)
MIB = 1024 * 1024

NN = (((1,), (0,)), ((), ()))
NT = (((1,), (1,)), ((), ()))
TN = (((0,), (0,)), ((), ()))


def dot(a, b, dims):
    return lax.dot_general(a, b, dims, preferred_element_type=jnp.float32)


def bf16(*shape):
    return jax.ShapeDtypeStruct(shape, jnp.bfloat16)


def place():
    index = lax.axis_index("ctx")
    return index // QUAD, index % QUAD


def columns(index, width):
    return pl.ds(pl.multiple_of(index * width, width), width)


def pack_keys(key_ref, value_ref, types_ref, table_ref, *refs):
    pieces, (keys, types, table, typed, arrived, placed) = refs[:QUAD], refs[QUAD:]
    _, member = place()
    copies = [
        pltpu.make_async_copy(source, target, arrived.at[i])
        for i, (source, target) in enumerate(
            [(types_ref, types), (table_ref.at[0], table), (key_ref.at[0], keys)]
        )
    ]
    placements = [
        pltpu.make_async_copy(
            value_ref.at[0, :, columns(member ^ d, HEAD)], pieces[d].at[:, HEAD:], placed.at[d]
        )
        for d in range(QUAD)
    ]
    for copy in copies + placements:
        copy.start()
    for copy in copies:
        copy.wait()
    onehot = (
        lax.broadcasted_iota(jnp.int32, (table.shape[0], types.shape[1]), 0) == types[...]
    ).astype(jnp.float32).astype(jnp.bfloat16)
    type_rows = dot(onehot, table[...], TN)
    typed[...] = (keys[...].astype(jnp.float32) + type_rows).astype(jnp.bfloat16)
    for d in range(QUAD):
        pieces[d][:, :HEAD] = typed[:, columns(member ^ d, HEAD)]
    for copy in placements:
        copy.wait()


def stack_keys(*refs):
    pieces, (out, placed) = refs[:QUAD], refs[QUAD:]
    rows = pieces[0].shape[0]
    copies = [
        pltpu.make_async_copy(pieces[d], out.at[d * rows : (d + 1) * rows, :], placed.at[d])
        for d in range(QUAD)
    ]
    for copy in copies:
        copy.start()
    for copy in copies:
        copy.wait()


def pack_queries(query_ref, grad_ref, forward_ref, *refs):
    pieces, placed = refs[:QUAD], refs[QUAD]
    _, member = place()
    width = query_ref.shape[2] // QUAD
    copies = [
        pltpu.make_async_copy(
            source.at[0, :, columns(member ^ d, width)],
            pieces[d].at[:, i * width : (i + 1) * width],
            placed.at[3 * d + i],
        )
        for d in reversed(range(QUAD))
        for i, source in enumerate([query_ref, grad_ref, forward_ref])
    ]
    for copy in copies:
        copy.start()
    for copy in copies:
        copy.wait()


def stretch_of(order_ref, quad_index, member, d, e):
    return order_ref[0, 2 * (quad_index * QUAD + (member ^ d)) + e]


def rows_at(index, count):
    return pl.ds(pl.multiple_of(index * count, count), count)


def in_sequence(order_ref, stacks, stretch_rows, keys, values):
    z, member = place()
    nz = len(stacks)
    for s, stack in enumerate(stacks):
        source = lax.rem(z - s + nz, nz)
        for d in range(QUAD):
            for e in range(2):
                rows = rows_at(stretch_of(order_ref, source, member, d, e), stretch_rows)
                lower = (2 * d + e) * stretch_rows
                keys[rows, :] = stack[lower : lower + stretch_rows, :HEAD]
                values[rows, :] = stack[lower : lower + stretch_rows, HEAD:]


def shrink_of(stretch, stretch_rows):
    pos = stretch * stretch_rows + lax.broadcasted_iota(jnp.int32, (stretch_rows, HEAD), 0)
    return lax.rsqrt((pos + 1).astype(jnp.float32))


def step_place(first, second, step, d, groups):
    blocks = first // groups + 1
    late = step >= blocks
    row = jnp.where(late, 2 * d + 1, 2 * d)
    stretch = jnp.where(late, second, first)
    block = jnp.where(late, step - blocks, step)
    return row, stretch, block


def sigmoid_of(raw, visible):
    part = pl.reciprocal(1.0 + jnp.exp2(raw * EXP2_SCALE), approx=True)
    return jnp.where(visible, part, 0.0)


def repeat(steps, together, advance):
    def several(i, _):
        for j in range(together):
            advance(i * together + j)
        return 0

    lax.fori_loop(0, steps // together, several, 0)
    for step in range(steps // together * together, steps):
        advance(step)


def forward_kernel(nz, parts, order_ref, *refs):
    queries, refs = refs[: len(parts)], refs[len(parts) :]
    stacks, refs = refs[:nz], refs[nz:]
    outs, refs = refs[: len(parts)], refs[len(parts) :]
    keys, values, stacked, total, gap = refs
    z, member = place()
    stretch_rows = queries[0].shape[0] // 2
    groups = outs[0].shape[1] // HEAD
    block_rows = groups * stretch_rows
    steps = keys.shape[0] // block_rows + 1
    in_sequence(order_ref, stacks, stretch_rows, keys, values)
    offset = 2 * groups * HEAD
    for i in range(len(parts)):
        for e in range(2):
            for g in range(groups):
                stacked[2 * i + e, g * stretch_rows : (g + 1) * stretch_rows, :] = queries[i][
                    e * stretch_rows : (e + 1) * stretch_rows,
                    offset + g * HEAD : offset + (g + 1) * HEAD,
                ]
    total[...] = jnp.zeros_like(total)
    gap[...] = lax.broadcasted_iota(jnp.int32, gap.shape, 1) - lax.rem(
        lax.broadcasted_iota(jnp.int32, gap.shape, 0), stretch_rows
    )

    def advance(step):
        for i, d in enumerate(parts):
            row, stretch, block = step_place(
                stretch_of(order_ref, z, member, d, 0),
                stretch_of(order_ref, z, member, d, 1),
                step,
                i,
                groups,
            )
            rows = rows_at(block, block_rows)
            raw = dot(stacked[row], keys[rows, :], NT)
            visible = gap[...] <= stretch * stretch_rows - block * block_rows
            weights = (raw * sigmoid_of(raw, visible)).astype(jnp.bfloat16)
            total[row] += dot(weights, values[rows, :], NN)

    repeat(steps, 9, advance)
    for i, d in enumerate(parts):
        for e in range(2):
            shrink = SCALE * shrink_of(stretch_of(order_ref, z, member, d, e), stretch_rows)
            for g in range(groups):
                outs[i][e * stretch_rows : (e + 1) * stretch_rows, g * HEAD : (g + 1) * HEAD] = (
                    total[2 * i + e, g * stretch_rows : (g + 1) * stretch_rows, :] * shrink
                ).astype(jnp.bfloat16)


def backward_kernel(nz, order_ref, *refs):
    queries, refs = refs[:QUAD], refs[QUAD:]
    stacks, refs = refs[:nz], refs[nz:]
    query_outs, refs = refs[:QUAD], refs[QUAD:]
    key_outs, refs = refs[:nz], refs[nz:]
    keys, values, keys_t, stacked, grads, total_t, key_total, value_total, gap = refs
    z, member = place()
    stretch_rows = queries[0].shape[0] // 2
    groups = query_outs[0].shape[1] // HEAD
    block_rows = groups * stretch_rows
    blocks = keys.shape[0] // block_rows
    steps = blocks + 1
    in_sequence(order_ref, stacks, stretch_rows, keys, values)
    for block in range(blocks):
        lower = block * block_rows
        keys_t[block] = keys[lower : lower + block_rows, :].T
    offset = groups * HEAD
    for d in range(QUAD):
        for e in range(2):
            shrink = shrink_of(stretch_of(order_ref, z, member, d, e), stretch_rows)
            rows = slice(e * stretch_rows, (e + 1) * stretch_rows)
            for g in range(groups):
                into = slice(g * stretch_rows, (g + 1) * stretch_rows)
                stacked[2 * d + e, into, :] = queries[d][rows, g * HEAD : (g + 1) * HEAD]
                grads[2 * d + e, into, :] = (
                    queries[d][rows, offset + g * HEAD : offset + (g + 1) * HEAD].astype(
                        jnp.float32
                    )
                    * shrink
                ).astype(jnp.bfloat16)
    total_t[...] = jnp.zeros_like(total_t)
    key_total[...] = jnp.zeros_like(key_total)
    value_total[...] = jnp.zeros_like(value_total)
    gap[...] = lax.broadcasted_iota(jnp.int32, gap.shape, 0) - lax.rem(
        lax.broadcasted_iota(jnp.int32, gap.shape, 1), stretch_rows
    )

    def advance(step):
        for d in range(QUAD):
            row, stretch, block = step_place(
                stretch_of(order_ref, z, member, d, 0),
                stretch_of(order_ref, z, member, d, 1),
                step,
                d,
                groups,
            )
            rows = rows_at(block, block_rows)
            raw = dot(keys[rows, :], stacked[row], NT)
            weight_grad = dot(values[rows, :], grads[row], NT)
            visible = gap[...] <= stretch * stretch_rows - block * block_rows
            part = sigmoid_of(raw, visible)
            weights = raw * SCALE * part
            score_grad = (weight_grad * (part + weights * (1.0 - part))).astype(jnp.bfloat16)
            weights = weights.astype(jnp.bfloat16)
            total_t[row] += dot(keys_t[block], score_grad, NN)
            key_total[rows, :] += dot(score_grad, stacked[row], NN)
            value_total[rows, :] += dot(weights, grads[row], NN)

    repeat(steps, 3, advance)
    for d in range(QUAD):
        for e in range(2):
            query_grad = (total_t[2 * d + e].T * SCALE).astype(jnp.bfloat16)
            for g in range(groups):
                query_outs[d][
                    e * stretch_rows : (e + 1) * stretch_rows, g * HEAD : (g + 1) * HEAD
                ] = query_grad[g * stretch_rows : (g + 1) * stretch_rows, :]
    for s in range(nz):
        target = lax.rem(z + s, nz)
        for d in range(QUAD):
            for e in range(2):
                rows = rows_at(stretch_of(order_ref, target, member, d, e), stretch_rows)
                lower = (2 * d + e) * stretch_rows
                key_outs[s][lower : lower + stretch_rows, :HEAD] = (
                    key_total[rows, :] * SCALE
                ).astype(jnp.bfloat16)
                key_outs[s][lower : lower + stretch_rows, HEAD:] = value_total[rows, :].astype(
                    jnp.bfloat16
                )


def sum_kernel(*refs):
    parts, pieces = refs[:3], refs[3:]
    rows = pieces[0].shape[0]
    for d in range(QUAD):
        lower = d * rows
        pieces[d][...] = sum(
            part[lower : lower + rows, :].astype(jnp.float32) for part in parts
        ).astype(jnp.bfloat16)


def key_grad_kernel(*refs):
    pieces, (key_out, value_out) = refs[:QUAD], refs[QUAD:]
    _, member = place()
    for d in range(QUAD):
        head = columns(member ^ d, HEAD)
        key_out[0, :, head] = pieces[d][:, :HEAD]
        value_out[0, :, head] = pieces[d][:, HEAD:]


def query_grad_kernel(*refs):
    pieces, out = refs[:QUAD], refs[QUAD]
    _, member = place()
    for d in range(QUAD):
        out[0, :, columns(member ^ d, pieces[d].shape[1])] = pieces[d][...]


def gate_kernel(*refs):
    pieces, (gate_ref, gain_ref, out) = refs[:QUAD], refs[QUAD:]
    _, member = place()
    attended = [piece[...].astype(jnp.float32) for piece in pieces]
    square = sum(jnp.sum(part * part, axis=1, keepdims=True) for part in attended)
    factor = lax.rsqrt(square / out.shape[2] + norm_eps)
    for d in range(QUAD):
        head = columns(member ^ d, pieces[d].shape[1])
        out[0, :, head] = (
            attended[d] * factor * gain_ref[:, head] * gate_ref[0, :, head].astype(jnp.float32)
        ).astype(jnp.bfloat16)


def call(kernel, name, out_shape, specs, *args, scratch=(), flops=0, transcendentals=0, vmem=40):
    size = sum(a.size * a.dtype.itemsize for a in args)
    size += sum(math.prod(o.shape) * o.dtype.itemsize for o in out_shape)
    return pl.pallas_call(
        kernel,
        name=name,
        out_shape=out_shape,
        in_specs=specs,
        out_specs=[VMEM] * len(out_shape),
        scratch_shapes=list(scratch),
        compiler_params=pltpu.CompilerParams(vmem_limit_bytes=vmem * MIB),
        cost_estimate=pl.CostEstimate(
            flops=flops, bytes_accessed=size, transcendentals=transcendentals
        ),
    )(*args)


def body(
    query_fwd,
    key_fwd,
    value_fwd,
    gate_fwd,
    types_fwd,
    query_bwd,
    key_bwd,
    value_bwd,
    grad_out,
    types_bwd,
    type_key,
    norm_gain,
    stretch_order,
):
    devices = lax.axis_size("ctx")
    nz = devices // QUAD
    rows = query_fwd.shape[1]
    total_rows = rows * devices
    width = query_fwd.shape[2] // QUAD
    groups = width // HEAD
    stretch_rows = rows // 2
    block_rows = groups * stretch_rows
    steps = total_rows // block_rows + 1
    pairs = steps * QUAD * block_rows * block_rows

    def swap_one(piece, d):
        return lax.ppermute(piece, "ctx", [(i, i ^ d) for i in range(devices)])

    def swap(pieces):
        return [pieces[0]] + [swap_one(pieces[d], d) for d in range(1, QUAD)]

    def turn(block, s):
        return lax.ppermute(
            block, "ctx", [(i, (i + s * QUAD) % devices) for i in range(devices)]
        )

    def hand(block, d):
        sections = lax.axis_size("pipe")
        route = [
            (i * sections + p, (i ^ d) * sections + (p + 1) % sections)
            for i in range(devices)
            for p in range(sections)
        ]
        return lax.ppermute(block, ("ctx", "pipe"), route)

    ahead = nz // 2

    def ring_up(block):
        return turn(block, 1)

    def ring_down(block):
        return turn(block, nz - 1)

    def reduce_first(parts):
        return ring_up(parts[ahead]), ring_down(parts[ahead + 1])

    def add(a, b):
        return (a.astype(jnp.float32) + b.astype(jnp.float32)).astype(jnp.bfloat16)

    def reduce_rest(parts, up, down):
        for s in range(ahead - 1, 0, -1):
            up = ring_up(add(up, parts[s]))
        for s in range(ahead + 2, nz):
            down = ring_down(add(down, parts[s]))
        return parts[0], up, down

    def gather(stack):
        return [stack] + [turn(stack, s) for s in range(1, nz)]

    def gather_ring(up):
        down = [ring_down(up[0])]
        while len(up) <= ahead:
            up.append(ring_up(up[-1]))
        while len(up) + len(down) < nz:
            down.append(ring_down(down[-1]))
        return up + down[::-1]

    def pack(key, value, types, name):
        return call(
            pack_keys,
            name,
            [bf16(rows, 2 * HEAD)] * QUAD,
            [HBM] * 4,
            key,
            value,
            types,
            type_key,
            scratch=[
                pltpu.VMEM(key.shape[1:], jnp.bfloat16),
                pltpu.VMEM(types.shape, jnp.int32),
                pltpu.VMEM(type_key.shape[1:], jnp.bfloat16),
                pltpu.VMEM(key.shape[1:], jnp.bfloat16),
                pltpu.SemaphoreType.DMA((3,)),
                pltpu.SemaphoreType.DMA((QUAD,)),
            ],
            vmem=60,
        )

    def stacked_keys(pieces, name):
        return call(
            stack_keys,
            name,
            [bf16(QUAD * rows, 2 * HEAD)],
            [HBM] * QUAD,
            *pieces,
            scratch=[pltpu.SemaphoreType.DMA((QUAD,))],
        )[0]

    back_pieces, gate_before = lax.optimization_barrier(
        (pack(key_bwd, value_bwd, types_bwd, "pack_keys_bwd"), gate_fwd)
    )
    back_pieces, gate_before = swap(back_pieces), hand(gate_before, 0)
    pieces = pack(key_fwd, value_fwd, types_fwd, "pack_keys_fwd")
    back_pieces, pieces = lax.optimization_barrier((back_pieces, pieces))
    pieces = swap(pieces)
    packed = call(
        pack_queries,
        "pack_queries",
        [bf16(rows, 3 * width)] * QUAD,
        [HBM] * 3,
        query_bwd,
        grad_out,
        query_fwd,
        scratch=[pltpu.SemaphoreType.DMA((3 * QUAD,))],
        vmem=60,
    )
    packed = list(packed)
    back_stack = stacked_keys(back_pieces, "stack_keys_bwd")
    up = [back_stack, ring_up(back_stack)]
    up, pieces, packed, gate_before, gain_before = lax.optimization_barrier(
        (up, pieces, packed, gate_before, norm_gain)
    )
    back_stacks = gather_ring(up)
    stack = stacked_keys(pieces, "stack_keys_fwd")
    gain_before = hand(gain_before, 0)
    back_stacks, stack, packed[1], gain_before = lax.optimization_barrier(
        (back_stacks, stack, packed[1], gain_before)
    )
    queries = swap(packed)
    stacks = gather(stack)

    sequence = [pltpu.VMEM((total_rows, HEAD), jnp.bfloat16)] * 2
    stacked = pltpu.VMEM((2 * QUAD, block_rows, HEAD), jnp.bfloat16)
    gap = pltpu.VMEM((block_rows, block_rows), jnp.int32)
    outs = call(
        functools.partial(backward_kernel, nz),
        "backward",
        [bf16(rows, width)] * QUAD + [bf16(QUAD * rows, 2 * HEAD)] * nz,
        [SMEM] + [VMEM] * (QUAD + nz),
        stretch_order,
        *queries,
        *back_stacks,
        scratch=sequence
        + [
            pltpu.VMEM((total_rows // block_rows, HEAD, block_rows), jnp.bfloat16),
            stacked,
            stacked,
            pltpu.VMEM((2 * QUAD, HEAD, block_rows), jnp.float32),
            pltpu.VMEM((total_rows, HEAD), jnp.float32),
            pltpu.VMEM((total_rows, HEAD), jnp.float32),
            gap,
        ],
        flops=10 * pairs * HEAD,
        transcendentals=2 * pairs,
    )
    query_pieces, key_parts = outs[:QUAD], outs[QUAD:]
    query_pieces = list(query_pieces)
    query_pieces[2:] = [swap_one(query_pieces[d], d) for d in range(2, QUAD)]
    stacks, key_parts = lax.optimization_barrier((stacks, key_parts))
    key_sums = reduce_first(key_parts)
    parts = tuple(range(QUAD))
    attended = call(
        functools.partial(forward_kernel, nz, parts),
        "forward",
        [bf16(rows, width)] * QUAD,
        [SMEM] + [VMEM] * (QUAD + nz),
        stretch_order,
        *queries,
        *stacks,
        scratch=sequence
        + [stacked, pltpu.VMEM((2 * QUAD, block_rows, HEAD), jnp.float32), gap],
    )
    attended, key_up, query_pieces = lax.optimization_barrier(
        (attended, key_sums[0], query_pieces)
    )
    attended = [hand(attended[d], d) for d in range(QUAD)]
    attended[0], query_pieces[1] = lax.optimization_barrier((attended[0], query_pieces[1]))
    query_pieces[1] = swap_one(query_pieces[1], 1)
    (handed,) = call(
        gate_kernel,
        "gate",
        [bf16(*gate_fwd.shape)],
        [VMEM] * (QUAD + 2),
        *attended,
        gate_before,
        gain_before,
    )
    key_sums = reduce_rest(key_parts, key_up, key_sums[1])
    key_pieces = swap(
        call(
            sum_kernel,
            "sum_key_parts",
            [bf16(rows, 2 * HEAD)] * QUAD,
            [VMEM] * 3,
            *key_sums,
        )
    )
    (query_grad,) = call(
        query_grad_kernel,
        "query_grad",
        [bf16(*query_bwd.shape)],
        [VMEM] * QUAD,
        *query_pieces,
    )
    key_grad, value_grad = call(
        key_grad_kernel,
        "key_grad",
        [bf16(*key_bwd.shape), bf16(*value_bwd.shape)],
        [VMEM] * QUAD,
        *key_pieces,
    )
    return handed, query_grad, key_grad, value_grad


def solution(mesh):
    rows = P("pipe", "ctx", None)
    types = P("pipe", "ctx")
    return jax.shard_map(
        body,
        mesh=mesh,
        in_specs=(
            rows,
            rows,
            rows,
            rows,
            types,
            rows,
            rows,
            rows,
            rows,
            types,
            P("pipe", None, None),
            P("pipe", None),
            P("pipe", None),
        ),
        out_specs=(rows, rows, rows, rows),
        check_vma=False,
    )
```

```python
import functools
import math

import jax
import jax.numpy as jnp
from jax import lax
from jax.experimental import pallas as pl
from jax.experimental.pallas import tpu as pltpu
from jax.sharding import PartitionSpec as P

HEAD = 128
QUAD = 4
SCALE = HEAD ** (-0.5)
EXP2_SCALE = -SCALE / math.log(2.0)
GAIN_ROWS = 16
norm_eps = 1e-06

VMEM = pl.BlockSpec(memory_space=pltpu.VMEM)
HBM = pl.BlockSpec(memory_space=pltpu.HBM)
SMEM = pl.BlockSpec(memory_space=pltpu.SMEM)
MIB = 1024 * 1024

NN = (((1,), (0,)), ((), ()))
NT = (((1,), (1,)), ((), ()))
TN = (((0,), (0,)), ((), ()))


def dot(a, b, dims):
    return lax.dot_general(a, b, dims, preferred_element_type=jnp.float32)


def bf16(*shape):
    return jax.ShapeDtypeStruct(shape, jnp.bfloat16)


def place():
    index = lax.axis_index("ctx")
    return index // QUAD, index % QUAD


def columns(index, width):
    return pl.ds(pl.multiple_of(index * width, width), width)


def pack_keys(key_ref, value_ref, types_ref, table_ref, *refs):
    pieces, (keys, types, table, typed, arrived, placed) = refs[:QUAD], refs[QUAD:]
    _, member = place()
    copies = [
        pltpu.make_async_copy(source, target, arrived.at[i])
        for i, (source, target) in enumerate(
            [(types_ref, types), (table_ref.at[0], table), (key_ref.at[0], keys)]
        )
    ]
    placements = [
        pltpu.make_async_copy(
            value_ref.at[0, :, columns(member ^ d, HEAD)], pieces[d].at[:, HEAD:], placed.at[d]
        )
        for d in range(QUAD)
    ]
    for copy in copies + placements:
        copy.start()
    for copy in copies:
        copy.wait()
    onehot = (
        lax.broadcasted_iota(jnp.int32, (table.shape[0], types.shape[1]), 0) == types[...]
    ).astype(jnp.float32).astype(jnp.bfloat16)
    type_rows = dot(onehot, table[...], TN)
    typed[...] = (keys[...].astype(jnp.float32) + type_rows).astype(jnp.bfloat16)
    for d in range(QUAD):
        pieces[d][:, :HEAD] = typed[:, columns(member ^ d, HEAD)]
    for copy in placements:
        copy.wait()


def stack_keys(*refs):
    pieces, (out, placed) = refs[:QUAD], refs[QUAD:]
    rows = pieces[0].shape[0]
    copies = [
        pltpu.make_async_copy(pieces[d], out.at[d * rows : (d + 1) * rows, :], placed.at[d])
        for d in range(QUAD)
    ]
    for copy in copies:
        copy.start()
    for copy in copies:
        copy.wait()


def pack_queries(query_ref, grad_ref, forward_ref, gate_ref, gain_ref, *refs):
    pieces, (gate_out, placed) = refs[:QUAD], refs[QUAD:]
    _, member = place()
    width = query_ref.shape[2] // QUAD
    rows = gate_ref.shape[1]
    copies = [
        pltpu.make_async_copy(
            source.at[0, :, columns(member ^ d, width)],
            pieces[d].at[:, i * width : (i + 1) * width],
            placed.at[3 * d + i],
        )
        for d in reversed(range(QUAD))
        for i, source in enumerate([query_ref, grad_ref, forward_ref])
    ]
    copies.append(
        pltpu.make_async_copy(gate_ref.at[0], gate_out.at[:rows, :], placed.at[3 * QUAD])
    )
    for copy in copies:
        copy.start()
    rest = gain_ref[...]
    parts = []
    for _ in range(3):
        part = rest.astype(jnp.bfloat16).astype(jnp.float32)
        parts.append(part)
        rest = rest - part
    parts.append(jnp.zeros((GAIN_ROWS - 3, rest.shape[1]), jnp.float32))
    gate_out[rows:, :] = jnp.concatenate(parts, axis=0).astype(jnp.bfloat16)
    for copy in copies:
        copy.wait()


def stretch_of(order_ref, quad_index, member, d, e):
    return order_ref[0, 2 * (quad_index * QUAD + (member ^ d)) + e]


def rows_at(index, count):
    return pl.ds(pl.multiple_of(index * count, count), count)


def in_sequence(order_ref, stacks, stretch_rows, keys, values):
    z, member = place()
    nz = len(stacks)
    for s, stack in enumerate(stacks):
        source = lax.rem(z - s + nz, nz)
        for d in range(QUAD):
            for e in range(2):
                rows = rows_at(stretch_of(order_ref, source, member, d, e), stretch_rows)
                lower = (2 * d + e) * stretch_rows
                keys[rows, :] = stack[lower : lower + stretch_rows, :HEAD]
                values[rows, :] = stack[lower : lower + stretch_rows, HEAD:]


def shrink_of(stretch, stretch_rows):
    pos = stretch * stretch_rows + lax.broadcasted_iota(jnp.int32, (stretch_rows, HEAD), 0)
    return lax.rsqrt((pos + 1).astype(jnp.float32))


def step_place(first, second, step, d, groups):
    blocks = first // groups + 1
    late = step >= blocks
    row = jnp.where(late, 2 * d + 1, 2 * d)
    stretch = jnp.where(late, second, first)
    block = jnp.where(late, step - blocks, step)
    return row, stretch, block


def sigmoid_of(raw, visible):
    part = pl.reciprocal(1.0 + jnp.exp2(raw * EXP2_SCALE), approx=True)
    return jnp.where(visible, part, 0.0)


def repeat(steps, together, advance):
    def several(i, _):
        for j in range(together):
            advance(i * together + j)
        return 0

    lax.fori_loop(0, steps // together, several, 0)
    for step in range(steps // together * together, steps):
        advance(step)


def forward_kernel(nz, parts, order_ref, *refs):
    queries, refs = refs[: len(parts)], refs[len(parts) :]
    stacks, refs = refs[:nz], refs[nz:]
    outs, refs = refs[: len(parts)], refs[len(parts) :]
    keys, values, stacked, total, gap = refs
    z, member = place()
    stretch_rows = queries[0].shape[0] // 2
    groups = outs[0].shape[1] // HEAD
    block_rows = groups * stretch_rows
    steps = keys.shape[0] // block_rows + 1
    in_sequence(order_ref, stacks, stretch_rows, keys, values)
    offset = 2 * groups * HEAD
    for i in range(len(parts)):
        for e in range(2):
            for g in range(groups):
                stacked[2 * i + e, g * stretch_rows : (g + 1) * stretch_rows, :] = queries[i][
                    e * stretch_rows : (e + 1) * stretch_rows,
                    offset + g * HEAD : offset + (g + 1) * HEAD,
                ]
    total[...] = jnp.zeros_like(total)
    gap[...] = lax.broadcasted_iota(jnp.int32, gap.shape, 1) - lax.rem(
        lax.broadcasted_iota(jnp.int32, gap.shape, 0), stretch_rows
    )

    def advance(step):
        for i, d in enumerate(parts):
            row, stretch, block = step_place(
                stretch_of(order_ref, z, member, d, 0),
                stretch_of(order_ref, z, member, d, 1),
                step,
                i,
                groups,
            )
            rows = rows_at(block, block_rows)
            raw = dot(stacked[row], keys[rows, :], NT)
            visible = gap[...] <= stretch * stretch_rows - block * block_rows
            weights = (raw * sigmoid_of(raw, visible)).astype(jnp.bfloat16)
            total[row] += dot(weights, values[rows, :], NN)

    repeat(steps, 9, advance)
    for i, d in enumerate(parts):
        for e in range(2):
            shrink = SCALE * shrink_of(stretch_of(order_ref, z, member, d, e), stretch_rows)
            for g in range(groups):
                outs[i][e * stretch_rows : (e + 1) * stretch_rows, g * HEAD : (g + 1) * HEAD] = (
                    total[2 * i + e, g * stretch_rows : (g + 1) * stretch_rows, :] * shrink
                ).astype(jnp.bfloat16)


def backward_kernel(nz, parts, first, order_ref, *refs):
    queries, refs = refs[: len(parts)], refs[len(parts) :]
    stacks, refs = refs[:nz], refs[nz:]
    if first:
        query_outs, refs = refs[: len(parts)], refs[len(parts) :]
        key_total, value_total, keys, values, keys_t, stacked, grads, total_t, gap = refs
        key_total[...] = jnp.zeros_like(key_total)
        value_total[...] = jnp.zeros_like(value_total)
    else:
        (key_before, value_before), refs = refs[:2], refs[2:]
        query_outs, refs = refs[: len(parts)], refs[len(parts) :]
        key_outs, refs = refs[:nz], refs[nz:]
        key_total, value_total, keys, values, keys_t, stacked, grads, total_t, gap = refs
        key_total[...] = key_before[...]
        value_total[...] = value_before[...]
    z, member = place()
    stretch_rows = queries[0].shape[0] // 2
    groups = query_outs[0].shape[1] // HEAD
    block_rows = groups * stretch_rows
    blocks = keys.shape[0] // block_rows
    steps = blocks + 1
    in_sequence(order_ref, stacks, stretch_rows, keys, values)
    for block in range(blocks):
        lower = block * block_rows
        keys_t[block] = keys[lower : lower + block_rows, :].T
    offset = groups * HEAD
    for i, d in enumerate(parts):
        for e in range(2):
            shrink = shrink_of(stretch_of(order_ref, z, member, d, e), stretch_rows)
            rows = slice(e * stretch_rows, (e + 1) * stretch_rows)
            for g in range(groups):
                into = slice(g * stretch_rows, (g + 1) * stretch_rows)
                stacked[2 * i + e, into, :] = queries[i][rows, g * HEAD : (g + 1) * HEAD]
                grads[2 * i + e, into, :] = (
                    queries[i][rows, offset + g * HEAD : offset + (g + 1) * HEAD].astype(
                        jnp.float32
                    )
                    * shrink
                ).astype(jnp.bfloat16)
    total_t[...] = jnp.zeros_like(total_t)
    gap[...] = lax.broadcasted_iota(jnp.int32, gap.shape, 0) - lax.rem(
        lax.broadcasted_iota(jnp.int32, gap.shape, 1), stretch_rows
    )

    def advance(step):
        for i, d in enumerate(parts):
            row, stretch, block = step_place(
                stretch_of(order_ref, z, member, d, 0),
                stretch_of(order_ref, z, member, d, 1),
                step,
                i,
                groups,
            )
            rows = rows_at(block, block_rows)
            raw = dot(keys[rows, :], stacked[row], NT)
            weight_grad = dot(values[rows, :], grads[row], NT)
            visible = gap[...] <= stretch * stretch_rows - block * block_rows
            part = sigmoid_of(raw, visible)
            weights = raw * SCALE * part
            score_grad = (weight_grad * (part + weights * (1.0 - part))).astype(jnp.bfloat16)
            weights = weights.astype(jnp.bfloat16)
            total_t[row] += dot(keys_t[block], score_grad, NN)
            key_total[rows, :] += dot(score_grad, stacked[row], NN)
            value_total[rows, :] += dot(weights, grads[row], NN)

    repeat(steps, 3, advance)
    for i in range(len(parts)):
        for e in range(2):
            query_grad = (total_t[2 * i + e].T * SCALE).astype(jnp.bfloat16)
            for g in range(groups):
                query_outs[i][
                    e * stretch_rows : (e + 1) * stretch_rows, g * HEAD : (g + 1) * HEAD
                ] = query_grad[g * stretch_rows : (g + 1) * stretch_rows, :]
    if first:
        return
    for s in range(nz):
        target = lax.rem(z + s, nz)
        for d in range(QUAD):
            for e in range(2):
                rows = rows_at(stretch_of(order_ref, target, member, d, e), stretch_rows)
                lower = (2 * d + e) * stretch_rows
                key_outs[s][lower : lower + stretch_rows, :HEAD] = (
                    key_total[rows, :] * SCALE
                ).astype(jnp.bfloat16)
                key_outs[s][lower : lower + stretch_rows, HEAD:] = value_total[rows, :].astype(
                    jnp.bfloat16
                )


def sum_kernel(*refs):
    parts, pieces = refs[:3], refs[3:]
    rows = pieces[0].shape[0]
    for d in range(QUAD):
        lower = d * rows
        pieces[d][...] = sum(
            part[lower : lower + rows, :].astype(jnp.float32) for part in parts
        ).astype(jnp.bfloat16)


def key_grad_kernel(*refs):
    pieces, (key_out, value_out) = refs[:QUAD], refs[QUAD:]
    _, member = place()
    for d in range(QUAD):
        head = columns(member ^ d, HEAD)
        key_out[0, :, head] = pieces[d][:, :HEAD]
        value_out[0, :, head] = pieces[d][:, HEAD:]


def query_grad_kernel(*refs):
    pieces, out = refs[:QUAD], refs[QUAD]
    _, member = place()
    for d in range(QUAD):
        out[0, :, columns(member ^ d, pieces[d].shape[1])] = pieces[d][...]


def gate_kernel(*refs):
    pieces, (gate_ref, out) = refs[:QUAD], refs[QUAD:]
    _, member = place()
    rows = out.shape[1]
    attended = [piece[...].astype(jnp.float32) for piece in pieces]
    square = sum(jnp.sum(part * part, axis=1, keepdims=True) for part in attended)
    factor = lax.rsqrt(square / out.shape[2] + norm_eps)
    for d in range(QUAD):
        head = columns(member ^ d, pieces[d].shape[1])
        gain = sum(gate_ref[rows : rows + GAIN_ROWS, head].astype(jnp.float32)[i : i + 1] for i in range(3))
        out[0, :, head] = (
            attended[d] * factor * gain * gate_ref[:rows, head].astype(jnp.float32)
        ).astype(jnp.bfloat16)


def call(kernel, name, out_shape, specs, *args, scratch=(), flops=0, transcendentals=0, vmem=40):
    size = sum(a.size * a.dtype.itemsize for a in args)
    size += sum(math.prod(o.shape) * o.dtype.itemsize for o in out_shape)
    return pl.pallas_call(
        kernel,
        name=name,
        out_shape=out_shape,
        in_specs=specs,
        out_specs=[VMEM] * len(out_shape),
        scratch_shapes=list(scratch),
        compiler_params=pltpu.CompilerParams(vmem_limit_bytes=vmem * MIB),
        cost_estimate=pl.CostEstimate(
            flops=flops, bytes_accessed=size, transcendentals=transcendentals
        ),
    )(*args)


def body(
    query_fwd,
    key_fwd,
    value_fwd,
    gate_fwd,
    types_fwd,
    query_bwd,
    key_bwd,
    value_bwd,
    grad_out,
    types_bwd,
    type_key,
    norm_gain,
    stretch_order,
):
    devices = lax.axis_size("ctx")
    nz = devices // QUAD
    rows = query_fwd.shape[1]
    total_rows = rows * devices
    width = query_fwd.shape[2] // QUAD
    groups = width // HEAD
    stretch_rows = rows // 2
    block_rows = groups * stretch_rows
    steps = total_rows // block_rows + 1
    pairs = steps * QUAD * block_rows * block_rows

    def swap_one(piece, d):
        return lax.ppermute(piece, "ctx", [(i, i ^ d) for i in range(devices)])

    def swap(pieces):
        return [pieces[0]] + [swap_one(pieces[d], d) for d in range(1, QUAD)]

    def turn(block, s):
        return lax.ppermute(
            block, "ctx", [(i, (i + s * QUAD) % devices) for i in range(devices)]
        )

    def hand(block, d):
        sections = lax.axis_size("pipe")
        route = [
            (i * sections + p, (i ^ d) * sections + (p + 1) % sections)
            for i in range(devices)
            for p in range(sections)
        ]
        return lax.ppermute(block, ("ctx", "pipe"), route)

    ahead = nz // 2

    def ring_up(block):
        return turn(block, 1)

    def ring_down(block):
        return turn(block, nz - 1)

    def reduce_first(parts):
        return ring_up(parts[ahead]), ring_down(parts[ahead + 1])

    def add(a, b):
        return (a.astype(jnp.float32) + b.astype(jnp.float32)).astype(jnp.bfloat16)

    def reduce_rest(parts, up, down):
        for s in range(ahead - 1, 0, -1):
            up = ring_up(add(up, parts[s]))
        for s in range(ahead + 2, nz):
            down = ring_down(add(down, parts[s]))
        return parts[0], up, down

    def gather(stack):
        return [stack] + [turn(stack, s) for s in range(1, nz)]

    def gather_ring(up):
        down = [ring_down(up[0])]
        while len(up) <= ahead:
            up.append(ring_up(up[-1]))
        while len(up) + len(down) < nz:
            down.append(ring_down(down[-1]))
        return up + down[::-1]

    def pack(key, value, types, name):
        return call(
            pack_keys,
            name,
            [bf16(rows, 2 * HEAD)] * QUAD,
            [HBM] * 4,
            key,
            value,
            types,
            type_key,
            scratch=[
                pltpu.VMEM(key.shape[1:], jnp.bfloat16),
                pltpu.VMEM(types.shape, jnp.int32),
                pltpu.VMEM(type_key.shape[1:], jnp.bfloat16),
                pltpu.VMEM(key.shape[1:], jnp.bfloat16),
                pltpu.SemaphoreType.DMA((3,)),
                pltpu.SemaphoreType.DMA((QUAD,)),
            ],
            vmem=60,
        )

    def stacked_keys(pieces, name):
        return call(
            stack_keys,
            name,
            [bf16(QUAD * rows, 2 * HEAD)],
            [HBM] * QUAD,
            *pieces,
            scratch=[pltpu.SemaphoreType.DMA((QUAD,))],
        )[0]

    back_pieces = swap(pack(key_bwd, value_bwd, types_bwd, "pack_keys_bwd"))
    pieces = pack(key_fwd, value_fwd, types_fwd, "pack_keys_fwd")
    back_pieces, pieces = lax.optimization_barrier((back_pieces, pieces))
    pieces = swap(pieces)
    packed = call(
        pack_queries,
        "pack_queries",
        [bf16(rows, 3 * width)] * QUAD + [bf16(rows + GAIN_ROWS, QUAD * width)],
        [HBM] * 4 + [VMEM],
        query_bwd,
        grad_out,
        query_fwd,
        gate_fwd,
        norm_gain,
        scratch=[pltpu.SemaphoreType.DMA((3 * QUAD + 1,))],
        vmem=60,
    )
    packed = list(packed)
    back_stack = stacked_keys(back_pieces, "stack_keys_bwd")
    up = [back_stack, ring_up(back_stack)]
    up, pieces, packed = lax.optimization_barrier((up, pieces, packed))
    back_stacks = gather_ring(up)
    stack = stacked_keys(pieces, "stack_keys_fwd")
    back_stacks, stack, packed[1], packed[QUAD] = lax.optimization_barrier(
        (back_stacks, stack, packed[1], packed[QUAD])
    )
    queries = swap(packed[:QUAD])
    up, down = [stack, ring_up(stack)], [ring_down(stack)]
    gate_before = hand(packed[QUAD], 0)

    sequence = [pltpu.VMEM((total_rows, HEAD), jnp.bfloat16)] * 2
    stacked = pltpu.VMEM((2 * QUAD, block_rows, HEAD), jnp.bfloat16)
    gap = pltpu.VMEM((block_rows, block_rows), jnp.int32)
    sums = jax.ShapeDtypeStruct((total_rows, HEAD), jnp.float32)

    def backward(parts, name, out_shape, scratch, *before):
        return call(
            functools.partial(backward_kernel, nz, parts, not before),
            name,
            [bf16(rows, width)] * len(parts) + out_shape,
            [SMEM] + [VMEM] * (len(parts) + nz + len(before)),
            stretch_order,
            *[queries[d] for d in parts],
            *back_stacks,
            *before,
            scratch=scratch
            + sequence
            + [
                pltpu.VMEM((total_rows // block_rows, HEAD, block_rows), jnp.bfloat16),
                pltpu.VMEM((2 * len(parts), block_rows, HEAD), jnp.bfloat16),
                pltpu.VMEM((2 * len(parts), block_rows, HEAD), jnp.bfloat16),
                pltpu.VMEM((2 * len(parts), HEAD, block_rows), jnp.float32),
                gap,
            ],
            flops=5 * pairs * HEAD,
            transcendentals=pairs,
        )

    far = backward((0, 2), "backward_first", [sums] * 2, [])
    far, up, down, gate_before = lax.optimization_barrier((far, up, down, gate_before))
    while len(up) <= ahead:
        up.append(ring_up(up[-1]))
    while len(up) + len(down) < nz:
        down.append(ring_down(down[-1]))
    stacks = up + down[::-1]
    far_piece = swap_one(far[1], 2)
    near = backward(
        (1, 3),
        "backward_second",
        [bf16(QUAD * rows, 2 * HEAD)] * nz,
        [pltpu.VMEM(sums.shape, jnp.float32)] * 2,
        *far[2:],
    )
    near, stacks, far_piece = lax.optimization_barrier((near, stacks, far_piece))
    query_pieces, key_parts = [far[0], near[0], far_piece, swap_one(near[1], 3)], near[2:]
    key_sums = reduce_first(key_parts)
    parts = tuple(range(QUAD))
    attended = call(
        functools.partial(forward_kernel, nz, parts),
        "forward",
        [bf16(rows, width)] * QUAD,
        [SMEM] + [VMEM] * (QUAD + nz),
        stretch_order,
        *queries,
        *stacks,
        scratch=sequence
        + [stacked, pltpu.VMEM((2 * QUAD, block_rows, HEAD), jnp.float32), gap],
    )
    attended, key_up, query_pieces = lax.optimization_barrier(
        (attended, key_sums[0], query_pieces)
    )
    attended = [hand(attended[d], d) for d in range(QUAD)]
    attended[0], query_pieces[1] = lax.optimization_barrier((attended[0], query_pieces[1]))
    query_pieces[1] = swap_one(query_pieces[1], 1)
    (handed,) = call(
        gate_kernel,
        "gate",
        [bf16(*gate_fwd.shape)],
        [VMEM] * (QUAD + 1),
        *attended,
        gate_before,
    )
    key_sums = reduce_rest(key_parts, key_up, key_sums[1])
    key_pieces = swap(
        call(
            sum_kernel,
            "sum_key_parts",
            [bf16(rows, 2 * HEAD)] * QUAD,
            [VMEM] * 3,
            *key_sums,
        )
    )
    (query_grad,) = call(
        query_grad_kernel,
        "query_grad",
        [bf16(*query_bwd.shape)],
        [VMEM] * QUAD,
        *query_pieces,
    )
    key_grad, value_grad = call(
        key_grad_kernel,
        "key_grad",
        [bf16(*key_bwd.shape), bf16(*value_bwd.shape)],
        [VMEM] * QUAD,
        *key_pieces,
    )
    return handed, query_grad, key_grad, value_grad


def solution(mesh):
    rows = P("pipe", "ctx", None)
    types = P("pipe", "ctx")
    return jax.shard_map(
        body,
        mesh=mesh,
        in_specs=(
            rows,
            rows,
            rows,
            rows,
            types,
            rows,
            rows,
            rows,
            rows,
            types,
            P("pipe", None, None),
            P("pipe", None),
            P("pipe", None),
        ),
        out_specs=(rows, rows, rows, rows),
        check_vma=False,
    )
```

```python
import functools
import math

import jax
import jax.numpy as jnp
from jax import lax
from jax.experimental import pallas as pl
from jax.experimental.pallas import tpu as pltpu
from jax.sharding import PartitionSpec as P

HEAD = 128
QUAD = 4
SCALE = HEAD ** (-0.5)
EXP2_SCALE = -SCALE / math.log(2.0)
GAIN_ROWS = 16
norm_eps = 1e-06

VMEM = pl.BlockSpec(memory_space=pltpu.VMEM)
HBM = pl.BlockSpec(memory_space=pltpu.HBM)
SMEM = pl.BlockSpec(memory_space=pltpu.SMEM)
MIB = 1024 * 1024

NN = (((1,), (0,)), ((), ()))
NT = (((1,), (1,)), ((), ()))
TN = (((0,), (0,)), ((), ()))


def dot(a, b, dims):
    return lax.dot_general(a, b, dims, preferred_element_type=jnp.float32)


def bf16(*shape):
    return jax.ShapeDtypeStruct(shape, jnp.bfloat16)


def place():
    index = lax.axis_index("ctx")
    return index // QUAD, index % QUAD


def columns(index, width):
    return pl.ds(pl.multiple_of(index * width, width), width)


def pack_keys(key_ref, value_ref, types_ref, table_ref, *refs):
    pieces, (keys, types, table, typed, arrived, placed) = refs[:QUAD], refs[QUAD:]
    _, member = place()
    copies = [
        pltpu.make_async_copy(source, target, arrived.at[i])
        for i, (source, target) in enumerate(
            [(types_ref, types), (table_ref.at[0], table), (key_ref.at[0], keys)]
        )
    ]
    placements = [
        pltpu.make_async_copy(
            value_ref.at[0, :, columns(member ^ d, HEAD)], pieces[d].at[:, HEAD:], placed.at[d]
        )
        for d in range(QUAD)
    ]
    for copy in copies + placements:
        copy.start()
    for copy in copies:
        copy.wait()
    onehot = (
        lax.broadcasted_iota(jnp.int32, (table.shape[0], types.shape[1]), 0) == types[...]
    ).astype(jnp.float32).astype(jnp.bfloat16)
    type_rows = dot(onehot, table[...], TN)
    typed[...] = (keys[...].astype(jnp.float32) + type_rows).astype(jnp.bfloat16)
    for d in range(QUAD):
        pieces[d][:, :HEAD] = typed[:, columns(member ^ d, HEAD)]
    for copy in placements:
        copy.wait()


def stack_keys(*refs):
    pieces, (out, placed) = refs[:QUAD], refs[QUAD:]
    rows = pieces[0].shape[0]
    copies = [
        pltpu.make_async_copy(pieces[d], out.at[d * rows : (d + 1) * rows, :], placed.at[d])
        for d in range(QUAD)
    ]
    for copy in copies:
        copy.start()
    for copy in copies:
        copy.wait()


def pack_queries(query_ref, grad_ref, forward_ref, gate_ref, gain_ref, *refs):
    pieces, (gate_out, placed) = refs[:QUAD], refs[QUAD:]
    _, member = place()
    width = query_ref.shape[2] // QUAD
    rows = gate_ref.shape[1]
    copies = [
        pltpu.make_async_copy(
            source.at[0, :, columns(member ^ d, width)],
            pieces[d].at[:, i * width : (i + 1) * width],
            placed.at[3 * d + i],
        )
        for d in reversed(range(QUAD))
        for i, source in enumerate([query_ref, grad_ref, forward_ref])
    ]
    copies.append(
        pltpu.make_async_copy(gate_ref.at[0], gate_out.at[:rows, :], placed.at[3 * QUAD])
    )
    for copy in copies:
        copy.start()
    rest = gain_ref[...]
    parts = []
    for _ in range(3):
        part = rest.astype(jnp.bfloat16).astype(jnp.float32)
        parts.append(part)
        rest = rest - part
    parts.append(jnp.zeros((GAIN_ROWS - 3, rest.shape[1]), jnp.float32))
    gate_out[rows:, :] = jnp.concatenate(parts, axis=0).astype(jnp.bfloat16)
    for copy in copies:
        copy.wait()


def stretch_of(order_ref, quad_index, member, d, e):
    return order_ref[0, 2 * (quad_index * QUAD + (member ^ d)) + e]


def rows_at(index, count):
    return pl.ds(pl.multiple_of(index * count, count), count)


def in_sequence(order_ref, stacks, stretch_rows, keys, values):
    z, member = place()
    nz = len(stacks)
    for s, stack in enumerate(stacks):
        source = lax.rem(z - s + nz, nz)
        for d in range(QUAD):
            for e in range(2):
                rows = rows_at(stretch_of(order_ref, source, member, d, e), stretch_rows)
                lower = (2 * d + e) * stretch_rows
                keys[rows, :] = stack[lower : lower + stretch_rows, :HEAD]
                values[rows, :] = stack[lower : lower + stretch_rows, HEAD:]


def shrink_of(stretch, stretch_rows):
    pos = stretch * stretch_rows + lax.broadcasted_iota(jnp.int32, (stretch_rows, HEAD), 0)
    return lax.rsqrt((pos + 1).astype(jnp.float32))


def step_place(first, second, step, d, groups):
    blocks = first // groups + 1
    late = step >= blocks
    row = jnp.where(late, 2 * d + 1, 2 * d)
    stretch = jnp.where(late, second, first)
    block = jnp.where(late, step - blocks, step)
    return row, stretch, block


def sigmoid_of(raw, visible):
    part = pl.reciprocal(1.0 + jnp.exp2(raw * EXP2_SCALE), approx=True)
    return jnp.where(visible, part, 0.0)


def repeat(steps, together, advance):
    def several(i, _):
        for j in range(together):
            advance(i * together + j)
        return 0

    lax.fori_loop(0, steps // together, several, 0)
    for step in range(steps // together * together, steps):
        advance(step)


def forward_kernel(nz, parts, order_ref, *refs):
    queries, refs = refs[: len(parts)], refs[len(parts) :]
    stacks, refs = refs[:nz], refs[nz:]
    outs, refs = refs[: len(parts)], refs[len(parts) :]
    keys, values, stacked, total, gap = refs
    z, member = place()
    stretch_rows = queries[0].shape[0] // 2
    groups = outs[0].shape[1] // HEAD
    block_rows = groups * stretch_rows
    steps = keys.shape[0] // block_rows + 1
    in_sequence(order_ref, stacks, stretch_rows, keys, values)
    offset = 2 * groups * HEAD
    for i in range(len(parts)):
        for e in range(2):
            for g in range(groups):
                stacked[2 * i + e, g * stretch_rows : (g + 1) * stretch_rows, :] = queries[i][
                    e * stretch_rows : (e + 1) * stretch_rows,
                    offset + g * HEAD : offset + (g + 1) * HEAD,
                ]
    total[...] = jnp.zeros_like(total)
    gap[...] = lax.broadcasted_iota(jnp.int32, gap.shape, 1) - lax.rem(
        lax.broadcasted_iota(jnp.int32, gap.shape, 0), stretch_rows
    )

    def advance(step):
        for i, d in enumerate(parts):
            row, stretch, block = step_place(
                stretch_of(order_ref, z, member, d, 0),
                stretch_of(order_ref, z, member, d, 1),
                step,
                i,
                groups,
            )
            rows = rows_at(block, block_rows)
            raw = dot(stacked[row], keys[rows, :], NT)
            visible = gap[...] <= stretch * stretch_rows - block * block_rows
            weights = (raw * sigmoid_of(raw, visible)).astype(jnp.bfloat16)
            total[row] += dot(weights, values[rows, :], NN)

    repeat(steps, 9, advance)
    for i, d in enumerate(parts):
        for e in range(2):
            shrink = SCALE * shrink_of(stretch_of(order_ref, z, member, d, e), stretch_rows)
            for g in range(groups):
                outs[i][e * stretch_rows : (e + 1) * stretch_rows, g * HEAD : (g + 1) * HEAD] = (
                    total[2 * i + e, g * stretch_rows : (g + 1) * stretch_rows, :] * shrink
                ).astype(jnp.bfloat16)


def backward_kernel(nz, parts, first, order_ref, *refs):
    queries, refs = refs[: len(parts)], refs[len(parts) :]
    stacks, refs = refs[:nz], refs[nz:]
    if first:
        query_outs, refs = refs[: len(parts)], refs[len(parts) :]
        key_total, value_total, keys, values, keys_t, stacked, grads, total_t, gap = refs
        key_total[...] = jnp.zeros_like(key_total)
        value_total[...] = jnp.zeros_like(value_total)
    else:
        (key_before, value_before), refs = refs[:2], refs[2:]
        query_outs, refs = refs[: len(parts)], refs[len(parts) :]
        key_outs, refs = refs[:nz], refs[nz:]
        key_total, value_total, keys, values, keys_t, stacked, grads, total_t, gap = refs
        key_total[...] = key_before[...]
        value_total[...] = value_before[...]
    z, member = place()
    stretch_rows = queries[0].shape[0] // 2
    groups = query_outs[0].shape[1] // HEAD
    block_rows = groups * stretch_rows
    blocks = keys.shape[0] // block_rows
    steps = blocks + 1
    in_sequence(order_ref, stacks, stretch_rows, keys, values)
    for block in range(blocks):
        lower = block * block_rows
        keys_t[block] = keys[lower : lower + block_rows, :].T
    offset = groups * HEAD
    for i, d in enumerate(parts):
        for e in range(2):
            shrink = shrink_of(stretch_of(order_ref, z, member, d, e), stretch_rows)
            rows = slice(e * stretch_rows, (e + 1) * stretch_rows)
            for g in range(groups):
                into = slice(g * stretch_rows, (g + 1) * stretch_rows)
                stacked[2 * i + e, into, :] = queries[i][rows, g * HEAD : (g + 1) * HEAD]
                grads[2 * i + e, into, :] = (
                    queries[i][rows, offset + g * HEAD : offset + (g + 1) * HEAD].astype(
                        jnp.float32
                    )
                    * shrink
                ).astype(jnp.bfloat16)
    total_t[...] = jnp.zeros_like(total_t)
    gap[...] = lax.broadcasted_iota(jnp.int32, gap.shape, 0) - lax.rem(
        lax.broadcasted_iota(jnp.int32, gap.shape, 1), stretch_rows
    )

    def advance(step):
        for i, d in enumerate(parts):
            row, stretch, block = step_place(
                stretch_of(order_ref, z, member, d, 0),
                stretch_of(order_ref, z, member, d, 1),
                step,
                i,
                groups,
            )
            rows = rows_at(block, block_rows)
            raw = dot(keys[rows, :], stacked[row], NT)
            weight_grad = dot(values[rows, :], grads[row], NT)
            visible = gap[...] <= stretch * stretch_rows - block * block_rows
            part = sigmoid_of(raw, visible)
            weights = raw * SCALE * part
            score_grad = (weight_grad * (part + weights * (1.0 - part))).astype(jnp.bfloat16)
            weights = weights.astype(jnp.bfloat16)
            total_t[row] += dot(keys_t[block], score_grad, NN)
            key_total[rows, :] += dot(score_grad, stacked[row], NN)
            value_total[rows, :] += dot(weights, grads[row], NN)

    repeat(steps, 9, advance)
    for i in range(len(parts)):
        for e in range(2):
            query_grad = (total_t[2 * i + e].T * SCALE).astype(jnp.bfloat16)
            for g in range(groups):
                query_outs[i][
                    e * stretch_rows : (e + 1) * stretch_rows, g * HEAD : (g + 1) * HEAD
                ] = query_grad[g * stretch_rows : (g + 1) * stretch_rows, :]
    if first:
        return
    for s in range(nz):
        target = lax.rem(z + s, nz)
        for d in range(QUAD):
            for e in range(2):
                rows = rows_at(stretch_of(order_ref, target, member, d, e), stretch_rows)
                lower = (2 * d + e) * stretch_rows
                key_outs[s][lower : lower + stretch_rows, :HEAD] = (
                    key_total[rows, :] * SCALE
                ).astype(jnp.bfloat16)
                key_outs[s][lower : lower + stretch_rows, HEAD:] = value_total[rows, :].astype(
                    jnp.bfloat16
                )


def sum_kernel(*refs):
    parts, pieces = refs[:3], refs[3:]
    rows = pieces[0].shape[0]
    for d in range(QUAD):
        lower = d * rows
        pieces[d][...] = sum(
            part[lower : lower + rows, :].astype(jnp.float32) for part in parts
        ).astype(jnp.bfloat16)


def key_grad_kernel(*refs):
    pieces, (key_out, value_out) = refs[:QUAD], refs[QUAD:]
    _, member = place()
    for d in range(QUAD):
        head = columns(member ^ d, HEAD)
        key_out[0, :, head] = pieces[d][:, :HEAD]
        value_out[0, :, head] = pieces[d][:, HEAD:]


def query_grad_kernel(*refs):
    pieces, out = refs[:QUAD], refs[QUAD]
    _, member = place()
    for d in range(QUAD):
        out[0, :, columns(member ^ d, pieces[d].shape[1])] = pieces[d][...]


def gate_kernel(*refs):
    pieces, (gate_ref, out) = refs[:QUAD], refs[QUAD:]
    _, member = place()
    rows = out.shape[1]
    attended = [piece[...].astype(jnp.float32) for piece in pieces]
    square = sum(jnp.sum(part * part, axis=1, keepdims=True) for part in attended)
    factor = lax.rsqrt(square / out.shape[2] + norm_eps)
    for d in range(QUAD):
        head = columns(member ^ d, pieces[d].shape[1])
        gain = sum(gate_ref[rows : rows + GAIN_ROWS, head].astype(jnp.float32)[i : i + 1] for i in range(3))
        out[0, :, head] = (
            attended[d] * factor * gain * gate_ref[:rows, head].astype(jnp.float32)
        ).astype(jnp.bfloat16)


def call(kernel, name, out_shape, specs, *args, scratch=(), flops=0, transcendentals=0, vmem=40):
    size = sum(a.size * a.dtype.itemsize for a in args)
    size += sum(math.prod(o.shape) * o.dtype.itemsize for o in out_shape)
    return pl.pallas_call(
        kernel,
        name=name,
        out_shape=out_shape,
        in_specs=specs,
        out_specs=[VMEM] * len(out_shape),
        scratch_shapes=list(scratch),
        compiler_params=pltpu.CompilerParams(vmem_limit_bytes=vmem * MIB),
        cost_estimate=pl.CostEstimate(
            flops=flops, bytes_accessed=size, transcendentals=transcendentals
        ),
    )(*args)


def body(
    query_fwd,
    key_fwd,
    value_fwd,
    gate_fwd,
    types_fwd,
    query_bwd,
    key_bwd,
    value_bwd,
    grad_out,
    types_bwd,
    type_key,
    norm_gain,
    stretch_order,
):
    devices = lax.axis_size("ctx")
    nz = devices // QUAD
    rows = query_fwd.shape[1]
    total_rows = rows * devices
    width = query_fwd.shape[2] // QUAD
    groups = width // HEAD
    stretch_rows = rows // 2
    block_rows = groups * stretch_rows
    steps = total_rows // block_rows + 1
    pairs = steps * QUAD * block_rows * block_rows

    def swap_one(piece, d):
        return lax.ppermute(piece, "ctx", [(i, i ^ d) for i in range(devices)])

    def swap(pieces):
        return [pieces[0]] + [swap_one(pieces[d], d) for d in range(1, QUAD)]

    def turn(block, s):
        return lax.ppermute(
            block, "ctx", [(i, (i + s * QUAD) % devices) for i in range(devices)]
        )

    def hand(block, d):
        sections = lax.axis_size("pipe")
        route = [
            (i * sections + p, (i ^ d) * sections + (p + 1) % sections)
            for i in range(devices)
            for p in range(sections)
        ]
        return lax.ppermute(block, ("ctx", "pipe"), route)

    ahead = nz // 2

    def ring_up(block):
        return turn(block, 1)

    def ring_down(block):
        return turn(block, nz - 1)

    def reduce_first(parts):
        return ring_up(parts[ahead]), ring_down(parts[ahead + 1])

    def add(a, b):
        return (a.astype(jnp.float32) + b.astype(jnp.float32)).astype(jnp.bfloat16)

    def reduce_rest(parts, up, down):
        for s in range(ahead - 1, 0, -1):
            up = ring_up(add(up, parts[s]))
        for s in range(ahead + 2, nz):
            down = ring_down(add(down, parts[s]))
        return parts[0], up, down

    def gather(stack):
        return [stack] + [turn(stack, s) for s in range(1, nz)]

    def gather_ring(up):
        down = [ring_down(up[0])]
        while len(up) <= ahead:
            up.append(ring_up(up[-1]))
        while len(up) + len(down) < nz:
            down.append(ring_down(down[-1]))
        return up + down[::-1]

    def pack(key, value, types, name):
        return call(
            pack_keys,
            name,
            [bf16(rows, 2 * HEAD)] * QUAD,
            [HBM] * 4,
            key,
            value,
            types,
            type_key,
            scratch=[
                pltpu.VMEM(key.shape[1:], jnp.bfloat16),
                pltpu.VMEM(types.shape, jnp.int32),
                pltpu.VMEM(type_key.shape[1:], jnp.bfloat16),
                pltpu.VMEM(key.shape[1:], jnp.bfloat16),
                pltpu.SemaphoreType.DMA((3,)),
                pltpu.SemaphoreType.DMA((QUAD,)),
            ],
            vmem=60,
        )

    def stacked_keys(pieces, name):
        return call(
            stack_keys,
            name,
            [bf16(QUAD * rows, 2 * HEAD)],
            [HBM] * QUAD,
            *pieces,
            scratch=[pltpu.SemaphoreType.DMA((QUAD,))],
        )[0]

    back_pieces = swap(pack(key_bwd, value_bwd, types_bwd, "pack_keys_bwd"))
    pieces = pack(key_fwd, value_fwd, types_fwd, "pack_keys_fwd")
    back_pieces, pieces = lax.optimization_barrier((back_pieces, pieces))
    pieces = swap(pieces)
    packed = call(
        pack_queries,
        "pack_queries",
        [bf16(rows, 3 * width)] * QUAD + [bf16(rows + GAIN_ROWS, QUAD * width)],
        [HBM] * 4 + [VMEM],
        query_bwd,
        grad_out,
        query_fwd,
        gate_fwd,
        norm_gain,
        scratch=[pltpu.SemaphoreType.DMA((3 * QUAD + 1,))],
        vmem=60,
    )
    packed = list(packed)
    back_stack = stacked_keys(back_pieces, "stack_keys_bwd")
    up = [back_stack, ring_up(back_stack)]
    up, pieces, packed = lax.optimization_barrier((up, pieces, packed))
    back_stacks = gather_ring(up)
    stack = stacked_keys(pieces, "stack_keys_fwd")
    back_stacks, stack, packed[1], packed[QUAD] = lax.optimization_barrier(
        (back_stacks, stack, packed[1], packed[QUAD])
    )
    queries = swap(packed[:QUAD])
    up, down = [stack, ring_up(stack)], [ring_down(stack)]
    gate_before = hand(packed[QUAD], 0)

    sequence = [pltpu.VMEM((total_rows, HEAD), jnp.bfloat16)] * 2
    stacked = pltpu.VMEM((2 * QUAD, block_rows, HEAD), jnp.bfloat16)
    gap = pltpu.VMEM((block_rows, block_rows), jnp.int32)
    sums = jax.ShapeDtypeStruct((total_rows, HEAD), jnp.float32)

    def backward(parts, name, out_shape, scratch, *before):
        return call(
            functools.partial(backward_kernel, nz, parts, not before),
            name,
            [bf16(rows, width)] * len(parts) + out_shape,
            [SMEM] + [VMEM] * (len(parts) + nz + len(before)),
            stretch_order,
            *[queries[d] for d in parts],
            *back_stacks,
            *before,
            scratch=scratch
            + sequence
            + [
                pltpu.VMEM((total_rows // block_rows, HEAD, block_rows), jnp.bfloat16),
                pltpu.VMEM((2 * len(parts), block_rows, HEAD), jnp.bfloat16),
                pltpu.VMEM((2 * len(parts), block_rows, HEAD), jnp.bfloat16),
                pltpu.VMEM((2 * len(parts), HEAD, block_rows), jnp.float32),
                gap,
            ],
            flops=5 * pairs * HEAD,
            transcendentals=pairs,
        )

    far = backward((0, 2), "backward_first", [sums] * 2, [])
    far, up, down, gate_before = lax.optimization_barrier((far, up, down, gate_before))
    while len(up) <= ahead:
        up.append(ring_up(up[-1]))
    while len(up) + len(down) < nz:
        down.append(ring_down(down[-1]))
    stacks = up + down[::-1]
    far_piece = swap_one(far[1], 2)
    near = backward(
        (1, 3),
        "backward_second",
        [bf16(QUAD * rows, 2 * HEAD)] * nz,
        [pltpu.VMEM(sums.shape, jnp.float32)] * 2,
        *far[2:],
    )
    near, stacks, far_piece = lax.optimization_barrier((near, stacks, far_piece))
    query_pieces, key_parts = [far[0], swap_one(near[0], 1), far_piece, swap_one(near[1], 3)], near[2:]
    key_sums = reduce_first(key_parts)
    parts = tuple(range(QUAD))
    attended = call(
        functools.partial(forward_kernel, nz, parts),
        "forward",
        [bf16(rows, width)] * QUAD,
        [SMEM] + [VMEM] * (QUAD + nz),
        stretch_order,
        *queries,
        *stacks,
        scratch=sequence
        + [stacked, pltpu.VMEM((2 * QUAD, block_rows, HEAD), jnp.float32), gap],
    )
    attended, key_up, query_pieces = lax.optimization_barrier(
        (attended, key_sums[0], query_pieces)
    )
    attended = [hand(attended[d], d) for d in range(QUAD)]
    (query_grad,) = call(
        query_grad_kernel,
        "query_grad",
        [bf16(*query_bwd.shape)],
        [VMEM] * QUAD,
        *query_pieces,
    )
    attended, query_grad = lax.optimization_barrier((attended, query_grad))
    (handed,) = call(
        gate_kernel,
        "gate",
        [bf16(*gate_fwd.shape)],
        [VMEM] * (QUAD + 1),
        *attended,
        gate_before,
    )
    key_sums = reduce_rest(key_parts, key_up, key_sums[1])
    key_pieces = swap(
        call(
            sum_kernel,
            "sum_key_parts",
            [bf16(rows, 2 * HEAD)] * QUAD,
            [VMEM] * 3,
            *key_sums,
        )
    )
    key_grad, value_grad = call(
        key_grad_kernel,
        "key_grad",
        [bf16(*key_bwd.shape), bf16(*value_bwd.shape)],
        [VMEM] * QUAD,
        *key_pieces,
    )
    return handed, query_grad, key_grad, value_grad


def solution(mesh):
    rows = P("pipe", "ctx", None)
    types = P("pipe", "ctx")
    return jax.shard_map(
        body,
        mesh=mesh,
        in_specs=(
            rows,
            rows,
            rows,
            rows,
            types,
            rows,
            rows,
            rows,
            rows,
            types,
            P("pipe", None, None),
            P("pipe", None),
            P("pipe", None),
        ),
        out_specs=(rows, rows, rows, rows),
        check_vma=False,
    )
```

```python
import functools
import math

import jax
import jax.numpy as jnp
from jax import lax
from jax.experimental import pallas as pl
from jax.experimental.pallas import tpu as pltpu
from jax.sharding import PartitionSpec as P

HEAD = 128
QUAD = 4
SCALE = HEAD ** (-0.5)
EXP2_SCALE = -SCALE / math.log(2.0)
GAIN_ROWS = 16
norm_eps = 1e-06

VMEM = pl.BlockSpec(memory_space=pltpu.VMEM)
HBM = pl.BlockSpec(memory_space=pltpu.HBM)
SMEM = pl.BlockSpec(memory_space=pltpu.SMEM)
MIB = 1024 * 1024

NN = (((1,), (0,)), ((), ()))
NT = (((1,), (1,)), ((), ()))
TN = (((0,), (0,)), ((), ()))


def dot(a, b, dims):
    return lax.dot_general(a, b, dims, preferred_element_type=jnp.float32)


def bf16(*shape):
    return jax.ShapeDtypeStruct(shape, jnp.bfloat16)


def place():
    index = lax.axis_index("ctx")
    return index // QUAD, index % QUAD


def columns(index, width):
    return pl.ds(pl.multiple_of(index * width, width), width)


def pack_keys(key_ref, value_ref, types_ref, table_ref, *refs):
    pieces, (keys, types, table, typed, arrived, placed) = refs[:QUAD], refs[QUAD:]
    _, member = place()
    copies = [
        pltpu.make_async_copy(source, target, arrived.at[i])
        for i, (source, target) in enumerate(
            [(types_ref, types), (table_ref.at[0], table), (key_ref.at[0], keys)]
        )
    ]
    placements = [
        pltpu.make_async_copy(
            value_ref.at[0, :, columns(member ^ d, HEAD)], pieces[d].at[:, HEAD:], placed.at[d]
        )
        for d in range(QUAD)
    ]
    for copy in copies + placements:
        copy.start()
    for copy in copies:
        copy.wait()
    onehot = (
        lax.broadcasted_iota(jnp.int32, (table.shape[0], types.shape[1]), 0) == types[...]
    ).astype(jnp.float32).astype(jnp.bfloat16)
    type_rows = dot(onehot, table[...], TN)
    typed[...] = (keys[...].astype(jnp.float32) + type_rows).astype(jnp.bfloat16)
    for d in range(QUAD):
        pieces[d][:, :HEAD] = typed[:, columns(member ^ d, HEAD)]
    for copy in placements:
        copy.wait()


def stack_keys(*refs):
    pieces, (out, placed) = refs[:QUAD], refs[QUAD:]
    rows = pieces[0].shape[0]
    copies = [
        pltpu.make_async_copy(pieces[d], out.at[d * rows : (d + 1) * rows, :], placed.at[d])
        for d in range(QUAD)
    ]
    for copy in copies:
        copy.start()
    for copy in copies:
        copy.wait()


def pack_queries(query_ref, grad_ref, forward_ref, gate_ref, gain_ref, *refs):
    pieces, (gate_out, placed) = refs[:QUAD], refs[QUAD:]
    _, member = place()
    width = query_ref.shape[2] // QUAD
    rows = gate_ref.shape[1]
    copies = [
        pltpu.make_async_copy(
            source.at[0, :, columns(member ^ d, width)],
            pieces[d].at[:, i * width : (i + 1) * width],
            placed.at[3 * d + i],
        )
        for d in reversed(range(QUAD))
        for i, source in enumerate([query_ref, grad_ref, forward_ref])
    ]
    copies.append(
        pltpu.make_async_copy(gate_ref.at[0], gate_out.at[:rows, :], placed.at[3 * QUAD])
    )
    for copy in copies:
        copy.start()
    rest = gain_ref[...]
    parts = []
    for _ in range(3):
        part = rest.astype(jnp.bfloat16).astype(jnp.float32)
        parts.append(part)
        rest = rest - part
    parts.append(jnp.zeros((GAIN_ROWS - 3, rest.shape[1]), jnp.float32))
    gate_out[rows:, :] = jnp.concatenate(parts, axis=0).astype(jnp.bfloat16)
    for copy in copies:
        copy.wait()


def stretch_of(order_ref, quad_index, member, d, e):
    return order_ref[0, 2 * (quad_index * QUAD + (member ^ d)) + e]


def rows_at(index, count):
    return pl.ds(pl.multiple_of(index * count, count), count)


def in_sequence(order_ref, stacks, stretch_rows, keys, values):
    z, member = place()
    nz = len(stacks)
    for s, stack in enumerate(stacks):
        source = lax.rem(z - s + nz, nz)
        for d in range(QUAD):
            for e in range(2):
                rows = rows_at(stretch_of(order_ref, source, member, d, e), stretch_rows)
                lower = (2 * d + e) * stretch_rows
                keys[rows, :] = stack[lower : lower + stretch_rows, :HEAD]
                values[rows, :] = stack[lower : lower + stretch_rows, HEAD:]


def shrink_of(stretch, stretch_rows):
    pos = stretch * stretch_rows + lax.broadcasted_iota(jnp.int32, (stretch_rows, HEAD), 0)
    return lax.rsqrt((pos + 1).astype(jnp.float32))


def step_place(first, second, step, d, groups):
    blocks = first // groups + 1
    late = step >= blocks
    row = jnp.where(late, 2 * d + 1, 2 * d)
    stretch = jnp.where(late, second, first)
    block = jnp.where(late, step - blocks, step)
    return row, stretch, block


def sigmoid_of(raw, visible):
    part = pl.reciprocal(1.0 + jnp.exp2(raw * EXP2_SCALE), approx=True)
    return jnp.where(visible, part, 0.0)


def repeat(steps, together, advance):
    def several(i, _):
        for j in range(together):
            advance(i * together + j)
        return 0

    lax.fori_loop(0, steps // together, several, 0)
    for step in range(steps // together * together, steps):
        advance(step)


def forward_kernel(nz, parts, order_ref, *refs):
    queries, refs = refs[: len(parts)], refs[len(parts) :]
    stacks, refs = refs[:nz], refs[nz:]
    outs, refs = refs[: len(parts)], refs[len(parts) :]
    keys, values, stacked, total, gap = refs
    z, member = place()
    stretch_rows = queries[0].shape[0] // 2
    groups = outs[0].shape[1] // HEAD
    block_rows = groups * stretch_rows
    steps = keys.shape[0] // block_rows + 1
    in_sequence(order_ref, stacks, stretch_rows, keys, values)
    offset = 2 * groups * HEAD
    for i in range(len(parts)):
        for e in range(2):
            for g in range(groups):
                stacked[2 * i + e, g * stretch_rows : (g + 1) * stretch_rows, :] = queries[i][
                    e * stretch_rows : (e + 1) * stretch_rows,
                    offset + g * HEAD : offset + (g + 1) * HEAD,
                ]
    total[...] = jnp.zeros_like(total)
    gap[...] = lax.broadcasted_iota(jnp.int32, gap.shape, 1) - lax.rem(
        lax.broadcasted_iota(jnp.int32, gap.shape, 0), stretch_rows
    )

    def advance(step):
        for i, d in enumerate(parts):
            row, stretch, block = step_place(
                stretch_of(order_ref, z, member, d, 0),
                stretch_of(order_ref, z, member, d, 1),
                step,
                i,
                groups,
            )
            rows = rows_at(block, block_rows)
            raw = dot(stacked[row], keys[rows, :], NT)
            visible = gap[...] <= stretch * stretch_rows - block * block_rows
            weights = (raw * sigmoid_of(raw, visible)).astype(jnp.bfloat16)
            total[row] += dot(weights, values[rows, :], NN)

    repeat(steps, 9, advance)
    for i, d in enumerate(parts):
        for e in range(2):
            shrink = SCALE * shrink_of(stretch_of(order_ref, z, member, d, e), stretch_rows)
            for g in range(groups):
                outs[i][e * stretch_rows : (e + 1) * stretch_rows, g * HEAD : (g + 1) * HEAD] = (
                    total[2 * i + e, g * stretch_rows : (g + 1) * stretch_rows, :] * shrink
                ).astype(jnp.bfloat16)


def backward_kernel(nz, parts, first, order_ref, *refs):
    queries, refs = refs[: len(parts)], refs[len(parts) :]
    stacks, refs = refs[:nz], refs[nz:]
    if first:
        query_outs, refs = refs[: len(parts)], refs[len(parts) :]
        key_total, value_total, keys, values, keys_t, stacked, grads, total_t, gap = refs
        key_total[...] = jnp.zeros_like(key_total)
        value_total[...] = jnp.zeros_like(value_total)
    else:
        (key_before, value_before), refs = refs[:2], refs[2:]
        query_outs, refs = refs[: len(parts)], refs[len(parts) :]
        key_outs, refs = refs[:nz], refs[nz:]
        key_total, value_total, keys, values, keys_t, stacked, grads, total_t, gap = refs
        key_total[...] = key_before[...]
        value_total[...] = value_before[...]
    z, member = place()
    stretch_rows = queries[0].shape[0] // 2
    groups = query_outs[0].shape[1] // HEAD
    block_rows = groups * stretch_rows
    blocks = keys.shape[0] // block_rows
    steps = blocks + 1
    in_sequence(order_ref, stacks, stretch_rows, keys, values)
    for block in range(blocks):
        lower = block * block_rows
        keys_t[block] = keys[lower : lower + block_rows, :].T
    offset = groups * HEAD
    for i, d in enumerate(parts):
        for e in range(2):
            shrink = shrink_of(stretch_of(order_ref, z, member, d, e), stretch_rows)
            rows = slice(e * stretch_rows, (e + 1) * stretch_rows)
            for g in range(groups):
                into = slice(g * stretch_rows, (g + 1) * stretch_rows)
                stacked[2 * i + e, into, :] = queries[i][rows, g * HEAD : (g + 1) * HEAD]
                grads[2 * i + e, into, :] = (
                    queries[i][rows, offset + g * HEAD : offset + (g + 1) * HEAD].astype(
                        jnp.float32
                    )
                    * shrink
                ).astype(jnp.bfloat16)
    total_t[...] = jnp.zeros_like(total_t)
    gap[...] = lax.broadcasted_iota(jnp.int32, gap.shape, 0) - lax.rem(
        lax.broadcasted_iota(jnp.int32, gap.shape, 1), stretch_rows
    )

    def advance(step):
        for i, d in enumerate(parts):
            row, stretch, block = step_place(
                stretch_of(order_ref, z, member, d, 0),
                stretch_of(order_ref, z, member, d, 1),
                step,
                i,
                groups,
            )
            rows = rows_at(block, block_rows)
            raw = dot(keys[rows, :], stacked[row], NT)
            weight_grad = dot(values[rows, :], grads[row], NT)
            visible = gap[...] <= stretch * stretch_rows - block * block_rows
            part = sigmoid_of(raw, visible)
            weights = raw * SCALE * part
            score_grad = (weight_grad * (part + weights * (1.0 - part))).astype(jnp.bfloat16)
            weights = weights.astype(jnp.bfloat16)
            total_t[row] += dot(keys_t[block], score_grad, NN)
            key_total[rows, :] += dot(score_grad, stacked[row], NN)
            value_total[rows, :] += dot(weights, grads[row], NN)

    repeat(steps, 9, advance)
    for i in range(len(parts)):
        for e in range(2):
            query_grad = (total_t[2 * i + e].T * SCALE).astype(jnp.bfloat16)
            for g in range(groups):
                query_outs[i][
                    e * stretch_rows : (e + 1) * stretch_rows, g * HEAD : (g + 1) * HEAD
                ] = query_grad[g * stretch_rows : (g + 1) * stretch_rows, :]
    if first:
        return
    for s in range(nz):
        target = lax.rem(z + s, nz)
        for d in range(QUAD):
            for e in range(2):
                rows = rows_at(stretch_of(order_ref, target, member, d, e), stretch_rows)
                lower = (2 * d + e) * stretch_rows
                key_outs[s][lower : lower + stretch_rows, :HEAD] = (
                    key_total[rows, :] * SCALE
                ).astype(jnp.bfloat16)
                key_outs[s][lower : lower + stretch_rows, HEAD:] = value_total[rows, :].astype(
                    jnp.bfloat16
                )


def sum_kernel(*refs):
    parts, pieces = refs[:3], refs[3:]
    rows = pieces[0].shape[0]
    for d in range(QUAD):
        lower = d * rows
        pieces[d][...] = sum(
            part[lower : lower + rows, :].astype(jnp.float32) for part in parts
        ).astype(jnp.bfloat16)


def key_grad_kernel(*refs):
    pieces, (key_out, value_out) = refs[:QUAD], refs[QUAD:]
    _, member = place()
    for d in range(QUAD):
        head = columns(member ^ d, HEAD)
        key_out[0, :, head] = pieces[d][:, :HEAD]
        value_out[0, :, head] = pieces[d][:, HEAD:]


def query_grad_kernel(*refs):
    pieces, out = refs[:QUAD], refs[QUAD]
    _, member = place()
    for d in range(QUAD):
        out[0, :, columns(member ^ d, pieces[d].shape[1])] = pieces[d][...]


def gate_kernel(*refs):
    pieces, (gate_ref, out) = refs[:QUAD], refs[QUAD:]
    _, member = place()
    rows = out.shape[1]
    attended = [piece[...].astype(jnp.float32) for piece in pieces]
    square = sum(jnp.sum(part * part, axis=1, keepdims=True) for part in attended)
    factor = lax.rsqrt(square / out.shape[2] + norm_eps)
    for d in range(QUAD):
        head = columns(member ^ d, pieces[d].shape[1])
        gain = sum(gate_ref[rows : rows + GAIN_ROWS, head].astype(jnp.float32)[i : i + 1] for i in range(3))
        out[0, :, head] = (
            attended[d] * factor * gain * gate_ref[:rows, head].astype(jnp.float32)
        ).astype(jnp.bfloat16)


def call(kernel, name, out_shape, specs, *args, scratch=(), flops=0, transcendentals=0, vmem=40):
    size = sum(a.size * a.dtype.itemsize for a in args)
    size += sum(math.prod(o.shape) * o.dtype.itemsize for o in out_shape)
    return pl.pallas_call(
        kernel,
        name=name,
        out_shape=out_shape,
        in_specs=specs,
        out_specs=[VMEM] * len(out_shape),
        scratch_shapes=list(scratch),
        compiler_params=pltpu.CompilerParams(vmem_limit_bytes=vmem * MIB),
        cost_estimate=pl.CostEstimate(
            flops=flops, bytes_accessed=size, transcendentals=transcendentals
        ),
    )(*args)


def body(
    query_fwd,
    key_fwd,
    value_fwd,
    gate_fwd,
    types_fwd,
    query_bwd,
    key_bwd,
    value_bwd,
    grad_out,
    types_bwd,
    type_key,
    norm_gain,
    stretch_order,
):
    devices = lax.axis_size("ctx")
    nz = devices // QUAD
    rows = query_fwd.shape[1]
    total_rows = rows * devices
    width = query_fwd.shape[2] // QUAD
    groups = width // HEAD
    stretch_rows = rows // 2
    block_rows = groups * stretch_rows
    steps = total_rows // block_rows + 1
    pairs = steps * QUAD * block_rows * block_rows

    def swap_one(piece, d):
        return lax.ppermute(piece, "ctx", [(i, i ^ d) for i in range(devices)])

    def swap(pieces):
        return [pieces[0]] + [swap_one(pieces[d], d) for d in range(1, QUAD)]

    def turn(block, s):
        return lax.ppermute(
            block, "ctx", [(i, (i + s * QUAD) % devices) for i in range(devices)]
        )

    def hand(block, d):
        sections = lax.axis_size("pipe")
        route = [
            (i * sections + p, (i ^ d) * sections + (p + 1) % sections)
            for i in range(devices)
            for p in range(sections)
        ]
        return lax.ppermute(block, ("ctx", "pipe"), route)

    ahead = nz // 2

    def ring_up(block):
        return turn(block, 1)

    def ring_down(block):
        return turn(block, nz - 1)

    def reduce_first(parts):
        return ring_up(parts[ahead]), ring_down(parts[ahead + 1])

    def add(a, b):
        return (a.astype(jnp.float32) + b.astype(jnp.float32)).astype(jnp.bfloat16)

    def reduce_rest(parts, up, down):
        for s in range(ahead - 1, 0, -1):
            up = ring_up(add(up, parts[s]))
        for s in range(ahead + 2, nz):
            down = ring_down(add(down, parts[s]))
        return parts[0], up, down

    def gather(stack):
        return [stack] + [turn(stack, s) for s in range(1, nz)]

    def gather_ring(up):
        down = [ring_down(up[0])]
        while len(up) <= ahead:
            up.append(ring_up(up[-1]))
        while len(up) + len(down) < nz:
            down.append(ring_down(down[-1]))
        return up + down[::-1]

    def pack(key, value, types, name):
        return call(
            pack_keys,
            name,
            [bf16(rows, 2 * HEAD)] * QUAD,
            [HBM] * 4,
            key,
            value,
            types,
            type_key,
            scratch=[
                pltpu.VMEM(key.shape[1:], jnp.bfloat16),
                pltpu.VMEM(types.shape, jnp.int32),
                pltpu.VMEM(type_key.shape[1:], jnp.bfloat16),
                pltpu.VMEM(key.shape[1:], jnp.bfloat16),
                pltpu.SemaphoreType.DMA((3,)),
                pltpu.SemaphoreType.DMA((QUAD,)),
            ],
            vmem=60,
        )

    def stacked_keys(pieces, name):
        return call(
            stack_keys,
            name,
            [bf16(QUAD * rows, 2 * HEAD)],
            [HBM] * QUAD,
            *pieces,
            scratch=[pltpu.SemaphoreType.DMA((QUAD,))],
        )[0]

    back_pieces = swap(pack(key_bwd, value_bwd, types_bwd, "pack_keys_bwd"))
    pieces = pack(key_fwd, value_fwd, types_fwd, "pack_keys_fwd")
    back_pieces, pieces = lax.optimization_barrier((back_pieces, pieces))
    pieces = swap(pieces)
    packed = call(
        pack_queries,
        "pack_queries",
        [bf16(rows, 3 * width)] * QUAD + [bf16(rows + GAIN_ROWS, QUAD * width)],
        [HBM] * 4 + [VMEM],
        query_bwd,
        grad_out,
        query_fwd,
        gate_fwd,
        norm_gain,
        scratch=[pltpu.SemaphoreType.DMA((3 * QUAD + 1,))],
        vmem=60,
    )
    packed = list(packed)
    back_stack = stacked_keys(back_pieces, "stack_keys_bwd")
    up = [back_stack, ring_up(back_stack)]
    up, pieces, packed = lax.optimization_barrier((up, pieces, packed))
    back_stacks = gather_ring(up)
    stack = stacked_keys(pieces, "stack_keys_fwd")
    back_stacks, stack, packed[1], packed[QUAD] = lax.optimization_barrier(
        (back_stacks, stack, packed[1], packed[QUAD])
    )
    queries = swap(packed[:QUAD])
    up, down = [stack, ring_up(stack)], [ring_down(stack)]
    gate_before = hand(packed[QUAD], 0)

    sequence = [pltpu.VMEM((total_rows, HEAD), jnp.bfloat16)] * 2
    stacked = pltpu.VMEM((2 * QUAD, block_rows, HEAD), jnp.bfloat16)
    gap = pltpu.VMEM((block_rows, block_rows), jnp.int32)
    sums = jax.ShapeDtypeStruct((total_rows, HEAD), jnp.float32)

    def backward(parts, name, out_shape, scratch, *before):
        return call(
            functools.partial(backward_kernel, nz, parts, not before),
            name,
            [bf16(rows, width)] * len(parts) + out_shape,
            [SMEM] + [VMEM] * (len(parts) + nz + len(before)),
            stretch_order,
            *[queries[d] for d in parts],
            *back_stacks,
            *before,
            scratch=scratch
            + sequence
            + [
                pltpu.VMEM((total_rows // block_rows, HEAD, block_rows), jnp.bfloat16),
                pltpu.VMEM((2 * len(parts), block_rows, HEAD), jnp.bfloat16),
                pltpu.VMEM((2 * len(parts), block_rows, HEAD), jnp.bfloat16),
                pltpu.VMEM((2 * len(parts), HEAD, block_rows), jnp.float32),
                gap,
            ],
            flops=5 * pairs * HEAD,
            transcendentals=pairs,
        )

    far = backward((0, 2), "backward_first", [sums] * 2, [])
    far, up, down, gate_before = lax.optimization_barrier((far, up, down, gate_before))
    while len(up) <= ahead:
        up.append(ring_up(up[-1]))
    while len(up) + len(down) < nz:
        down.append(ring_down(down[-1]))
    stacks = up + down[::-1]
    far_piece = swap_one(far[1], 2)
    near = backward(
        (1, 3),
        "backward_second",
        [bf16(QUAD * rows, 2 * HEAD)] * nz,
        [pltpu.VMEM(sums.shape, jnp.float32)] * 2,
        *far[2:],
    )
    near, stacks, far_piece = lax.optimization_barrier((near, stacks, far_piece))
    query_pieces, key_parts = [far[0], swap_one(near[0], 1), far_piece, swap_one(near[1], 3)], near[2:]
    key_sums = reduce_first(key_parts)
    parts = tuple(range(QUAD))
    attended = call(
        functools.partial(forward_kernel, nz, parts),
        "forward",
        [bf16(rows, width)] * QUAD,
        [SMEM] + [VMEM] * (QUAD + nz),
        stretch_order,
        *queries,
        *stacks,
        scratch=sequence
        + [stacked, pltpu.VMEM((2 * QUAD, block_rows, HEAD), jnp.float32), gap],
    )
    attended, key_up, query_pieces = lax.optimization_barrier(
        (attended, key_sums[0], query_pieces)
    )
    attended = [hand(attended[d], d) for d in range(QUAD)]
    (query_grad,) = call(
        query_grad_kernel,
        "query_grad",
        [bf16(*query_bwd.shape)],
        [VMEM] * QUAD,
        *query_pieces,
    )
    attended, query_grad = lax.optimization_barrier((attended, query_grad))
    (handed,) = call(
        gate_kernel,
        "gate",
        [bf16(*gate_fwd.shape)],
        [VMEM] * (QUAD + 1),
        *attended,
        gate_before,
    )
    key_sums = reduce_rest(key_parts, key_up, key_sums[1])
    key_pieces = list(
        call(
            sum_kernel,
            "sum_key_parts",
            [bf16(rows, 2 * HEAD)] * QUAD,
            [VMEM] * 3,
            *key_sums,
        )
    )
    key_pieces[1] = swap_one(key_pieces[1], 1)
    key_pieces = lax.optimization_barrier(key_pieces)
    key_pieces[2:] = [swap_one(key_pieces[d], d) for d in range(2, QUAD)]
    key_grad, value_grad = call(
        key_grad_kernel,
        "key_grad",
        [bf16(*key_bwd.shape), bf16(*value_bwd.shape)],
        [VMEM] * QUAD,
        *key_pieces,
    )
    return handed, query_grad, key_grad, value_grad


def solution(mesh):
    rows = P("pipe", "ctx", None)
    types = P("pipe", "ctx")
    return jax.shard_map(
        body,
        mesh=mesh,
        in_specs=(
            rows,
            rows,
            rows,
            rows,
            types,
            rows,
            rows,
            rows,
            rows,
            types,
            P("pipe", None, None),
            P("pipe", None),
            P("pipe", None),
        ),
        out_specs=(rows, rows, rows, rows),
        check_vma=False,
    )
```
